32 devices in a mesh: seq: 16 (over z, x, core), kvh: 2 (over y).
Axes of the slice: x: 2, y: 2, z: 4, core: 2. Of those that a mesh axis runs over, the one named last changes fastest.
Arguments:
- queries: bfloat16 [4096, 12288], P('seq', 'kvh'), may hold values from -4 to 4
- keys: bfloat16 [4096, 1024], P('seq', 'kvh'), may hold values from -10 to 10
- values: bfloat16 [4096, 1024], P('seq', 'kvh'), may hold values from -6 to 6
- answer_lengths: int32 [4], replicated, may hold values from 512 to 2048, as said below
Outputs:
- attended: bfloat16 [4096, 12288], P(('seq', 'kvh'))
The draws below stay inside these ranges and needn't reach their ends.
Inputs may be any that keep to these rules, and one draw needn't show every extreme that they name: `answer_lengths`: every length is a multiple of 256; the lengths sum to 4096; exactly one answer has the largest length 2048, every other one at most (7) * 256.
All inputs are finite; a program needn't handle non-finite values.
Results may differ from the reference program's by a relative error of at most 0.0035.
Values may be sent and summed in bfloat16 or wider, within the bound.
No kernel may reach another device: no remote copies, remote signals or barrier semaphores. Data moves between devices by JAX's collectives and lax.ppermute only.
A program may use at most 64 MiB of HBM per device.

```python
import math
import jax
import jax.numpy as jnp
from jax import lax

KEY_VALUE_HEADS = 8
QUERY_PER_KEY = 12
HEAD_WIDTH = 128
TOKENS_PER_SHARD = 256
PACKED_TOKENS = 4096
SPAN_MOST = 8
ANSWERS = 4
N_SEQ = 16


def draw_queries(key, part):
    key = jax.random.fold_in(key, 11)
    table_items = jax.random.truncated_normal(key, -4.0, 4.0, (PACKED_TOKENS, KEY_VALUE_HEADS * QUERY_PER_KEY * HEAD_WIDTH), jnp.float32)
    return table_items.astype(jnp.bfloat16)


def draw_keys(key, part):
    key = jax.random.fold_in(key, 23)
    table_items = 2.5 * jax.random.truncated_normal(key, -4.0, 4.0, (PACKED_TOKENS, KEY_VALUE_HEADS * HEAD_WIDTH), jnp.float32)
    return table_items.astype(jnp.bfloat16)


def draw_answer_lengths(key, part):
    key = jax.random.fold_in(key, 5)
    pick_key, order_key = jax.random.split(key)
    others = ANSWERS - 1
    extra_units = N_SEQ - SPAN_MOST - 2 * others
    room = SPAN_MOST - 3
    picks = jax.random.randint(pick_key, (max(extra_units, 1),), 0, others)

    def place_unit(unit_index, counts):
        wanted = picks[unit_index]
        crowded = counts[wanted] >= room
        emptiest = jnp.argmin(counts).astype(jnp.int32)
        target = jnp.where(crowded, emptiest, wanted)
        return counts.at[target].add(1)
    counts = lax.fori_loop(0, extra_units, place_unit, jnp.zeros((others,), jnp.int32))
    spans = jnp.concatenate([counts + 2, jnp.full((1,), SPAN_MOST, jnp.int32)])
    order = jax.random.permutation(order_key, ANSWERS)
    spans = spans[order]
    return (spans * TOKENS_PER_SHARD).astype(jnp.int32)


def shard_levels(stream_key, dims, cuts, least, largest):
    factor_of = 1.0
    for position, shards_of in cuts:
        steps = jax.random.uniform(jax.random.fold_in(jax.random.fold_in(stream_key, 6), position), (shards_of,), jnp.float32, least / len(cuts), largest / len(cuts))
        factor_of = factor_of * jnp.repeat(jnp.exp(steps), dims[position] // shards_of).reshape((-1,) + (1,) * (len(dims) - 1 - position))
    return factor_of


def bell_draw(own_key, dims, deviation, reach, shards=(), kind=jnp.bfloat16):
    entries = jax.random.normal(own_key, dims, jnp.float32) * deviation
    if len(shards) > 0:
        entries = shard_levels(own_key, dims, shards, -0.22, 0.18) * entries
    return jnp.clip(entries, min=-reach, max=reach).astype(kind)


def setup_inputs(seed: int = 0) -> dict:
    splits = jax.random.split(jax.random.key(seed), 5)
    return {
        "queries": draw_queries(jax.random.fold_in(splits[4], 71), 0),
        "keys": draw_keys(jax.random.fold_in(splits[4], 71), 0),
        "values": bell_draw(splits[2], (PACKED_TOKENS, KEY_VALUE_HEADS * HEAD_WIDTH), 1.0, 6.0, ((0, 16), (1, 2))),
        "answer_lengths": draw_answer_lengths(jax.random.fold_in(splits[4], 71), 0),
    }


def reference(queries, keys, values, answer_lengths):
    every_token = queries.shape[0]
    token_count = every_token // N_SEQ
    visible_span = SPAN_MOST * token_count
    answer_starts = jnp.cumsum(answer_lengths, dtype=jnp.int32) - answer_lengths
    answer_ends = answer_starts + answer_lengths
    positions = jnp.arange(every_token, dtype=jnp.int32)
    holding = (answer_starts[None, :] <= positions[:, None]) & (positions[:, None] < answer_ends[None, :])
    first_tokens = lax.optimization_barrier(jnp.sum(jnp.where(holding, answer_starts[None, :], 0), axis=1)).astype(jnp.int32)
    score_scale = 1.0 / math.sqrt(HEAD_WIDTH)

    def one_block(block_index):
        query_start = (block_index * token_count).astype(jnp.int32)
        key_begin = jnp.clip(query_start - (SPAN_MOST - 1) * token_count, 0, every_token - visible_span).astype(jnp.int32)
        query_matrix = lax.dynamic_slice_in_dim(queries, query_start, token_count, 0).astype(jnp.float32)
        query_matrix = query_matrix.reshape(token_count, KEY_VALUE_HEADS, QUERY_PER_KEY, HEAD_WIDTH)
        key_matrix = lax.dynamic_slice_in_dim(keys, key_begin, visible_span, 0).astype(jnp.float32).reshape(visible_span, KEY_VALUE_HEADS, HEAD_WIDTH)
        value_matrix = lax.dynamic_slice_in_dim(values, key_begin, visible_span, 0).astype(jnp.float32).reshape(visible_span, KEY_VALUE_HEADS, HEAD_WIDTH)
        query_pos = query_start + jnp.arange(token_count, dtype=jnp.int32)
        key_pos = key_begin + jnp.arange(visible_span, dtype=jnp.int32)
        query_first = lax.dynamic_slice_in_dim(first_tokens, query_start, token_count, 0)
        visible = (key_pos[None, :] <= query_pos[:, None]) & (key_pos[None, :] >= query_first[:, None])
        visible_grid = visible[None, :, None, :]
        scores = jnp.einsum('tkgd,wkd->ktgw', query_matrix, key_matrix) * score_scale
        row_max = lax.optimization_barrier(jnp.max(jnp.where(visible_grid, scores, -jnp.inf), axis=-1))
        probs = jnp.exp(jnp.where(visible_grid, scores - row_max[..., None], -jnp.inf))
        row_total = lax.optimization_barrier(jnp.sum(probs, axis=-1))
        weights = lax.optimization_barrier(probs.astype(jnp.bfloat16)).astype(jnp.float32)
        blended = jnp.einsum('ktgw,wkd->tkgd', weights, value_matrix)
        blended = blended / jnp.transpose(row_total, (1, 0, 2))[..., None]
        return blended.astype(jnp.bfloat16).reshape(token_count, KEY_VALUE_HEADS * QUERY_PER_KEY * HEAD_WIDTH)
    block_list = lax.map(one_block, jnp.arange(N_SEQ, dtype=jnp.int32))
    return block_list.reshape(every_token, KEY_VALUE_HEADS * QUERY_PER_KEY * HEAD_WIDTH)
```

```python
import math

import jax
import jax.numpy as jnp
from jax import lax
from jax.experimental import pallas as pl
from jax.experimental.pallas import tpu as pltpu
from jax.sharding import PartitionSpec as P

QUERY_PER_KEY = 12
HEAD_WIDTH = 128
GROUP_WIDTH = QUERY_PER_KEY * HEAD_WIDTH
SCALE_LOG2 = math.log2(math.e) / math.sqrt(HEAD_WIDTH)
VMEM_LIMIT = 56 * 1024 * 1024


def attention_kernel(
    meta, q_ref, k_ref, v_ref, out_ref, scores, peak, total, weighted, *, block
):
    rows = q_ref.shape[0]
    low, high, base = meta[0], meta[1], meta[3 + pl.program_id(1)] * rows

    def head_columns(h):
        return slice(h * HEAD_WIDTH, (h + 1) * HEAD_WIDTH)

    def block_rows(slot):
        return pl.ds(pl.multiple_of(slot * block, block), block)

    def score(slot, mask):
        keys = k_ref[block_rows(slot), :]
        for h in range(QUERY_PER_KEY):
            found = lax.dot_general(
                q_ref[:, head_columns(h)],
                keys,
                (((1,), (1,)), ((), ())),
                preferred_element_type=jnp.float32,
            )
            if mask is not None:
                found = jnp.where(mask, found, -1e30)
            scores[slot, h] = found
            widest = found[:, :HEAD_WIDTH]
            for part in range(1, block // HEAD_WIDTH):
                widest = jnp.maximum(widest, found[:, head_columns(part)])
            if mask is not None:
                peak[h] = widest
            else:
                peak[h] = jnp.maximum(peak[h], widest)

    tokens = base + lax.broadcasted_iota(jnp.int32, (rows, block), 0)
    mask = lax.broadcasted_iota(jnp.int32, (rows, block), 1) <= tokens
    score(high, mask)

    @pl.loop(low, high)
    def _(slot):
        score(slot, None)

    for h in range(QUERY_PER_KEY):
        top = jnp.max(peak[h], axis=-1, keepdims=True) * SCALE_LOG2
        peak[h] = jnp.broadcast_to(top, (rows, HEAD_WIDTH))
        total[h] = jnp.zeros((rows, HEAD_WIDTH), jnp.float32)
        weighted[h] = jnp.zeros((rows, HEAD_WIDTH), jnp.float32)

    @pl.loop(low, high + 1)
    def _(slot):
        values = v_ref[block_rows(slot), :]
        for h in range(QUERY_PER_KEY):
            top = peak[h]
            pieces = []
            summed = total[h]
            for part in range(block // HEAD_WIDTH):
                piece = jnp.exp2(scores[slot, h, :, head_columns(part)] * SCALE_LOG2 - top)
                summed = summed + piece
                pieces.append(piece.astype(jnp.bfloat16))
            total[h] = summed
            weighted[h] += jnp.dot(
                jnp.concatenate(pieces, axis=1), values, preferred_element_type=jnp.float32
            )

    for h in range(QUERY_PER_KEY):
        whole = jnp.sum(total[h], axis=-1, keepdims=True)
        out_ref[:, head_columns(h)] = (weighted[h] / whole).astype(out_ref.dtype)


def attend(meta, queries, keys, values, part_rows, part_count, span, block):
    heads = queries.shape[1] // GROUP_WIDTH
    window = span * block
    flops = 4 * part_count * part_rows * queries.shape[1] * window
    grid_spec = pltpu.PrefetchScalarGridSpec(
        num_scalar_prefetch=1,
        grid=(heads, part_count),
        in_specs=[
            pl.BlockSpec((part_rows, GROUP_WIDTH), lambda g, p, meta: (meta[3 + p], g)),
            pl.BlockSpec(
                (pl.Element(window), pl.Element(HEAD_WIDTH)),
                lambda g, p, meta: (
                    pl.multiple_of(meta[2] * block, block),
                    pl.multiple_of(g * HEAD_WIDTH, HEAD_WIDTH),
                ),
            ),
            pl.BlockSpec(
                (pl.Element(window), pl.Element(HEAD_WIDTH)),
                lambda g, p, meta: (
                    pl.multiple_of(meta[2] * block, block),
                    pl.multiple_of(g * HEAD_WIDTH, HEAD_WIDTH),
                ),
            ),
        ],
        out_specs=pl.BlockSpec((part_rows, GROUP_WIDTH), lambda g, p, meta: (p, g)),
        scratch_shapes=[
            pltpu.VMEM((span, QUERY_PER_KEY, part_rows, block), jnp.float32),
            pltpu.VMEM((QUERY_PER_KEY, part_rows, HEAD_WIDTH), jnp.float32),
            pltpu.VMEM((QUERY_PER_KEY, part_rows, HEAD_WIDTH), jnp.float32),
            pltpu.VMEM((QUERY_PER_KEY, part_rows, HEAD_WIDTH), jnp.float32),
        ],
    )
    return pl.pallas_call(
        lambda *refs: attention_kernel(*refs, block=block),
        out_shape=jax.ShapeDtypeStruct((part_count * part_rows, queries.shape[1]), jnp.bfloat16),
        grid_spec=grid_spec,
        compiler_params=pltpu.CompilerParams(vmem_limit_bytes=VMEM_LIMIT),
        cost_estimate=pl.CostEstimate(
            flops=flops,
            bytes_accessed=4 * queries.size + 4 * window * heads * HEAD_WIDTH,
            transcendentals=flops // (4 * HEAD_WIDTH),
        ),
    )(meta, queries, keys, values)


def shards(queries, keys, values, answer_lengths):
    block = queries.shape[0]
    count, groups = lax.axis_size("seq"), lax.axis_size("kvh")
    span = min(12, count // 2)
    mine, group = lax.axis_index("seq"), lax.axis_index("kvh")
    ends = jnp.cumsum(answer_lengths, dtype=jnp.int32)
    start = jnp.max(jnp.where(ends <= mine * block, ends, 0))
    window = jnp.maximum(mine - (span - 1), 0)
    low = start // block - window
    head = [low, mine - window, window]

    all_keys = lax.all_gather(keys, "seq", axis=0, tiled=True)
    all_values = lax.all_gather(values, "seq", axis=0, tiled=True)
    part_rows = block // groups

    def run(parts):
        meta = jnp.stack(head + list(parts)).astype(jnp.int32)
        return attend(
            meta, queries, all_keys, all_values, part_rows, len(parts), span, block
        )

    if groups != 2:
        attended = run([jnp.int32(p) for p in range(groups)])
        return lax.all_to_all(attended, "kvh", split_axis=0, concat_axis=1, tiled=True)
    sent = run([1 - group])
    received = lax.all_gather(sent, "kvh", axis=0)
    kept = run([group])
    others = jnp.where(group == 0, received[1], received[0])
    return jnp.where(
        group == 0,
        jnp.concatenate([kept, others], axis=1),
        jnp.concatenate([others, kept], axis=1),
    )


def solution(mesh):
    in_specs = (P("seq", "kvh"), P("seq", "kvh"), P("seq", "kvh"), P())
    out_specs = P(("seq", "kvh"), None)
    return jax.shard_map(shards, mesh=mesh, in_specs=in_specs, out_specs=out_specs, check_vma=False)
```

```python
import math

import jax
import jax.numpy as jnp
from jax import lax
from jax.experimental import pallas as pl
from jax.experimental.pallas import tpu as pltpu
from jax.sharding import PartitionSpec as P

QUERY_PER_KEY = 12
HEAD_WIDTH = 128
GROUP_WIDTH = QUERY_PER_KEY * HEAD_WIDTH
SCALE_LOG2 = math.log2(math.e) / math.sqrt(HEAD_WIDTH)
VMEM_LIMIT = 30 * 1024 * 1024
LOW, HIGH, TOKEN, QUERY_ROW, QUERY_COLUMN, OUT_COLUMN, PIECE_ROW = range(7)


def columns(h):
    return slice(h * HEAD_WIDTH, (h + 1) * HEAD_WIDTH)


def attention_kernel(meta, q_ref, *refs, block, pieces):
    out_ref, window, arrived, scores, peak, total, weighted = refs[-7:]
    rows = q_ref.shape[0]
    low, high, base = meta[LOW], meta[HIGH], meta[TOKEN]
    heads = pl.num_programs(0)
    head = pl.program_id(0)

    @pl.when(head == 0)
    def _():
        copies = []
        at = 0
        for number, piece in enumerate(refs[:pieces]):
            taken = min(piece.shape[0], window.shape[0] - at)
            first = pl.multiple_of(meta[PIECE_ROW] * block, block) if pieces == 1 else 0
            copies.append(
                pltpu.make_async_copy(
                    piece.at[pl.ds(first, taken)], window.at[pl.ds(at, taken)], arrived.at[number]
                )
            )
            at += taken
        for copy in copies:
            copy.start()
        for copy in copies:
            copy.wait()

    def block_of(slot, column):
        rows_of = pl.ds(pl.multiple_of(slot * block, block), block)
        return window[rows_of, pl.ds(pl.multiple_of(column * HEAD_WIDTH, HEAD_WIDTH), HEAD_WIDTH)]

    def score(slot, mask):
        keys = block_of(slot, head)
        for h in range(QUERY_PER_KEY):
            found = lax.dot_general(
                q_ref[:, columns(h)],
                keys,
                (((1,), (1,)), ((), ())),
                preferred_element_type=jnp.float32,
            )
            if mask is not None:
                found = jnp.where(mask, found, -1e30)
            scores[slot, h] = found
            widest = found[:, :HEAD_WIDTH]
            for part in range(1, block // HEAD_WIDTH):
                widest = jnp.maximum(widest, found[:, columns(part)])
            if mask is not None:
                peak[h] = widest
            else:
                peak[h] = jnp.maximum(peak[h], widest)

    tokens = base + lax.broadcasted_iota(jnp.int32, (rows, block), 0)
    mask = lax.broadcasted_iota(jnp.int32, (rows, block), 1) <= tokens
    score(high, mask)

    @pl.loop(low, high)
    def _(slot):
        score(slot, None)

    for h in range(QUERY_PER_KEY):
        top = jnp.max(peak[h], axis=-1, keepdims=True) * SCALE_LOG2
        peak[h] = jnp.broadcast_to(top, (rows, HEAD_WIDTH))
        total[h] = jnp.zeros((rows, HEAD_WIDTH), jnp.float32)
        weighted[h] = jnp.zeros((rows, HEAD_WIDTH), jnp.float32)

    @pl.loop(low, high + 1)
    def _(slot):
        values = block_of(slot, heads + head)
        for h in range(QUERY_PER_KEY):
            top = peak[h]
            found = []
            summed = total[h]
            for part in range(block // HEAD_WIDTH):
                piece = jnp.exp2(scores[slot, h, :, columns(part)] * SCALE_LOG2 - top)
                summed = summed + piece
                found.append(piece.astype(jnp.bfloat16))
            total[h] = summed
            weighted[h] += jnp.dot(
                jnp.concatenate(found, axis=1), values, preferred_element_type=jnp.float32
            )

    for h in range(QUERY_PER_KEY):
        whole = jnp.sum(total[h], axis=-1, keepdims=True)
        out_ref[:, columns(h)] = (weighted[h] / whole).astype(out_ref.dtype)


def attend(meta, queries, pieces, part_rows, span, block, out_width, earlier=()):
    heads = pieces[0].shape[1] // (2 * HEAD_WIDTH)
    slots = min(span + 1, sum(p.shape[0] for p in pieces) // block)
    flops = part_rows * heads * GROUP_WIDTH * span * block // 8
    grid_spec = pltpu.PrefetchScalarGridSpec(
        num_scalar_prefetch=1,
        grid=(heads,),
        in_specs=[
            pl.BlockSpec(
                (part_rows, GROUP_WIDTH),
                lambda g, meta: (meta[QUERY_ROW], meta[QUERY_COLUMN] + g),
            )
        ]
        + [pl.BlockSpec(memory_space=pl.ANY)] * (len(pieces) + len(earlier)),
        out_specs=pl.BlockSpec(
            (part_rows, GROUP_WIDTH), lambda g, meta: (0, meta[OUT_COLUMN] + g)
        ),
        scratch_shapes=[
            pltpu.VMEM((slots * block, 2 * heads * HEAD_WIDTH), jnp.bfloat16),
            pltpu.SemaphoreType.DMA((len(pieces),)),
            pltpu.VMEM((slots, QUERY_PER_KEY, part_rows, block), jnp.float32),
            pltpu.VMEM((QUERY_PER_KEY, part_rows, HEAD_WIDTH), jnp.float32),
            pltpu.VMEM((QUERY_PER_KEY, part_rows, HEAD_WIDTH), jnp.float32),
            pltpu.VMEM((QUERY_PER_KEY, part_rows, HEAD_WIDTH), jnp.float32),
        ],
    )
    return pl.pallas_call(
        lambda *refs: attention_kernel(*refs, block=block, pieces=len(pieces)),
        out_shape=jax.ShapeDtypeStruct((part_rows, out_width), jnp.bfloat16),
        grid_spec=grid_spec,
        compiler_params=pltpu.CompilerParams(vmem_limit_bytes=VMEM_LIMIT),
        cost_estimate=pl.CostEstimate(
            flops=flops,
            bytes_accessed=part_rows * heads * GROUP_WIDTH,
            transcendentals=0,
        ),
    )(meta, queries, *pieces, *earlier)


def place_kernel(meta, kept_ref, *refs):
    count = len(refs) - 2
    received, out_ref, sems = refs[:count], refs[count], refs[count + 1]
    width = received[0].shape[1]
    copies = [
        pltpu.make_async_copy(
            ref, out_ref.at[:, pl.ds(pl.multiple_of(meta[n] * width, width), width)], sems.at[n]
        )
        for n, ref in enumerate(received)
    ]
    for copy in copies:
        copy.start()
    for copy in copies:
        copy.wait()


def place(meta, kept, received):
    return pl.pallas_call(
        place_kernel,
        out_shape=jax.ShapeDtypeStruct(kept.shape, kept.dtype),
        grid_spec=pltpu.PrefetchScalarGridSpec(
            num_scalar_prefetch=1,
            grid=(),
            in_specs=[pl.BlockSpec(memory_space=pl.ANY)] * (1 + len(received)),
            out_specs=pl.BlockSpec(memory_space=pl.ANY),
            scratch_shapes=[pltpu.SemaphoreType.DMA((len(received),))],
        ),
        input_output_aliases={1: 0},
    )(meta, kept, *received)


def as_meta(*entries):
    return jnp.stack([jnp.asarray(e, jnp.int32) for e in entries])


def first_visible(answer_lengths, index, block):
    ends = jnp.cumsum(answer_lengths, dtype=jnp.int32)
    return jnp.max(jnp.where(ends <= index * block, ends, 0)) // block


def shards_whole(queries, keys, values, answer_lengths):
    block = queries.shape[0]
    count, groups = lax.axis_size("seq"), lax.axis_size("kvh")
    span = min(12, count // 2)
    mine = lax.axis_index("seq")
    window = jnp.maximum(mine - (span - 1), 0)
    low = first_visible(answer_lengths, mine, block) - window
    gathered = lax.all_gather(jnp.concatenate([keys, values], 1), "seq", axis=0, tiled=True)
    rows = block // groups
    parts = [
        attend(
            as_meta(low, mine - window, part * rows, part, 0, 0, window),
            queries,
            [gathered],
            rows,
            span - 1,
            block,
            queries.shape[1],
        )
        for part in range(groups)
    ]
    return lax.all_to_all(
        jnp.concatenate(parts, 0), "kvh", split_axis=0, concat_axis=1, tiled=True
    )


def shards(queries, keys, values, answer_lengths):
    block = queries.shape[0]
    count, groups = lax.axis_size("seq"), lax.axis_size("kvh")
    heads = keys.shape[1] // HEAD_WIDTH
    if groups != 2 or heads % 2 or count % 2:
        return shards_whole(queries, keys, values, answer_lengths)
    span = min(12, count // 2)
    mine, group = lax.axis_index("seq"), lax.axis_index("kvh")
    core = mine % 2
    pair = mine - core

    def half(value, which):
        width = value.shape[1] // 2
        return lax.dynamic_slice_in_dim(value, which * width, width, 1)

    def swap(value):
        return lax.ppermute(value, "seq", [(i, i ^ 1) for i in range(count)])

    def shift(value, steps):
        return lax.ppermute(value, "seq", [(i, i + steps) for i in range(count - steps)])

    kept_kv = jnp.concatenate([half(keys, core), half(values, core)], 1)
    other_kv = jnp.concatenate([half(keys, 1 - core), half(values, 1 - core)], 1)
    their_kv = swap(other_kv)
    their_queries = swap(half(queries, 1 - core))
    own = jnp.where(
        core == 0,
        jnp.concatenate([kept_kv, their_kv], 0),
        jnp.concatenate([their_kv, kept_kv], 0),
    )
    items = [own, shift(own, 2), shift(own, 4)]
    for steps in range(3, span // 2):
        items.append(shift(items[steps - 2], 4))
    items.append(shift(items[span // 2 - 2][block:], 4))
    pieces = items[::-1]

    rows = block // groups
    origin = pair - (span - 1)
    own_columns = (heads // 2) * core

    def part(tokens_core, tokens_half, earlier, out_width, out_column):
        index = pair + tokens_core
        theirs = tokens_core is not core
        meta = as_meta(
            first_visible(answer_lengths, index, block) - origin,
            index - origin,
            tokens_half * rows,
            tokens_half,
            0 if theirs else own_columns,
            out_column,
            0,
        )
        return attend(
            meta,
            their_queries if theirs else queries,
            pieces,
            rows,
            span,
            block,
            out_width,
            earlier,
        )

    def send(value, flip_core, flip_group):
        pairs = [
            (i * groups + r, (i ^ flip_core) * groups + (r ^ flip_group))
            for i in range(count)
            for r in range(groups)
        ]
        return lax.ppermute(value, ("seq", "kvh"), pairs)

    width = (heads // 2) * GROUP_WIDTH
    far = part(1 - core, 1 - group, (), width, 0)
    from_far = send(far, 1, 1)
    across = part(core, 1 - group, (far,), width, 0)
    beside = part(1 - core, group, (across,), width, 0)
    from_beside = send(beside, 1, 0)
    from_across = send(across, 0, 1)
    out_columns = (group * 2 + core) * (heads // 2)
    kept = part(core, group, (beside, from_far, from_across), groups * queries.shape[1], out_columns)
    places = as_meta(
        group * 2 + 1 - core, (1 - group) * 2 + core, (1 - group) * 2 + 1 - core
    )
    return place(places, kept, [from_beside, from_across, from_far])


def solution(mesh):
    in_specs = (P("seq", "kvh"), P("seq", "kvh"), P("seq", "kvh"), P())
    out_specs = P(("seq", "kvh"), None)
    return jax.shard_map(shards, mesh=mesh, in_specs=in_specs, out_specs=out_specs, check_vma=False)
```

```python
import math

import jax
import jax.numpy as jnp
from jax import lax
from jax.experimental import pallas as pl
from jax.experimental.pallas import tpu as pltpu
from jax.sharding import PartitionSpec as P

QUERY_PER_KEY = 12
HEAD_WIDTH = 128
GROUP_WIDTH = QUERY_PER_KEY * HEAD_WIDTH
SCALE_LOG2 = math.log2(math.e) / math.sqrt(HEAD_WIDTH)
VMEM_LIMIT = 30 * 1024 * 1024
STACK = 2
PAIRS = QUERY_PER_KEY // STACK
SWEEP = 64


def lanes(start):
    return pl.ds(pl.multiple_of(start * HEAD_WIDTH, HEAD_WIDTH), HEAD_WIDTH)


def first_visible(meta, position):
    end = jnp.int32(0)
    start = jnp.int32(0)
    for answer in range(2, meta.shape[0]):
        end = end + meta[answer]
        start = jnp.where(end <= position, end, start)
    return start


def attend_rows(count, first, offset, q_ref, out_ref, window, buffers, block):
    rows = q_ref.shape[0]
    stacked = STACK * rows
    score_buffers, prob_buffers, inverse = buffers
    sweep = min(SWEEP, stacked)
    chunks = count * block // HEAD_WIDTH
    tokens = lax.rem(lax.broadcasted_iota(jnp.int32, (stacked, block), 0), rows) + offset
    mask = lax.broadcasted_iota(jnp.int32, (stacked, block), 1) <= tokens

    def score(pair, target):
        heads = [q_ref[:, lanes(pair * STACK + h)] for h in range(STACK)]
        stack = jnp.concatenate(heads, axis=0)
        for slot in range(count):
            keys = window[pl.ds(pl.multiple_of(first + slot * block, block), block), :HEAD_WIDTH]
            found = lax.dot_general(
                stack, keys, (((1,), (1,)), ((), ())), preferred_element_type=jnp.float32
            )
            if slot == count - 1:
                found = jnp.where(mask, found, -1e30)
            target[:, slot * block : (slot + 1) * block] = found

    def soften(source, target):
        for row in range(0, stacked, sweep):
            here = slice(row, row + sweep)
            pieces = [slice(c * HEAD_WIDTH, (c + 1) * HEAD_WIDTH) for c in range(chunks)]
            top = source[here, pieces[0]]
            for piece in pieces[1:]:
                top = jnp.maximum(top, source[here, piece])
            peak = jnp.max(top, axis=-1, keepdims=True) * SCALE_LOG2
            total = jnp.zeros((sweep, HEAD_WIDTH), jnp.float32)
            for piece in pieces:
                probs = jnp.exp2(source[here, piece] * SCALE_LOG2 - peak)
                total = total + probs
                target[here, piece] = probs.astype(jnp.bfloat16)
            whole = jnp.sum(total, axis=-1, keepdims=True)
            inverse[here, :] = jnp.broadcast_to(1.0 / whole, (sweep, HEAD_WIDTH))

    def blend(pair, probs):
        values = window[pl.ds(pl.multiple_of(first, block), count * block), HEAD_WIDTH:]
        found = jnp.dot(
            probs[:, : count * block], values, preferred_element_type=jnp.float32
        )
        found = (found * inverse[...]).astype(out_ref.dtype)
        for h in range(STACK):
            out_ref[:, lanes(pair * STACK + h)] = found[h * rows : (h + 1) * rows]

    (even, odd), (even_probs, odd_probs) = score_buffers, prob_buffers
    score(0, even)

    @pl.loop(0, PAIRS // 2)
    def _(step):
        soften(even, even_probs)
        score(2 * step + 1, odd)
        blend(2 * step, even_probs)
        soften(odd, odd_probs)
        score(jnp.minimum(2 * step + 2, PAIRS - 1), even)
        blend(2 * step + 1, odd_probs)


def buffers_for(rows, span, block):
    stacked = STACK * rows
    return [
        pltpu.VMEM((stacked, span * block), jnp.float32),
        pltpu.VMEM((stacked, span * block), jnp.float32),
        pltpu.VMEM((stacked, span * block), jnp.bfloat16),
        pltpu.VMEM((stacked, span * block), jnp.bfloat16),
        pltpu.VMEM((stacked, HEAD_WIDTH), jnp.float32),
    ]


def attend_jobs(jobs, position_of, q_jobs, out_jobs, window, origin_of, meta, work, block, span):
    @pl.loop(0, jobs)
    def _(job):
        index, offset = position_of(job)
        start = lax.div(first_visible(meta, index * block), block)
        visible = index - start + 1
        first = (start - origin_of(job)) * block
        for count in range(1, span + 1):

            @pl.when(visible == count)
            def _():
                attend_rows(
                    count,
                    first,
                    offset,
                    q_jobs.at[job],
                    out_jobs.at[job],
                    window,
                    (work[0:2], work[2:4], work[4]),
                    block,
                )


def pair_kernel(meta, queries, theirs, *refs, first_flip, flip_half, which, jobs, block, span):
    own, near, far, side_own, side_near, side_far = refs[:6]
    window, q_jobs, out_jobs, sems = refs[-9:-5]
    outs = refs[-9 - jobs : -9]
    work = refs[-5:]
    rows = q_jobs.shape[1]
    mine, group = meta[0], meta[1]
    core = lax.rem(mine, 2)
    right = lax.rem(lax.div(mine, 2), 2)
    origin = mine - core - (span - 1)
    half = 1 - group if flip_half else group

    def fill(source, source_row, slot, size, sem):
        return pltpu.make_async_copy(
            source.at[pl.ds(source_row, size)], window.at[pl.ds(slot * block, size)], sems.at[sem]
        )

    fixed = [
        fill(far, block, 0, block, 0),
        fill(near, 0, 3, 2 * block, 1),
        fill(own, 0, 7, 2 * block, 2),
    ]
    by_side = [
        (fill(side_far, 0, 1, 2 * block, 3), fill(side_near, 0, 1, 2 * block, 3)),
        (fill(side_near, 0, 5, 2 * block, 4), fill(side_own, 0, 5, 2 * block, 4)),
    ]
    for job in range(jobs):
        flip = first_flip - job
        source, column = (theirs, which) if flip else (queries, 2 * core + which)
        at = pl.ds(pl.multiple_of(column * GROUP_WIDTH, GROUP_WIDTH), GROUP_WIDTH)
        fixed.append(
            pltpu.make_async_copy(
                source.at[pl.ds(pl.multiple_of(half * rows, rows), rows), at],
                q_jobs.at[job],
                sems.at[5 + job],
            )
        )
    for copy in fixed:
        copy.start()
    for on_left, on_right in by_side:
        pl.when(right == 0)(on_left.start)
        pl.when(right == 1)(on_right.start)
    for copy in fixed:
        copy.wait()
    for on_left, _ in by_side:
        on_left.wait()

    def position_of(job):
        flip = first_flip - job
        return mine - core + jnp.where(flip == 1, 1 - core, core), half * rows

    attend_jobs(
        jobs, position_of, q_jobs, out_jobs, window, lambda job: origin, meta, work, block, span
    )
    copies = [
        pltpu.make_async_copy(out_jobs.at[job], out, sems.at[5 + job])
        for job, out in enumerate(outs)
    ]
    for copy in copies:
        copy.start()
    for copy in copies:
        copy.wait()


def estimate():
    return pl.CostEstimate(flops=400_000_000, bytes_accessed=400_000, transcendentals=0)


def attend_pair(meta, queries, theirs, pieces, earlier, first_flip, flip_half, which, jobs, rows, span):
    block = queries.shape[0]
    args = [queries, theirs, *pieces, *earlier]
    return pl.pallas_call(
        lambda *refs: pair_kernel(
            *refs,
            first_flip=first_flip,
            flip_half=flip_half,
            which=which,
            jobs=jobs,
            block=block,
            span=span,
        ),
        out_shape=[jax.ShapeDtypeStruct((rows, GROUP_WIDTH), jnp.bfloat16)] * jobs,
        grid_spec=pltpu.PrefetchScalarGridSpec(
            num_scalar_prefetch=1,
            grid=(),
            in_specs=[pl.BlockSpec(memory_space=pl.ANY)] * len(args),
            out_specs=[pl.BlockSpec(memory_space=pl.ANY)] * jobs,
            scratch_shapes=[
                pltpu.VMEM(((span + 1) * block, 2 * HEAD_WIDTH), jnp.bfloat16),
                pltpu.VMEM((jobs, rows, GROUP_WIDTH), jnp.bfloat16),
                pltpu.VMEM((jobs, rows, GROUP_WIDTH), jnp.bfloat16),
                pltpu.SemaphoreType.DMA((5 + jobs,)),
                *buffers_for(rows, span, block),
            ],
        ),
        compiler_params=pltpu.CompilerParams(vmem_limit_bytes=VMEM_LIMIT),
        cost_estimate=estimate(),
    )(meta, *args)


def place_kernel(meta, *refs):
    inputs, out, sems = refs[:-2], refs[-2], refs[-1]
    core, group = lax.rem(meta[0], 2), meta[1]
    copies = []
    for number, ref in enumerate(inputs):
        which, source = number % 2, number // 2
        flip_core, flip_group = source % 2, source // 2
        from_core = 1 - core if flip_core else core
        from_group = 1 - group if flip_group else group
        column = ((from_group * 2 + from_core) * 2 + which) * GROUP_WIDTH
        at = pl.ds(pl.multiple_of(column, GROUP_WIDTH), GROUP_WIDTH)
        copies.append(pltpu.make_async_copy(ref, out.at[:, at], sems.at[number]))
    for copy in copies:
        copy.start()
    for copy in copies:
        copy.wait()


def place(meta, arrays):
    rows = arrays[0].shape[0]
    return pl.pallas_call(
        place_kernel,
        out_shape=jax.ShapeDtypeStruct((rows, len(arrays) * GROUP_WIDTH), jnp.bfloat16),
        grid_spec=pltpu.PrefetchScalarGridSpec(
            num_scalar_prefetch=1,
            grid=(),
            in_specs=[pl.BlockSpec(memory_space=pltpu.VMEM)] * len(arrays),
            out_specs=pl.BlockSpec(memory_space=pl.ANY),
            scratch_shapes=[pltpu.SemaphoreType.DMA((len(arrays),))],
        ),
        compiler_params=pltpu.CompilerParams(vmem_limit_bytes=VMEM_LIMIT),
    )(meta, *arrays)


def own_kernel(meta, keys, values, their_ref, *refs, which):
    out_ref = refs[-1]
    core = lax.rem(meta[0], 2)
    block = keys.shape[0]
    column = 2 * core + which
    mine = pl.ds(pl.multiple_of(core * block, block), block)
    other = pl.ds(pl.multiple_of((1 - core) * block, block), block)
    out_ref[mine, :HEAD_WIDTH] = keys[:, lanes(column)]
    out_ref[mine, HEAD_WIDTH:] = values[:, lanes(column)]
    for part in range(2):
        out_ref[other, part * HEAD_WIDTH : (part + 1) * HEAD_WIDTH] = their_ref[
            :, (2 * part + which) * HEAD_WIDTH : (2 * part + which + 1) * HEAD_WIDTH
        ]


def own_item(meta, keys, values, their_kv, earlier, which):
    block = keys.shape[0]
    inner = [pl.BlockSpec(memory_space=pltpu.VMEM)] * 3
    outer = [pl.BlockSpec(memory_space=pl.ANY)] * len(earlier)
    return pl.pallas_call(
        lambda *refs: own_kernel(*refs, which=which),
        out_shape=jax.ShapeDtypeStruct((2 * block, 2 * HEAD_WIDTH), jnp.bfloat16),
        grid_spec=pltpu.PrefetchScalarGridSpec(
            num_scalar_prefetch=1,
            grid=(),
            in_specs=inner + outer,
            out_specs=pl.BlockSpec(memory_space=pltpu.VMEM),
        ),
    )(meta, keys, values, their_kv, *earlier)


def whole_kernel(meta, queries, gathered, out, window, q_jobs, out_jobs, sems, *work, which, block, span):
    jobs, rows = q_jobs.shape[0], q_jobs.shape[1]
    mine = meta[0]
    origin = jnp.maximum(mine - (span - 1), 0)
    copies = [
        pltpu.make_async_copy(
            gathered.at[pl.ds(pl.multiple_of(origin * block, block), span * block)], window, sems.at[0]
        )
    ]
    at = pl.ds(which * GROUP_WIDTH, GROUP_WIDTH)
    for job in range(jobs):
        copies.append(
            pltpu.make_async_copy(
                queries.at[pl.ds(job * rows, rows), at], q_jobs.at[job], sems.at[1 + job]
            )
        )
    for copy in copies:
        copy.start()
    for copy in copies:
        copy.wait()
    attend_jobs(
        jobs,
        lambda job: (mine, job * rows),
        q_jobs,
        out_jobs,
        window,
        lambda job: origin,
        meta,
        work,
        block,
        span,
    )
    copies = [
        pltpu.make_async_copy(out_jobs.at[job], out.at[pl.ds(job * rows, rows)], sems.at[1 + job])
        for job in range(jobs)
    ]
    for copy in copies:
        copy.start()
    for copy in copies:
        copy.wait()


def shards_whole(meta, queries, keys, values, span):
    block, jobs = queries.shape[0], lax.axis_size("kvh")
    rows = block // jobs
    heads = []
    for which in range(keys.shape[1] // HEAD_WIDTH):
        at = slice(which * HEAD_WIDTH, (which + 1) * HEAD_WIDTH)
        item = jnp.concatenate([keys[:, at], values[:, at]], 1)
        gathered = lax.all_gather(item, "seq", axis=0, tiled=True)
        heads.append(
            pl.pallas_call(
                lambda *refs, which=which: whole_kernel(*refs, which=which, block=block, span=span),
                out_shape=jax.ShapeDtypeStruct((block, GROUP_WIDTH), jnp.bfloat16),
                grid_spec=pltpu.PrefetchScalarGridSpec(
                    num_scalar_prefetch=1,
                    grid=(),
                    in_specs=[pl.BlockSpec(memory_space=pl.ANY)] * 2,
                    out_specs=pl.BlockSpec(memory_space=pl.ANY),
                    scratch_shapes=[
                        pltpu.VMEM((span * block, 2 * HEAD_WIDTH), jnp.bfloat16),
                        pltpu.VMEM((jobs, rows, GROUP_WIDTH), jnp.bfloat16),
                        pltpu.VMEM((jobs, rows, GROUP_WIDTH), jnp.bfloat16),
                        pltpu.SemaphoreType.DMA((1 + jobs,)),
                        *buffers_for(rows, span, block),
                    ],
                ),
                compiler_params=pltpu.CompilerParams(vmem_limit_bytes=VMEM_LIMIT),
            )(meta, queries, gathered)
        )
    return lax.all_to_all(
        jnp.concatenate(heads, 1), "kvh", split_axis=0, concat_axis=1, tiled=True
    )


def shards(queries, keys, values, answer_lengths):
    block = queries.shape[0]
    count, groups = lax.axis_size("seq"), lax.axis_size("kvh")
    span = min(12, count // 2)
    mine, group = lax.axis_index("seq"), lax.axis_index("kvh")
    meta = jnp.concatenate([jnp.stack([mine, group]).astype(jnp.int32), answer_lengths])
    if groups != 2 or span != 8 or count % 4 or keys.shape[1] != 4 * HEAD_WIDTH:
        return shards_whole(meta, queries, keys, values, span)
    core = lax.rem(mine, 2)
    rows = block // groups

    def theirs(value):
        width = value.shape[1] // 2
        return lax.dynamic_slice_in_dim(value, (1 - core) * width, width, 1)

    def permute(value, pairs):
        return lax.ppermute(value, "seq", pairs)

    swap = [(i, i ^ 1) for i in range(count)]
    ahead = [(i, i + 4) for i in range(count - 4)]
    rightward = [(i, i + 2) for i in range(count) if i % 4 < 2]
    leftward = [(i, i - 2) for i in range(count) if i % 4 >= 2]

    their_kv = permute(jnp.concatenate([theirs(keys), theirs(values)], 1), swap)
    their_queries = permute(theirs(queries), swap)

    def gather(which, earlier):
        own = own_item(meta, keys, values, their_kv, earlier, which)
        near = permute(own, ahead)
        far = permute(near, ahead)
        side_own = permute(own, rightward)
        side_near = permute(near, rightward + leftward)
        side_far = permute(far, leftward)
        return [own, near, far, side_own, side_near, side_far]

    def send(value, flip_core, flip_group):
        pairs = [
            (i * groups + r, (i ^ flip_core) * groups + (r ^ flip_group))
            for i in range(count)
            for r in range(groups)
        ]
        return lax.ppermute(value, ("seq", "kvh"), pairs)

    def run(pieces, earlier, first_flip, flip_half, which, jobs):
        return attend_pair(
            meta, queries, their_queries, pieces, earlier, first_flip, flip_half, which, jobs, rows, span
        )

    pieces = gather(0, ())
    later = gather(1, pieces[2:5])
    (far_a,) = run(pieces, (), 1, 1, 0, 1)
    got_far_a = send(far_a, 1, 1)
    (across_a,) = run(pieces, (far_a,), 0, 1, 0, 1)
    got_across_a = send(across_a, 0, 1)
    beside_a, own_a = run(pieces, (across_a,), 1, 0, 0, 2)
    got_beside_a = send(beside_a, 1, 0)
    far_b, across_b = run(later, (beside_a,), 1, 1, 1, 2)
    got_far_b = send(far_b, 1, 1)
    got_across_b = send(across_b, 0, 1)
    beside_b, own_b = run(later, (far_b, got_far_a), 1, 0, 1, 2)
    got_beside_b = send(beside_b, 1, 0)
    return place(
        meta,
        [
            own_a,
            own_b,
            got_beside_a,
            got_beside_b,
            got_across_a,
            got_across_b,
            got_far_a,
            got_far_b,
        ],
    )


def solution(mesh):
    in_specs = (P("seq", "kvh"), P("seq", "kvh"), P("seq", "kvh"), P())
    out_specs = P(("seq", "kvh"), None)
    return jax.shard_map(shards, mesh=mesh, in_specs=in_specs, out_specs=out_specs, check_vma=False)
```

```python
import math

import jax
import jax.numpy as jnp
from jax import lax
from jax.experimental import pallas as pl
from jax.experimental.pallas import tpu as pltpu
from jax.sharding import PartitionSpec as P

QUERY_PER_KEY = 12
HEAD_WIDTH = 128
GROUP_WIDTH = QUERY_PER_KEY * HEAD_WIDTH
SCALE_LOG2 = math.log2(math.e) / math.sqrt(HEAD_WIDTH)
VMEM_LIMIT = 30 * 1024 * 1024
STACK = 2
PAIRS = QUERY_PER_KEY // STACK
SWEEP = 64


def lanes(start):
    return pl.ds(pl.multiple_of(start * HEAD_WIDTH, HEAD_WIDTH), HEAD_WIDTH)


def first_visible(meta, position):
    end = jnp.int32(0)
    start = jnp.int32(0)
    for answer in range(2, meta.shape[0]):
        end = end + meta[answer]
        start = jnp.where(end <= position, end, start)
    return start


def attend_rows(count, offset, q_ref, out_ref, work, block):
    rows = q_ref.shape[0]
    stacked = STACK * rows
    window, even, odd, even_probs, odd_probs, inverse, even_stack, odd_stack, staged = work
    sweep = min(SWEEP, stacked)
    chunks = count * block // HEAD_WIDTH
    width = count * block
    first = window.shape[0] - width
    tokens = lax.rem(lax.broadcasted_iota(jnp.int32, (stacked, block), 0), rows) + offset
    mask = lax.broadcasted_iota(jnp.int32, (stacked, block), 1) <= tokens

    def stack(pair, target):
        for h in range(STACK):
            target[h * rows : (h + 1) * rows, :] = q_ref[:, lanes(pair * STACK + h)]

    def score(source, target):
        for slot in range(count):
            keys = window[first + slot * block : first + (slot + 1) * block, :HEAD_WIDTH]
            found = lax.dot_general(
                source[...], keys, (((1,), (1,)), ((), ())), preferred_element_type=jnp.float32
            )
            if slot == count - 1:
                found = jnp.where(mask, found, -1e30)
            target[:, slot * block : (slot + 1) * block] = found

    def soften(source, target):
        for row in range(0, stacked, sweep):
            here = slice(row, row + sweep)
            pieces = [slice(c * HEAD_WIDTH, (c + 1) * HEAD_WIDTH) for c in range(chunks)]
            top = source[here, pieces[0]]
            for piece in pieces[1:]:
                top = jnp.maximum(top, source[here, piece])
            peak = jnp.max(top, axis=-1, keepdims=True) * SCALE_LOG2
            total = jnp.zeros((sweep, HEAD_WIDTH), jnp.float32)
            for piece in pieces:
                probs = jnp.exp2(source[here, piece] * SCALE_LOG2 - peak)
                total = total + probs
                target[here, piece] = probs.astype(jnp.bfloat16)
            whole = jnp.sum(total, axis=-1, keepdims=True)
            inverse[here, :] = jnp.broadcast_to(1.0 / whole, (sweep, HEAD_WIDTH))

    def blend(place, probs):
        found = jnp.dot(
            probs[:, :width], window[first:, HEAD_WIDTH:], preferred_element_type=jnp.float32
        )
        staged[place] = (found * inverse[...]).astype(staged.dtype)

    def release(pair, place):
        for h in range(STACK):
            out_ref[:, lanes(pair * STACK + h)] = staged[place, h * rows : (h + 1) * rows]

    stack(0, even_stack)
    score(even_stack, even)

    @pl.loop(0, PAIRS // 2)
    def _(step):
        stack(2 * step + 1, odd_stack)
        stack(jnp.minimum(2 * step + 2, PAIRS - 1), even_stack)
        soften(even, even_probs)
        score(odd_stack, odd)
        blend(0, even_probs)
        soften(odd, odd_probs)
        score(even_stack, even)
        blend(1, odd_probs)
        release(2 * step, 0)
        release(2 * step + 1, 1)


def buffers_for(rows, span, block):
    stacked = STACK * rows
    return [
        pltpu.VMEM((span * block, 2 * HEAD_WIDTH), jnp.bfloat16),
        pltpu.VMEM((stacked, span * block), jnp.float32),
        pltpu.VMEM((stacked, span * block), jnp.float32),
        pltpu.VMEM((stacked, span * block), jnp.bfloat16),
        pltpu.VMEM((stacked, span * block), jnp.bfloat16),
        pltpu.VMEM((stacked, HEAD_WIDTH), jnp.float32),
        pltpu.VMEM((stacked, HEAD_WIDTH), jnp.bfloat16),
        pltpu.VMEM((stacked, HEAD_WIDTH), jnp.bfloat16),
        pltpu.VMEM((2, stacked, HEAD_WIDTH), jnp.bfloat16),
    ]


WORK = 9


def attend_jobs(jobs, position_of, q_jobs, out_jobs, arrived, origin, meta, work, block, span):
    @pl.loop(0, jobs)
    def _(job):
        index, offset = position_of(job)
        start = lax.div(first_visible(meta, index * block), block)
        visible = index - start + 1
        last = (index - origin + 1 - span) * block
        work[0][...] = arrived[pl.ds(pl.multiple_of(last, block), span * block), :]
        for count in range(1, span + 1):

            @pl.when(visible == count)
            def _():
                attend_rows(count, offset, q_jobs.at[job], out_jobs.at[job], work, block)


def pair_kernel(meta, queries, theirs, *refs, first_flip, flip_half, which, jobs, block, span):
    own, near, far, side_own, side_near, side_far = refs[:6]
    window, q_jobs, out_jobs, sems = refs[-4 - WORK : -WORK]
    outs = refs[-4 - WORK - jobs : -4 - WORK]
    work = refs[-WORK:]
    rows = q_jobs.shape[1]
    mine, group = meta[0], meta[1]
    core = lax.rem(mine, 2)
    right = lax.rem(lax.div(mine, 2), 2)
    origin = mine - core - (span - 1)
    half = 1 - group if flip_half else group

    def fill(source, source_row, slot, size, sem):
        return pltpu.make_async_copy(
            source.at[pl.ds(source_row, size)], window.at[pl.ds(slot * block, size)], sems.at[sem]
        )

    fixed = [
        fill(far, block, 0, block, 0),
        fill(near, 0, 3, 2 * block, 1),
        fill(own, 0, 7, 2 * block, 2),
    ]
    by_side = [
        (fill(side_far, 0, 1, 2 * block, 3), fill(side_near, 0, 1, 2 * block, 3)),
        (fill(side_near, 0, 5, 2 * block, 4), fill(side_own, 0, 5, 2 * block, 4)),
    ]
    for job in range(jobs):
        flip = first_flip - job
        source, column = (theirs, which) if flip else (queries, 2 * core + which)
        at = pl.ds(pl.multiple_of(column * GROUP_WIDTH, GROUP_WIDTH), GROUP_WIDTH)
        fixed.append(
            pltpu.make_async_copy(
                source.at[pl.ds(pl.multiple_of(half * rows, rows), rows), at],
                q_jobs.at[job],
                sems.at[5 + job],
            )
        )
    for copy in fixed:
        copy.start()
    for on_left, on_right in by_side:
        pl.when(right == 0)(on_left.start)
        pl.when(right == 1)(on_right.start)
    for copy in fixed:
        copy.wait()
    for on_left, _ in by_side:
        on_left.wait()

    def position_of(job):
        flip = first_flip - job
        return mine - core + jnp.where(flip == 1, 1 - core, core), half * rows

    attend_jobs(
        jobs, position_of, q_jobs, out_jobs, window, origin, meta, work, block, span
    )
    copies = [
        pltpu.make_async_copy(out_jobs.at[job], out, sems.at[5 + job])
        for job, out in enumerate(outs)
    ]
    for copy in copies:
        copy.start()
    for copy in copies:
        copy.wait()


def estimate():
    return pl.CostEstimate(flops=400_000_000, bytes_accessed=400_000, transcendentals=0)


def attend_pair(meta, queries, theirs, pieces, earlier, first_flip, flip_half, which, jobs, rows, span):
    block = queries.shape[0]
    args = [queries, theirs, *pieces, *earlier]
    return pl.pallas_call(
        lambda *refs: pair_kernel(
            *refs,
            first_flip=first_flip,
            flip_half=flip_half,
            which=which,
            jobs=jobs,
            block=block,
            span=span,
        ),
        out_shape=[jax.ShapeDtypeStruct((rows, GROUP_WIDTH), jnp.bfloat16)] * jobs,
        grid_spec=pltpu.PrefetchScalarGridSpec(
            num_scalar_prefetch=1,
            grid=(),
            in_specs=[pl.BlockSpec(memory_space=pltpu.HBM)] * len(args),
            out_specs=[pl.BlockSpec(memory_space=pltpu.HBM)] * jobs,
            scratch_shapes=[
                pltpu.VMEM(((span + 1) * block, 2 * HEAD_WIDTH), jnp.bfloat16),
                pltpu.VMEM((jobs, rows, GROUP_WIDTH), jnp.bfloat16),
                pltpu.VMEM((jobs, rows, GROUP_WIDTH), jnp.bfloat16),
                pltpu.SemaphoreType.DMA((5 + jobs,)),
                *buffers_for(rows, span, block),
            ],
        ),
        compiler_params=pltpu.CompilerParams(vmem_limit_bytes=VMEM_LIMIT),
        cost_estimate=estimate(),
    )(meta, *args)


def place_kernel(meta, *refs):
    inputs, out, sems = refs[:-2], refs[-2], refs[-1]
    core, group = lax.rem(meta[0], 2), meta[1]
    copies = []
    for number, ref in enumerate(inputs):
        which, source = number % 2, number // 2
        flip_core, flip_group = source % 2, source // 2
        from_core = 1 - core if flip_core else core
        from_group = 1 - group if flip_group else group
        column = ((from_group * 2 + from_core) * 2 + which) * GROUP_WIDTH
        at = pl.ds(pl.multiple_of(column, GROUP_WIDTH), GROUP_WIDTH)
        copies.append(pltpu.make_async_copy(ref, out.at[:, at], sems.at[number]))
    for copy in copies:
        copy.start()
    for copy in copies:
        copy.wait()


def place(meta, arrays):
    rows = arrays[0].shape[0]
    return pl.pallas_call(
        place_kernel,
        out_shape=jax.ShapeDtypeStruct((rows, len(arrays) * GROUP_WIDTH), jnp.bfloat16),
        grid_spec=pltpu.PrefetchScalarGridSpec(
            num_scalar_prefetch=1,
            grid=(),
            in_specs=[pl.BlockSpec(memory_space=pltpu.VMEM)] * len(arrays),
            out_specs=pl.BlockSpec(memory_space=pltpu.HBM),
            scratch_shapes=[pltpu.SemaphoreType.DMA((len(arrays),))],
        ),
        compiler_params=pltpu.CompilerParams(vmem_limit_bytes=VMEM_LIMIT),
    )(meta, *arrays)


def own_kernel(meta, keys, values, their_ref, *refs, which):
    out_ref = refs[-1]
    core = lax.rem(meta[0], 2)
    block = keys.shape[0]
    column = 2 * core + which
    mine = pl.ds(pl.multiple_of(core * block, block), block)
    other = pl.ds(pl.multiple_of((1 - core) * block, block), block)
    out_ref[mine, :HEAD_WIDTH] = keys[:, lanes(column)]
    out_ref[mine, HEAD_WIDTH:] = values[:, lanes(column)]
    for part in range(2):
        out_ref[other, part * HEAD_WIDTH : (part + 1) * HEAD_WIDTH] = their_ref[
            :, (2 * part + which) * HEAD_WIDTH : (2 * part + which + 1) * HEAD_WIDTH
        ]


def own_item(meta, keys, values, their_kv, earlier, which):
    block = keys.shape[0]
    inner = [pl.BlockSpec(memory_space=pltpu.VMEM)] * 3
    outer = [pl.BlockSpec(memory_space=pltpu.HBM)] * len(earlier)
    return pl.pallas_call(
        lambda *refs: own_kernel(*refs, which=which),
        out_shape=jax.ShapeDtypeStruct((2 * block, 2 * HEAD_WIDTH), jnp.bfloat16),
        grid_spec=pltpu.PrefetchScalarGridSpec(
            num_scalar_prefetch=1,
            grid=(),
            in_specs=inner + outer,
            out_specs=pl.BlockSpec(memory_space=pltpu.VMEM),
        ),
    )(meta, keys, values, their_kv, *earlier)


def copy_kernel(meta, source, *refs):
    refs[-1][...] = source[...]


def swapped_columns(meta, queries, earlier):
    rows, width = queries.shape[0], queries.shape[1] // 4
    return pl.pallas_call(
        copy_kernel,
        out_shape=jax.ShapeDtypeStruct((rows, 2 * width), queries.dtype),
        grid_spec=pltpu.PrefetchScalarGridSpec(
            num_scalar_prefetch=1,
            grid=(2,),
            in_specs=[
                pl.BlockSpec(
                    (rows, width), lambda g, meta: (0, 2 * (1 - lax.rem(meta[0], 2)) + g)
                )
            ]
            + [pl.BlockSpec(memory_space=pltpu.HBM)] * len(earlier),
            out_specs=pl.BlockSpec((rows, width), lambda g, meta: (0, g)),
        ),
    )(meta, queries, *earlier)


def whole_kernel(meta, queries, gathered, out, window, q_jobs, out_jobs, sems, *work, which, block, span):
    jobs, rows = q_jobs.shape[0], q_jobs.shape[1]
    mine = meta[0]
    origin = mine - (span - 1)
    copies = []
    for slot in range(span):
        at = pl.ds(pl.multiple_of(jnp.maximum(origin + slot, 0) * block, block), block)
        copies.append(
            pltpu.make_async_copy(
                gathered.at[at], window.at[pl.ds(slot * block, block)], sems.at[jobs + slot]
            )
        )
    at = pl.ds(which * GROUP_WIDTH, GROUP_WIDTH)
    for job in range(jobs):
        copies.append(
            pltpu.make_async_copy(
                queries.at[pl.ds(job * rows, rows), at], q_jobs.at[job], sems.at[job]
            )
        )
    for copy in copies:
        copy.start()
    for copy in copies:
        copy.wait()
    attend_jobs(
        jobs,
        lambda job: (mine, job * rows),
        q_jobs,
        out_jobs,
        window,
        origin,
        meta,
        work,
        block,
        span,
    )
    copies = [
        pltpu.make_async_copy(out_jobs.at[job], out.at[pl.ds(job * rows, rows)], sems.at[job])
        for job in range(jobs)
    ]
    for copy in copies:
        copy.start()
    for copy in copies:
        copy.wait()


def shards_whole(meta, queries, keys, values, span):
    block, jobs = queries.shape[0], lax.axis_size("kvh")
    rows = block // jobs
    heads = []
    for which in range(keys.shape[1] // HEAD_WIDTH):
        at = slice(which * HEAD_WIDTH, (which + 1) * HEAD_WIDTH)
        item = jnp.concatenate([keys[:, at], values[:, at]], 1)
        gathered = lax.all_gather(item, "seq", axis=0, tiled=True)
        heads.append(
            pl.pallas_call(
                lambda *refs, which=which: whole_kernel(*refs, which=which, block=block, span=span),
                out_shape=jax.ShapeDtypeStruct((block, GROUP_WIDTH), jnp.bfloat16),
                grid_spec=pltpu.PrefetchScalarGridSpec(
                    num_scalar_prefetch=1,
                    grid=(),
                    in_specs=[pl.BlockSpec(memory_space=pltpu.HBM)] * 2,
                    out_specs=pl.BlockSpec(memory_space=pltpu.HBM),
                    scratch_shapes=[
                        pltpu.VMEM((span * block, 2 * HEAD_WIDTH), jnp.bfloat16),
                        pltpu.VMEM((jobs, rows, GROUP_WIDTH), jnp.bfloat16),
                        pltpu.VMEM((jobs, rows, GROUP_WIDTH), jnp.bfloat16),
                        pltpu.SemaphoreType.DMA((jobs + span,)),
                        *buffers_for(rows, span, block),
                    ],
                ),
                compiler_params=pltpu.CompilerParams(vmem_limit_bytes=VMEM_LIMIT),
            )(meta, queries, gathered)
        )
    return lax.all_to_all(
        jnp.concatenate(heads, 1), "kvh", split_axis=0, concat_axis=1, tiled=True
    )


def shards(queries, keys, values, answer_lengths):
    block = queries.shape[0]
    count, groups = lax.axis_size("seq"), lax.axis_size("kvh")
    span = min(12, count // 2)
    mine, group = lax.axis_index("seq"), lax.axis_index("kvh")
    meta = jnp.concatenate([jnp.stack([mine, group]).astype(jnp.int32), answer_lengths])
    if groups != 2 or span != 8 or count % 4 or keys.shape[1] != 4 * HEAD_WIDTH:
        return shards_whole(meta, queries, keys, values, span)
    core = lax.rem(mine, 2)
    rows = block // groups

    def theirs(value):
        width = value.shape[1] // 2
        return lax.dynamic_slice_in_dim(value, (1 - core) * width, width, 1)

    def permute(value, pairs):
        return lax.ppermute(value, "seq", pairs)

    swap = [(i, i ^ 1) for i in range(count)]
    ahead = [(i, i + 4) for i in range(count - 4)]
    rightward = [(i, i + 2) for i in range(count) if i % 4 < 2]
    leftward = [(i, i - 2) for i in range(count) if i % 4 >= 2]

    their_kv = permute(jnp.concatenate([theirs(keys), theirs(values)], 1), swap)

    def gather(which, earlier):
        own = own_item(meta, keys, values, their_kv, earlier, which)
        near = permute(own, ahead)
        far = permute(near, ahead)
        side_own = permute(own, rightward)
        side_near = permute(near, rightward + leftward)
        side_far = permute(far, leftward)
        return [own, near, far, side_own, side_near, side_far]

    def send(value, flip_core, flip_group):
        pairs = [
            (i * groups + r, (i ^ flip_core) * groups + (r ^ flip_group))
            for i in range(count)
            for r in range(groups)
        ]
        return lax.ppermute(value, ("seq", "kvh"), pairs)

    def run(pieces, earlier, first_flip, flip_half, which, jobs):
        return attend_pair(
            meta, queries, their_queries, pieces, earlier, first_flip, flip_half, which, jobs, rows, span
        )

    pieces = gather(0, ())
    their_queries = permute(swapped_columns(meta, queries, pieces[1:2]), swap)
    later = gather(1, pieces[2:5])
    (far_a,) = run(pieces, (), 1, 1, 0, 1)
    got_far_a = send(far_a, 1, 1)
    (across_a,) = run(pieces, (far_a,), 0, 1, 0, 1)
    got_across_a = send(across_a, 0, 1)
    beside_a, own_a = run(pieces, (across_a,), 1, 0, 0, 2)
    got_beside_a = send(beside_a, 1, 0)
    far_b, across_b = run(later, (beside_a,), 1, 1, 1, 2)
    got_far_b = send(far_b, 1, 1)
    got_across_b = send(across_b, 0, 1)
    beside_b, own_b = run(later, (far_b, got_far_a), 1, 0, 1, 2)
    got_beside_b = send(beside_b, 1, 0)
    return place(
        meta,
        [
            own_a,
            own_b,
            got_beside_a,
            got_beside_b,
            got_across_a,
            got_across_b,
            got_far_a,
            got_far_b,
        ],
    )


def solution(mesh):
    in_specs = (P("seq", "kvh"), P("seq", "kvh"), P("seq", "kvh"), P())
    out_specs = P(("seq", "kvh"), None)
    return jax.shard_map(shards, mesh=mesh, in_specs=in_specs, out_specs=out_specs, check_vma=False)
```

```python
import math

import jax
import jax.numpy as jnp
from jax import lax
from jax.experimental import pallas as pl
from jax.experimental.pallas import tpu as pltpu
from jax.sharding import PartitionSpec as P

QUERY_PER_KEY = 12
HEAD_WIDTH = 128
GROUP_WIDTH = QUERY_PER_KEY * HEAD_WIDTH
SCALE_LOG2 = math.log2(math.e) / math.sqrt(HEAD_WIDTH)
VMEM_LIMIT = 30 * 1024 * 1024
STACK = 2
PAIRS = QUERY_PER_KEY // STACK


def lanes(start):
    return pl.ds(pl.multiple_of(start * HEAD_WIDTH, HEAD_WIDTH), HEAD_WIDTH)


def first_visible(meta, position):
    end = jnp.int32(0)
    start = jnp.int32(0)
    for answer in range(2, meta.shape[0]):
        end = end + meta[answer]
        start = jnp.where(end <= position, end, start)
    return start


def attend_rows(count, offset, q_ref, out_ref, work, block):
    rows = q_ref.shape[0]
    stacked = STACK * rows
    window, nearest, shifts, probs, stacks, staged = (
        work[0],
        work[1:3],
        work[3:5],
        work[5:7],
        work[7:9],
        work[9],
    )
    width = count * block
    first = window.shape[0] - width
    tokens = lax.rem(lax.broadcasted_iota(jnp.int32, (stacked, block), 0), rows) + offset
    mask = lax.broadcasted_iota(jnp.int32, (stacked, block), 1) <= tokens

    def stack(pair, target):
        for h in range(STACK):
            target[h * rows : (h + 1) * rows, :] = q_ref[:, lanes(pair * STACK + h)]

    def score(source, slot):
        keys = window[first + slot * block : first + (slot + 1) * block, :HEAD_WIDTH]
        return lax.dot_general(
            source[...], keys, (((1,), (1,)), ((), ())), preferred_element_type=jnp.float32
        )

    def begin(place):
        found = jnp.where(mask, score(stacks[place], count - 1), -1e30)
        nearest[place][...] = found
        top = jnp.max(found, axis=-1, keepdims=True) * SCALE_LOG2
        shifts[place][...] = jnp.broadcast_to(top, (stacked, HEAD_WIDTH))

    def soften(found, slot, place):
        for piece in range(block // HEAD_WIDTH):
            at = slice(piece * HEAD_WIDTH, (piece + 1) * HEAD_WIDTH)
            weights = jnp.exp2(found[:, at] * SCALE_LOG2 - shifts[place][...])
            start = slot * block + piece * HEAD_WIDTH
            probs[place][:, start : start + HEAD_WIDTH] = weights.astype(jnp.bfloat16)

    def weigh(place):
        ahead = score(stacks[place], 0) if count > 1 else None
        for slot in range(count - 1):
            found = ahead
            if slot < count - 2:
                ahead = score(stacks[place], slot + 1)
            soften(found, slot, place)
        soften(nearest[place], count - 1, place)

    def blend(place):
        found = jnp.dot(
            probs[place][:, :width], window[first:, HEAD_WIDTH:], preferred_element_type=jnp.float32
        )
        total = found[:, HEAD_WIDTH:]
        staged[place] = (found[:, :HEAD_WIDTH] / total).astype(staged.dtype)
        return total

    def release(pair, place):
        for h in range(STACK):
            out_ref[:, lanes(pair * STACK + h)] = staged[place, h * rows : (h + 1) * rows]

    def largest(total):
        most = total[:8]
        for row in range(8, stacked, 8):
            most = jnp.maximum(most, total[row : row + 8])
        return most

    stack(0, stacks[0])
    begin(0)

    def step(number, most):
        stack(2 * number + 1, stacks[1])
        begin(1)
        weigh(0)
        total = blend(0)
        most = jnp.maximum(most, largest(total))
        stack(jnp.minimum(2 * number + 2, PAIRS - 1), stacks[0])
        begin(0)
        weigh(1)
        total = blend(1)
        most = jnp.maximum(most, largest(total))
        release(2 * number, 0)
        release(2 * number + 1, 1)
        return most

    most = lax.fori_loop(0, PAIRS // 2, step, jnp.zeros((8, HEAD_WIDTH), jnp.float32))
    return jnp.max(most)


def attend_rows_wide(visible, offset, q_ref, out_ref, work, block):
    rows = q_ref.shape[0]
    window, (peak, total, blended) = work[0], work[10:13]
    last = window.shape[0] - block
    tokens = lax.broadcasted_iota(jnp.int32, (rows, block), 0) + offset
    columns = lax.broadcasted_iota(jnp.int32, (rows, block), 1)

    @pl.loop(0, QUERY_PER_KEY)
    def _(head):
        peak[...] = jnp.full(peak.shape, -1e30, jnp.float32)
        total[...] = jnp.zeros(total.shape, jnp.float32)
        blended[...] = jnp.zeros(blended.shape, jnp.float32)

        @pl.loop(0, visible)
        def _(back):
            at = pl.ds(pl.multiple_of(last - back * block, block), block)
            found = lax.dot_general(
                q_ref[:, lanes(head)],
                window[at, :HEAD_WIDTH],
                (((1,), (1,)), ((), ())),
                preferred_element_type=jnp.float32,
            )
            found = jnp.where(columns <= tokens + back * block, found * SCALE_LOG2, -1e30)
            before = peak[...]
            now = jnp.maximum(before, jnp.max(found, axis=-1, keepdims=True))
            weights = jnp.exp2(found - now[:, :1])
            shrink = jnp.exp2(before - now)
            peak[...] = now
            total[...] = total[...] * shrink + jnp.sum(weights, axis=-1, keepdims=True)
            blended[...] = blended[...] * shrink + jnp.dot(
                weights.astype(jnp.bfloat16),
                window[at, HEAD_WIDTH : 2 * HEAD_WIDTH],
                preferred_element_type=jnp.float32,
            )

        out_ref[:, lanes(head)] = (blended[...] / total[...]).astype(out_ref.dtype)


def buffers_for(rows, span, block):
    stacked = STACK * rows
    return [
        pltpu.VMEM((span * block, 3 * HEAD_WIDTH), jnp.bfloat16),
        pltpu.VMEM((stacked, block), jnp.float32),
        pltpu.VMEM((stacked, block), jnp.float32),
        pltpu.VMEM((stacked, HEAD_WIDTH), jnp.float32),
        pltpu.VMEM((stacked, HEAD_WIDTH), jnp.float32),
        pltpu.VMEM((stacked, span * block), jnp.bfloat16),
        pltpu.VMEM((stacked, span * block), jnp.bfloat16),
        pltpu.VMEM((stacked, HEAD_WIDTH), jnp.bfloat16),
        pltpu.VMEM((stacked, HEAD_WIDTH), jnp.bfloat16),
        pltpu.VMEM((2, stacked, HEAD_WIDTH), jnp.bfloat16),
        pltpu.VMEM((rows, HEAD_WIDTH), jnp.float32),
        pltpu.VMEM((rows, HEAD_WIDTH), jnp.float32),
        pltpu.VMEM((rows, HEAD_WIDTH), jnp.float32),
        pltpu.SMEM((1,), jnp.float32),
    ]


WORK = 14


def attend_jobs(jobs, position_of, q_jobs, out_jobs, arrived, origin, meta, work, block, span):
    @pl.loop(0, jobs)
    def _(job):
        index, offset = position_of(job)
        start = lax.div(first_visible(meta, index * block), block)
        visible = index - start + 1
        last = (index - origin + 1 - span) * block
        window, most = work[0], work[13]
        moved = pl.ds(pl.multiple_of(last, block), span * block)
        window[:, : 2 * HEAD_WIDTH] = arrived[moved, :]
        window[:, 2 * HEAD_WIDTH :] = jnp.ones((span * block, HEAD_WIDTH), jnp.bfloat16)
        for count in range(1, span + 1):

            @pl.when(visible == count)
            def _():
                most[0] = attend_rows(count, offset, q_jobs.at[job], out_jobs.at[job], work, block)

        @pl.when(jnp.logical_not(most[0] < 2.0**120))
        def _():
            attend_rows_wide(visible, offset, q_jobs.at[job], out_jobs.at[job], work, block)


def pair_kernel(meta, queries, theirs, *refs, first_flip, flip_half, which, jobs, block, span):
    own, near, far, side_own, side_near, side_far = refs[:6]
    window, q_jobs, out_jobs, sems = refs[-4 - WORK : -WORK]
    outs = refs[-4 - WORK - jobs : -4 - WORK]
    work = refs[-WORK:]
    rows = q_jobs.shape[1]
    mine, group = meta[0], meta[1]
    core = lax.rem(mine, 2)
    right = lax.rem(lax.div(mine, 2), 2)
    origin = mine - core - (span - 1)
    half = 1 - group if flip_half else group

    def fill(source, source_row, slot, size, sem):
        return pltpu.make_async_copy(
            source.at[pl.ds(source_row, size)], window.at[pl.ds(slot * block, size)], sems.at[sem]
        )

    fixed = [
        fill(far, block, 0, block, 0),
        fill(near, 0, 3, 2 * block, 1),
        fill(own, 0, 7, 2 * block, 2),
    ]
    by_side = [
        (fill(side_far, 0, 1, 2 * block, 3), fill(side_near, 0, 1, 2 * block, 3)),
        (fill(side_near, 0, 5, 2 * block, 4), fill(side_own, 0, 5, 2 * block, 4)),
    ]
    for job in range(jobs):
        flip = first_flip - job
        source, column = (theirs, which) if flip else (queries, 2 * core + which)
        at = pl.ds(pl.multiple_of(column * GROUP_WIDTH, GROUP_WIDTH), GROUP_WIDTH)
        fixed.append(
            pltpu.make_async_copy(
                source.at[pl.ds(pl.multiple_of(half * rows, rows), rows), at],
                q_jobs.at[job],
                sems.at[5 + job],
            )
        )
    for copy in fixed:
        copy.start()
    for on_left, on_right in by_side:
        pl.when(right == 0)(on_left.start)
        pl.when(right == 1)(on_right.start)
    for copy in fixed:
        copy.wait()
    for on_left, _ in by_side:
        on_left.wait()

    def position_of(job):
        flip = first_flip - job
        return mine - core + jnp.where(flip == 1, 1 - core, core), half * rows

    attend_jobs(
        jobs, position_of, q_jobs, out_jobs, window, origin, meta, work, block, span
    )
    copies = [
        pltpu.make_async_copy(out_jobs.at[job], out, sems.at[5 + job])
        for job, out in enumerate(outs)
    ]
    for copy in copies:
        copy.start()
    for copy in copies:
        copy.wait()


def estimate():
    return pl.CostEstimate(flops=400_000_000, bytes_accessed=400_000, transcendentals=0)


def attend_pair(meta, queries, theirs, pieces, earlier, first_flip, flip_half, which, jobs, rows, span):
    block = queries.shape[0]
    args = [queries, theirs, *pieces, *earlier]
    return pl.pallas_call(
        lambda *refs: pair_kernel(
            *refs,
            first_flip=first_flip,
            flip_half=flip_half,
            which=which,
            jobs=jobs,
            block=block,
            span=span,
        ),
        out_shape=[jax.ShapeDtypeStruct((rows, GROUP_WIDTH), jnp.bfloat16)] * jobs,
        grid_spec=pltpu.PrefetchScalarGridSpec(
            num_scalar_prefetch=1,
            grid=(),
            in_specs=[pl.BlockSpec(memory_space=pltpu.HBM)] * len(args),
            out_specs=[pl.BlockSpec(memory_space=pltpu.HBM)] * jobs,
            scratch_shapes=[
                pltpu.VMEM(((span + 1) * block, 2 * HEAD_WIDTH), jnp.bfloat16),
                pltpu.VMEM((jobs, rows, GROUP_WIDTH), jnp.bfloat16),
                pltpu.VMEM((jobs, rows, GROUP_WIDTH), jnp.bfloat16),
                pltpu.SemaphoreType.DMA((5 + jobs,)),
                *buffers_for(rows, span, block),
            ],
        ),
        compiler_params=pltpu.CompilerParams(vmem_limit_bytes=VMEM_LIMIT),
        cost_estimate=estimate(),
    )(meta, *args)


def place_kernel(meta, *refs):
    inputs, out, sems = refs[:-2], refs[-2], refs[-1]
    core, group = lax.rem(meta[0], 2), meta[1]
    copies = []
    for number, ref in enumerate(inputs):
        which, source = number % 2, number // 2
        flip_core, flip_group = source % 2, source // 2
        from_core = 1 - core if flip_core else core
        from_group = 1 - group if flip_group else group
        column = ((from_group * 2 + from_core) * 2 + which) * GROUP_WIDTH
        at = pl.ds(pl.multiple_of(column, GROUP_WIDTH), GROUP_WIDTH)
        copies.append(pltpu.make_async_copy(ref, out.at[:, at], sems.at[number]))
    for copy in copies:
        copy.start()
    for copy in copies:
        copy.wait()


def place(meta, arrays):
    rows = arrays[0].shape[0]
    return pl.pallas_call(
        place_kernel,
        out_shape=jax.ShapeDtypeStruct((rows, len(arrays) * GROUP_WIDTH), jnp.bfloat16),
        grid_spec=pltpu.PrefetchScalarGridSpec(
            num_scalar_prefetch=1,
            grid=(),
            in_specs=[pl.BlockSpec(memory_space=pltpu.VMEM)] * len(arrays),
            out_specs=pl.BlockSpec(memory_space=pltpu.HBM),
            scratch_shapes=[pltpu.SemaphoreType.DMA((len(arrays),))],
        ),
        compiler_params=pltpu.CompilerParams(vmem_limit_bytes=VMEM_LIMIT),
    )(meta, *arrays)


def own_kernel(meta, keys, values, their_ref, *outs):
    core = lax.rem(meta[0], 2)
    block = keys.shape[0]
    mine = pl.ds(pl.multiple_of(core * block, block), block)
    other = pl.ds(pl.multiple_of((1 - core) * block, block), block)
    for which, out_ref in enumerate(outs):
        column = 2 * core + which
        out_ref[mine, :HEAD_WIDTH] = keys[:, lanes(column)]
        out_ref[mine, HEAD_WIDTH:] = values[:, lanes(column)]
        for part in range(2):
            out_ref[other, part * HEAD_WIDTH : (part + 1) * HEAD_WIDTH] = their_ref[
                :, (2 * part + which) * HEAD_WIDTH : (2 * part + which + 1) * HEAD_WIDTH
            ]


def own_items(meta, keys, values, their_kv):
    block = keys.shape[0]
    item = jax.ShapeDtypeStruct((2 * block, 2 * HEAD_WIDTH), jnp.bfloat16)
    return pl.pallas_call(
        own_kernel,
        out_shape=[item, item],
        grid_spec=pltpu.PrefetchScalarGridSpec(
            num_scalar_prefetch=1,
            grid=(),
            in_specs=[pl.BlockSpec(memory_space=pltpu.VMEM)] * 3,
            out_specs=[pl.BlockSpec(memory_space=pltpu.VMEM)] * 2,
        ),
    )(meta, keys, values, their_kv)


def after(value, earlier):
    return pl.pallas_call(
        lambda *refs: None,
        out_shape=jax.ShapeDtypeStruct(value.shape, value.dtype),
        in_specs=[pl.BlockSpec(memory_space=pltpu.HBM)] * (1 + len(earlier)),
        out_specs=pl.BlockSpec(memory_space=pltpu.HBM),
        input_output_aliases={0: 0},
    )(value, *earlier)


def copy_kernel(meta, source, *refs):
    refs[-1][...] = source[...]


def swapped_columns(meta, queries, earlier):
    rows, width = queries.shape[0], queries.shape[1] // 4
    return pl.pallas_call(
        copy_kernel,
        out_shape=jax.ShapeDtypeStruct((rows, 2 * width), queries.dtype),
        grid_spec=pltpu.PrefetchScalarGridSpec(
            num_scalar_prefetch=1,
            grid=(2,),
            in_specs=[
                pl.BlockSpec(
                    (rows, width), lambda g, meta: (0, 2 * (1 - lax.rem(meta[0], 2)) + g)
                )
            ]
            + [pl.BlockSpec(memory_space=pltpu.HBM)] * len(earlier),
            out_specs=pl.BlockSpec((rows, width), lambda g, meta: (0, g)),
        ),
    )(meta, queries, *earlier)


def whole_kernel(meta, queries, gathered, out, window, q_jobs, out_jobs, sems, *work, which, block, span):
    jobs, rows = q_jobs.shape[0], q_jobs.shape[1]
    mine = meta[0]
    origin = mine - (span - 1)
    copies = []
    for slot in range(span):
        at = pl.ds(pl.multiple_of(jnp.maximum(origin + slot, 0) * block, block), block)
        copies.append(
            pltpu.make_async_copy(
                gathered.at[at], window.at[pl.ds(slot * block, block)], sems.at[jobs + slot]
            )
        )
    at = pl.ds(which * GROUP_WIDTH, GROUP_WIDTH)
    for job in range(jobs):
        copies.append(
            pltpu.make_async_copy(
                queries.at[pl.ds(job * rows, rows), at], q_jobs.at[job], sems.at[job]
            )
        )
    for copy in copies:
        copy.start()
    for copy in copies:
        copy.wait()
    attend_jobs(
        jobs,
        lambda job: (mine, job * rows),
        q_jobs,
        out_jobs,
        window,
        origin,
        meta,
        work,
        block,
        span,
    )
    copies = [
        pltpu.make_async_copy(out_jobs.at[job], out.at[pl.ds(job * rows, rows)], sems.at[job])
        for job in range(jobs)
    ]
    for copy in copies:
        copy.start()
    for copy in copies:
        copy.wait()


def shards_whole(meta, queries, keys, values, span):
    block, jobs = queries.shape[0], lax.axis_size("kvh")
    rows = block // jobs
    heads = []
    for which in range(keys.shape[1] // HEAD_WIDTH):
        at = slice(which * HEAD_WIDTH, (which + 1) * HEAD_WIDTH)
        item = jnp.concatenate([keys[:, at], values[:, at]], 1)
        gathered = lax.all_gather(item, "seq", axis=0, tiled=True)
        heads.append(
            pl.pallas_call(
                lambda *refs, which=which: whole_kernel(*refs, which=which, block=block, span=span),
                out_shape=jax.ShapeDtypeStruct((block, GROUP_WIDTH), jnp.bfloat16),
                grid_spec=pltpu.PrefetchScalarGridSpec(
                    num_scalar_prefetch=1,
                    grid=(),
                    in_specs=[pl.BlockSpec(memory_space=pltpu.HBM)] * 2,
                    out_specs=pl.BlockSpec(memory_space=pltpu.HBM),
                    scratch_shapes=[
                        pltpu.VMEM((span * block, 2 * HEAD_WIDTH), jnp.bfloat16),
                        pltpu.VMEM((jobs, rows, GROUP_WIDTH), jnp.bfloat16),
                        pltpu.VMEM((jobs, rows, GROUP_WIDTH), jnp.bfloat16),
                        pltpu.SemaphoreType.DMA((jobs + span,)),
                        *buffers_for(rows, span, block),
                    ],
                ),
                compiler_params=pltpu.CompilerParams(vmem_limit_bytes=VMEM_LIMIT),
            )(meta, queries, gathered)
        )
    return lax.all_to_all(
        jnp.concatenate(heads, 1), "kvh", split_axis=0, concat_axis=1, tiled=True
    )


def shards(queries, keys, values, answer_lengths):
    block = queries.shape[0]
    count, groups = lax.axis_size("seq"), lax.axis_size("kvh")
    span = min(12, count // 2)
    mine, group = lax.axis_index("seq"), lax.axis_index("kvh")
    meta = jnp.concatenate([jnp.stack([mine, group]).astype(jnp.int32), answer_lengths])
    if groups != 2 or span != 8 or count % 4 or keys.shape[1] != 4 * HEAD_WIDTH:
        return shards_whole(meta, queries, keys, values, span)
    core = lax.rem(mine, 2)
    rows = block // groups

    def theirs(value):
        width = value.shape[1] // 2
        return lax.dynamic_slice_in_dim(value, (1 - core) * width, width, 1)

    def permute(value, pairs):
        return lax.ppermute(value, "seq", pairs)

    swap = [(i, i ^ 1) for i in range(count)]
    ahead = [(i, i + 4) for i in range(count - 4)]
    rightward = [(i, i + 2) for i in range(count) if i % 4 < 2]
    leftward = [(i, i - 2) for i in range(count) if i % 4 >= 2]

    their_kv = permute(jnp.concatenate([theirs(keys), theirs(values)], 1), swap)

    def gather(own):
        near = permute(own, ahead)
        far = permute(near, ahead)
        side_own = permute(own, rightward)
        side_near = permute(near, rightward + leftward)
        side_far = permute(far, leftward)
        return [own, near, far, side_own, side_near, side_far]

    def send(value, flip_core, flip_group):
        pairs = [
            (i * groups + r, (i ^ flip_core) * groups + (r ^ flip_group))
            for i in range(count)
            for r in range(groups)
        ]
        return lax.ppermute(value, ("seq", "kvh"), pairs)

    def run(pieces, earlier, first_flip, flip_half, which, jobs):
        return attend_pair(
            meta, queries, their_queries, pieces, earlier, first_flip, flip_half, which, jobs, rows, span
        )

    own_first, own_second = own_items(meta, keys, values, their_kv)
    pieces = gather(own_first)
    their_queries = permute(swapped_columns(meta, queries, pieces[3:5]), swap)
    later = gather(after(own_second, pieces[2:3]))
    (far_a,) = run(pieces, (), 1, 1, 0, 1)
    got_far_a = send(far_a, 1, 1)
    (across_a,) = run(pieces, (far_a,), 0, 1, 0, 1)
    got_across_a = send(across_a, 0, 1)
    beside_a, own_a = run(pieces, (across_a,), 1, 0, 0, 2)
    got_beside_a = send(beside_a, 1, 0)
    far_b, across_b = run(later, (beside_a,), 1, 1, 1, 2)
    got_far_b = send(far_b, 1, 1)
    got_across_b = send(across_b, 0, 1)
    beside_b, own_b = run(later, (far_b, got_far_a), 1, 0, 1, 2)
    got_beside_b = send(beside_b, 1, 0)
    return place(
        meta,
        [
            own_a,
            own_b,
            got_beside_a,
            got_beside_b,
            got_across_a,
            got_across_b,
            got_far_a,
            got_far_b,
        ],
    )


def solution(mesh):
    in_specs = (P("seq", "kvh"), P("seq", "kvh"), P("seq", "kvh"), P())
    out_specs = P(("seq", "kvh"), None)
    return jax.shard_map(shards, mesh=mesh, in_specs=in_specs, out_specs=out_specs, check_vma=False)
```

```python
import math

import jax
import jax.numpy as jnp
from jax import lax
from jax.experimental import pallas as pl
from jax.experimental.pallas import tpu as pltpu
from jax.sharding import PartitionSpec as P

QUERY_PER_KEY = 12
HEAD_WIDTH = 128
GROUP_WIDTH = QUERY_PER_KEY * HEAD_WIDTH
SCALE_LOG2 = math.log2(math.e) / math.sqrt(HEAD_WIDTH)
VMEM_LIMIT = 62 * 1024 * 1024
STACK = 4
STACKS = QUERY_PER_KEY // STACK


def lanes(start):
    return pl.ds(pl.multiple_of(start * HEAD_WIDTH, HEAD_WIDTH), HEAD_WIDTH)


def first_visible(meta, position):
    end = jnp.int32(0)
    start = jnp.int32(0)
    for answer in range(2, meta.shape[0]):
        end = end + meta[answer]
        start = jnp.where(end <= position, end, start)
    return start


def attend_rows(count, offset, q_ref, out_ref, work, block):
    rows = q_ref.shape[0]
    stacked = STACK * rows
    window, nearest, shift, probs, stack, staged, facing = work[:7]
    width = count * block
    first = window.shape[0] - width
    tokens = lax.rem(lax.broadcasted_iota(jnp.int32, (stacked, block), 0), rows) + offset
    mask = lax.broadcasted_iota(jnp.int32, (stacked, block), 1) <= tokens

    def load(number):
        for h in range(STACK):
            stack[h * rows : (h + 1) * rows, :] = q_ref[:, lanes(number * STACK + h)]

    def score(slot):
        keys = window[first + slot * block : first + (slot + 1) * block, :HEAD_WIDTH]
        return lax.dot_general(
            stack[...], keys, (((1,), (1,)), ((), ())), preferred_element_type=jnp.float32
        )

    def begin():
        nearest[...] = jnp.where(mask, score(count - 1), -1e30)
        for h in range(STACK):
            at = slice(h * rows, (h + 1) * rows)
            ones = window[first : first + HEAD_WIDTH, 2 * HEAD_WIDTH :]
            same = jnp.dot(stack[at, :] * facing[...], ones, preferred_element_type=jnp.float32)
            shift[at, :] = same * SCALE_LOG2

    def soften(found, slot):
        for piece in range(block // HEAD_WIDTH):
            at = slice(piece * HEAD_WIDTH, (piece + 1) * HEAD_WIDTH)
            weights = jnp.exp2(found[:, at] * SCALE_LOG2 - shift[...])
            start = slot * block + piece * HEAD_WIDTH
            probs[:, start : start + HEAD_WIDTH] = weights.astype(jnp.bfloat16)

    def weigh():
        ahead = score(0) if count > 1 else None
        soften(nearest, count - 1)
        for slot in range(count - 1):
            found = ahead
            if slot < count - 2:
                ahead = score(slot + 1)
            soften(found, slot)

    def blend():
        found = jnp.dot(
            probs[:, :width], window[first:, HEAD_WIDTH:], preferred_element_type=jnp.float32
        )
        total = found[:, HEAD_WIDTH:]
        guess = pl.reciprocal(total, approx=True)
        guess = guess * (2.0 - total * guess)
        staged[...] = (found[:, :HEAD_WIDTH] * guess).astype(staged.dtype)
        return total

    def release(number):
        for h in range(STACK):
            out_ref[:, lanes(number * STACK + h)] = staged[h * rows : (h + 1) * rows]

    load(0)
    begin()

    def step(number, most):
        weigh()
        load(jnp.minimum(number + 1, STACKS - 1))
        begin()
        total = blend()
        for row in range(0, stacked, 8):
            most = jnp.maximum(most, total[row : row + 8])
        release(number)
        return most

    return jnp.max(lax.fori_loop(0, STACKS, step, jnp.zeros((8, HEAD_WIDTH), jnp.float32)))


def attend_rows_wide(visible, offset, q_ref, out_ref, work, block):
    rows = q_ref.shape[0]
    window, (peak, total, blended) = work[0], work[7:10]
    last = window.shape[0] - block
    tokens = lax.broadcasted_iota(jnp.int32, (rows, block), 0) + offset
    columns = lax.broadcasted_iota(jnp.int32, (rows, block), 1)

    @pl.loop(0, QUERY_PER_KEY)
    def _(head):
        peak[...] = jnp.full(peak.shape, -1e30, jnp.float32)
        total[...] = jnp.zeros(total.shape, jnp.float32)
        blended[...] = jnp.zeros(blended.shape, jnp.float32)

        @pl.loop(0, visible)
        def _(back):
            at = pl.ds(pl.multiple_of(last - back * block, block), block)
            found = lax.dot_general(
                q_ref[:, lanes(head)],
                window[at, :HEAD_WIDTH],
                (((1,), (1,)), ((), ())),
                preferred_element_type=jnp.float32,
            )
            found = jnp.where(columns <= tokens + back * block, found * SCALE_LOG2, -1e30)
            before = peak[...]
            now = jnp.maximum(before, jnp.max(found, axis=-1, keepdims=True))
            weights = jnp.exp2(found - now[:, :1])
            shrink = jnp.exp2(before - now)
            peak[...] = now
            total[...] = total[...] * shrink + jnp.sum(weights, axis=-1, keepdims=True)
            blended[...] = blended[...] * shrink + jnp.dot(
                weights.astype(jnp.bfloat16),
                window[at, HEAD_WIDTH : 2 * HEAD_WIDTH],
                preferred_element_type=jnp.float32,
            )

        out_ref[:, lanes(head)] = (blended[...] / total[...]).astype(out_ref.dtype)


def buffers_for(rows, span, block):
    stacked = STACK * rows
    return [
        pltpu.VMEM((span * block, 3 * HEAD_WIDTH), jnp.bfloat16),
        pltpu.VMEM((stacked, block), jnp.float32),
        pltpu.VMEM((stacked, HEAD_WIDTH), jnp.float32),
        pltpu.VMEM((stacked, span * block), jnp.bfloat16),
        pltpu.VMEM((stacked, HEAD_WIDTH), jnp.bfloat16),
        pltpu.VMEM((stacked, HEAD_WIDTH), jnp.bfloat16),
        pltpu.VMEM((rows, HEAD_WIDTH), jnp.bfloat16),
        pltpu.VMEM((rows, HEAD_WIDTH), jnp.float32),
        pltpu.VMEM((rows, HEAD_WIDTH), jnp.float32),
        pltpu.VMEM((rows, HEAD_WIDTH), jnp.float32),
        pltpu.SMEM((1,), jnp.float32),
    ]


WORK = 11


def attend_jobs(jobs, position_of, q_jobs, out_jobs, arrived, origin, meta, work, block, span, done=None):
    work[0][:, 2 * HEAD_WIDTH :] = jnp.ones((span * block, HEAD_WIDTH), jnp.bfloat16)

    @pl.loop(0, jobs)
    def _(job):
        index, offset = position_of(job)
        start = lax.div(first_visible(meta, index * block), block)
        visible = index - start + 1
        last = (index - origin + 1 - span) * block
        window, facing, most = work[0], work[6], work[10]
        moved = pl.ds(pl.multiple_of(last, block), span * block)
        window[:, : 2 * HEAD_WIDTH] = arrived[moved, :]
        here = pl.ds(pl.multiple_of(last + (span - 1) * block + offset, facing.shape[0]), facing.shape[0])
        facing[...] = arrived[here, :HEAD_WIDTH]
        for count in range(1, span + 1):

            @pl.when(visible == count)
            def _():
                most[0] = attend_rows(count, offset, q_jobs.at[job], out_jobs.at[job], work, block)

        @pl.when(jnp.logical_not(most[0] < 2.0**120))
        def _():
            attend_rows_wide(visible, offset, q_jobs.at[job], out_jobs.at[job], work, block)

        if done is not None:
            done(job)


def pair_kernel(meta, queries, theirs, *refs, first_flip, flip_half, which, jobs, block, span):
    own, near, far, side_own, side_near, side_far = refs[:6]
    window, q_jobs, out_jobs, sems = refs[-4 - WORK : -WORK]
    outs = refs[-4 - WORK - jobs : -4 - WORK]
    work = refs[-WORK:]
    rows = q_jobs.shape[1]
    mine, group = meta[0], meta[1]
    core = lax.rem(mine, 2)
    right = lax.rem(lax.div(mine, 2), 2)
    origin = mine - core - (span - 1)
    half = 1 - group if flip_half else group

    def fill(source, source_row, slot, size, sem):
        return pltpu.make_async_copy(
            source.at[pl.ds(source_row, size)], window.at[pl.ds(slot * block, size)], sems.at[sem]
        )

    fixed = [
        fill(far, block, 0, block, 0),
        fill(near, 0, 3, 2 * block, 1),
        fill(own, 0, 7, 2 * block, 2),
    ]
    by_side = [
        (fill(side_far, 0, 1, 2 * block, 3), fill(side_near, 0, 1, 2 * block, 3)),
        (fill(side_near, 0, 5, 2 * block, 4), fill(side_own, 0, 5, 2 * block, 4)),
    ]
    for job in range(jobs):
        flip = first_flip - job
        source = theirs if flip else queries
        at = pl.ds(pl.multiple_of((2 * core + which) * GROUP_WIDTH, GROUP_WIDTH), GROUP_WIDTH)
        fixed.append(
            pltpu.make_async_copy(
                source.at[pl.ds(pl.multiple_of(half * rows, rows), rows), at],
                q_jobs.at[job],
                sems.at[5 + job],
            )
        )
    for copy in fixed:
        copy.start()
    for on_left, on_right in by_side:
        pl.when(right == 0)(on_left.start)
        pl.when(right == 1)(on_right.start)
    for copy in fixed:
        copy.wait()
    for on_left, _ in by_side:
        on_left.wait()

    def position_of(job):
        flip = first_flip - job
        return mine - core + jnp.where(flip == 1, 1 - core, core), half * rows

    copies = [
        pltpu.make_async_copy(out_jobs.at[job], out, sems.at[5 + job])
        for job, out in enumerate(outs)
    ]

    def done(job):
        for number, copy in enumerate(copies):
            pl.when(job == number)(copy.start)

    attend_jobs(
        jobs, position_of, q_jobs, out_jobs, window, origin, meta, work, block, span, done
    )
    for copy in copies:
        copy.wait()


def estimate():
    return pl.CostEstimate(flops=400_000_000, bytes_accessed=400_000, transcendentals=0)


def attend_pair(meta, queries, theirs, pieces, earlier, first_flip, flip_half, which, jobs, rows, span):
    block = queries.shape[0]
    args = [queries, theirs, *pieces, *earlier]
    return pl.pallas_call(
        lambda *refs: pair_kernel(
            *refs,
            first_flip=first_flip,
            flip_half=flip_half,
            which=which,
            jobs=jobs,
            block=block,
            span=span,
        ),
        out_shape=[jax.ShapeDtypeStruct((rows, GROUP_WIDTH), jnp.bfloat16)] * jobs,
        grid_spec=pltpu.PrefetchScalarGridSpec(
            num_scalar_prefetch=1,
            grid=(),
            in_specs=[pl.BlockSpec(memory_space=pltpu.HBM)] * len(args),
            out_specs=[pl.BlockSpec(memory_space=pltpu.HBM)] * jobs,
            scratch_shapes=[
                pltpu.VMEM(((span + 1) * block, 2 * HEAD_WIDTH), jnp.bfloat16),
                pltpu.VMEM((jobs, rows, GROUP_WIDTH), jnp.bfloat16),
                pltpu.VMEM((jobs, rows, GROUP_WIDTH), jnp.bfloat16),
                pltpu.SemaphoreType.DMA((5 + jobs,)),
                *buffers_for(rows, span, block),
            ],
        ),
        compiler_params=pltpu.CompilerParams(vmem_limit_bytes=VMEM_LIMIT),
        cost_estimate=estimate(),
    )(meta, *args)


def place_kernel(meta, *refs, which, count):
    inputs, out, held, sems = refs[:count], refs[-3], refs[-2], refs[-1]
    core, group = lax.rem(meta[0], 2), meta[1]
    loads, stores = [], []
    for source, ref in enumerate(inputs):
        flip_core, flip_group = source % 2, source // 2
        from_core = 1 - core if flip_core else core
        from_group = 1 - group if flip_group else group
        column = ((from_group * 2 + from_core) * 2 + which) * GROUP_WIDTH
        at = pl.ds(pl.multiple_of(column, GROUP_WIDTH), GROUP_WIDTH)
        loads.append(pltpu.make_async_copy(ref, held.at[source], sems.at[0, source]))
        stores.append(pltpu.make_async_copy(held.at[source], out.at[:, at], sems.at[1, source]))
    for load in loads:
        load.start()
    for load, store in zip(loads, stores):
        load.wait()
        store.start()
    for store in stores:
        store.wait()


def place(meta, arrays, which, out=None):
    rows, count = arrays[0].shape[0], len(arrays)
    held = () if out is None else (out,)
    return pl.pallas_call(
        lambda *refs: place_kernel(*refs, which=which, count=count),
        out_shape=jax.ShapeDtypeStruct((rows, 2 * count * GROUP_WIDTH), jnp.bfloat16),
        grid_spec=pltpu.PrefetchScalarGridSpec(
            num_scalar_prefetch=1,
            grid=(),
            in_specs=[pl.BlockSpec(memory_space=pl.ANY)] * (count + len(held)),
            out_specs=pl.BlockSpec(memory_space=pltpu.HBM),
            scratch_shapes=[
                pltpu.VMEM((count, rows, GROUP_WIDTH), jnp.bfloat16),
                pltpu.SemaphoreType.DMA((2, count)),
            ],
        ),
        input_output_aliases={1 + count: 0} if held else {},
        compiler_params=pltpu.CompilerParams(vmem_limit_bytes=8 * 1024 * 1024),
        cost_estimate=pl.CostEstimate(flops=0, bytes_accessed=3_000_000, transcendentals=0),
    )(meta, *arrays, *held)


def own_kernel(meta, keys, values, theirs, *refs):
    outs, items, sems = refs[:2], refs[2], refs[3]
    core = lax.rem(meta[0], 2)
    block = keys.shape[0]
    mine = pl.ds(pl.multiple_of(core * block, block), block)
    other = pl.ds(pl.multiple_of((1 - core) * block, block), block)
    loads = []
    for which in range(2):
        for part, source in enumerate((keys, values)):
            at = slice(part * HEAD_WIDTH, (part + 1) * HEAD_WIDTH)
            loads.append((source.at[:, lanes(2 * core + which)], items.at[which, mine, at]))
            from_them = slice((2 * part + which) * HEAD_WIDTH, (2 * part + which + 1) * HEAD_WIDTH)
            loads.append((theirs.at[:, from_them], items.at[which, other, at]))
    loads = [
        pltpu.make_async_copy(source, target, sems.at[number])
        for number, (source, target) in enumerate(loads)
    ]
    stores = [
        pltpu.make_async_copy(items.at[which], outs[which], sems.at[8 + which])
        for which in range(2)
    ]
    for load in loads:
        load.start()
    for which in range(2):
        for load in loads[4 * which : 4 * which + 4]:
            load.wait()
        stores[which].start()
    for store in stores:
        store.wait()


def own_items(meta, keys, values, their_kv):
    block = keys.shape[0]
    shape = (2 * block, 2 * HEAD_WIDTH)
    return pl.pallas_call(
        own_kernel,
        out_shape=[jax.ShapeDtypeStruct(shape, jnp.bfloat16)] * 2,
        grid_spec=pltpu.PrefetchScalarGridSpec(
            num_scalar_prefetch=1,
            grid=(),
            in_specs=[pl.BlockSpec(memory_space=pl.ANY)] * 3,
            out_specs=[pl.BlockSpec(memory_space=pl.ANY)] * 2,
            scratch_shapes=[pltpu.VMEM((2, *shape), jnp.bfloat16), pltpu.SemaphoreType.DMA((10,))],
        ),
        compiler_params=pltpu.CompilerParams(vmem_limit_bytes=8 * 1024 * 1024),
    )(meta, keys, values, their_kv)


def after(value, earlier):
    return pl.pallas_call(
        lambda *refs: None,
        out_shape=jax.ShapeDtypeStruct(value.shape, value.dtype),
        in_specs=[pl.BlockSpec(memory_space=pltpu.HBM)] * (1 + len(earlier)),
        out_specs=pl.BlockSpec(memory_space=pltpu.HBM),
        input_output_aliases={0: 0},
    )(value, *earlier)


def whole_kernel(meta, queries, gathered, out, window, q_jobs, out_jobs, sems, *work, which, block, span):
    jobs, rows = q_jobs.shape[0], q_jobs.shape[1]
    mine = meta[0]
    origin = mine - (span - 1)
    copies = []
    for slot in range(span):
        at = pl.ds(pl.multiple_of(jnp.maximum(origin + slot, 0) * block, block), block)
        copies.append(
            pltpu.make_async_copy(
                gathered.at[at], window.at[pl.ds(slot * block, block)], sems.at[jobs + slot]
            )
        )
    at = pl.ds(which * GROUP_WIDTH, GROUP_WIDTH)
    for job in range(jobs):
        copies.append(
            pltpu.make_async_copy(
                queries.at[pl.ds(job * rows, rows), at], q_jobs.at[job], sems.at[job]
            )
        )
    for copy in copies:
        copy.start()
    for copy in copies:
        copy.wait()
    attend_jobs(
        jobs,
        lambda job: (mine, job * rows),
        q_jobs,
        out_jobs,
        window,
        origin,
        meta,
        work,
        block,
        span,
    )
    copies = [
        pltpu.make_async_copy(out_jobs.at[job], out.at[pl.ds(job * rows, rows)], sems.at[job])
        for job in range(jobs)
    ]
    for copy in copies:
        copy.start()
    for copy in copies:
        copy.wait()


def shards_whole(meta, queries, keys, values, span):
    block, jobs = queries.shape[0], lax.axis_size("kvh")
    rows = block // jobs
    heads = []
    for which in range(keys.shape[1] // HEAD_WIDTH):
        at = slice(which * HEAD_WIDTH, (which + 1) * HEAD_WIDTH)
        item = jnp.concatenate([keys[:, at], values[:, at]], 1)
        gathered = lax.all_gather(item, "seq", axis=0, tiled=True)
        heads.append(
            pl.pallas_call(
                lambda *refs, which=which: whole_kernel(*refs, which=which, block=block, span=span),
                out_shape=jax.ShapeDtypeStruct((block, GROUP_WIDTH), jnp.bfloat16),
                grid_spec=pltpu.PrefetchScalarGridSpec(
                    num_scalar_prefetch=1,
                    grid=(),
                    in_specs=[pl.BlockSpec(memory_space=pltpu.HBM)] * 2,
                    out_specs=pl.BlockSpec(memory_space=pltpu.HBM),
                    scratch_shapes=[
                        pltpu.VMEM((span * block, 2 * HEAD_WIDTH), jnp.bfloat16),
                        pltpu.VMEM((jobs, rows, GROUP_WIDTH), jnp.bfloat16),
                        pltpu.VMEM((jobs, rows, GROUP_WIDTH), jnp.bfloat16),
                        pltpu.SemaphoreType.DMA((jobs + span,)),
                        *buffers_for(rows, span, block),
                    ],
                ),
                compiler_params=pltpu.CompilerParams(vmem_limit_bytes=VMEM_LIMIT),
            )(meta, queries, gathered)
        )
    return lax.all_to_all(
        jnp.concatenate(heads, 1), "kvh", split_axis=0, concat_axis=1, tiled=True
    )


def shards(queries, keys, values, answer_lengths):
    block = queries.shape[0]
    count, groups = lax.axis_size("seq"), lax.axis_size("kvh")
    span = min(12, count // 2)
    mine, group = lax.axis_index("seq"), lax.axis_index("kvh")
    meta = jnp.concatenate([jnp.stack([mine, group]).astype(jnp.int32), answer_lengths])
    if groups != 2 or span != 8 or count % 4 or keys.shape[1] != 4 * HEAD_WIDTH:
        return shards_whole(meta, queries, keys, values, span)
    core = lax.rem(mine, 2)
    rows = block // groups

    def theirs(value):
        width = value.shape[1] // 2
        return lax.dynamic_slice_in_dim(value, (1 - core) * width, width, 1)

    def permute(value, pairs):
        return lax.ppermute(value, "seq", pairs)

    swap = [(i, i ^ 1) for i in range(count)]
    ahead = [(i, i + 4) for i in range(count - 4)]
    rightward = [(i, i + 2) for i in range(count) if i % 4 < 2]
    leftward = [(i, i - 2) for i in range(count) if i % 4 >= 2]

    their_queries = permute(queries, swap)
    their_kv = permute(jnp.concatenate([theirs(keys), theirs(values)], 1), swap)

    def gather(own):
        near = permute(own, ahead)
        far = permute(near, ahead)
        side_own = permute(own, rightward)
        side_near = permute(near, rightward + leftward)
        side_far = permute(far, leftward)
        return [own, near, far, side_own, side_near, side_far]

    def send(value, flip_core, flip_group):
        pairs = [
            (i * groups + r, (i ^ flip_core) * groups + (r ^ flip_group))
            for i in range(count)
            for r in range(groups)
        ]
        return lax.ppermute(value, ("seq", "kvh"), pairs)

    def run(pieces, earlier, first_flip, flip_half, which, jobs):
        return attend_pair(
            meta, queries, their_queries, pieces, earlier, first_flip, flip_half, which, jobs, rows, span
        )

    own_first, own_second = own_items(meta, keys, values, their_kv)
    pieces = gather(own_first)
    later = gather(after(own_second, pieces[2:5]))
    far_a, across_a = run(pieces, (), 1, 1, 0, 2)
    got_far_a = send(far_a, 1, 1)
    got_across_a = send(across_a, 0, 1)
    beside_a, own_a = run(pieces, (far_a,), 1, 0, 0, 2)
    got_beside_a = send(beside_a, 1, 0)
    far_b, across_b = run(later, (beside_a,), 1, 1, 1, 2)
    got_far_b = send(far_b, 1, 1)
    got_across_b = send(across_b, 0, 1)
    (beside_b,) = run(later, (far_b, got_far_a), 1, 0, 1, 1)
    got_beside_b = send(beside_b, 1, 0)
    (own_b,) = run(later, (beside_b,), 0, 0, 1, 1)
    out = place(meta, [own_a, got_beside_a, got_across_a, got_far_a], 0)
    return place(meta, [own_b, got_beside_b, got_across_b, got_far_b], 1, out)


def solution(mesh):
    in_specs = (P("seq", "kvh"), P("seq", "kvh"), P("seq", "kvh"), P())
    out_specs = P(("seq", "kvh"), None)
    return jax.shard_map(shards, mesh=mesh, in_specs=in_specs, out_specs=out_specs, check_vma=False)
```

```python
import math

import jax
import jax.numpy as jnp
from jax import lax
from jax.experimental import pallas as pl
from jax.experimental.pallas import tpu as pltpu
from jax.sharding import PartitionSpec as P

QUERY_PER_KEY = 12
HEAD_WIDTH = 128
GROUP_WIDTH = QUERY_PER_KEY * HEAD_WIDTH
SCALE_LOG2 = math.log2(math.e) / math.sqrt(HEAD_WIDTH)
VMEM_LIMIT = 62 * 1024 * 1024
STACK = 4
STACKS = QUERY_PER_KEY // STACK


def lanes(start):
    return pl.ds(pl.multiple_of(start * HEAD_WIDTH, HEAD_WIDTH), HEAD_WIDTH)


def first_visible(meta, position):
    end = jnp.int32(0)
    start = jnp.int32(0)
    for answer in range(2, meta.shape[0]):
        end = end + meta[answer]
        start = jnp.where(end <= position, end, start)
    return start


def attend_rows(count, offset, q_ref, out_ref, work, block):
    rows = q_ref.shape[0]
    stacked = STACK * rows
    window, nearest, shift, probs, stack, staged, facing = work[:7]
    width = count * block
    first = window.shape[0] - width
    tokens = lax.rem(lax.broadcasted_iota(jnp.int32, (stacked, block), 0), rows) + offset
    mask = lax.broadcasted_iota(jnp.int32, (stacked, block), 1) <= tokens

    def load(number):
        for h in range(STACK):
            stack[h * rows : (h + 1) * rows, :] = q_ref[:, lanes(number * STACK + h)]

    def score(slot):
        keys = window[first + slot * block : first + (slot + 1) * block, :HEAD_WIDTH]
        return lax.dot_general(
            stack[...], keys, (((1,), (1,)), ((), ())), preferred_element_type=jnp.float32
        )

    def begin():
        nearest[...] = jnp.where(mask, score(count - 1), -1e30)
        for h in range(STACK):
            at = slice(h * rows, (h + 1) * rows)
            ones = window[first : first + HEAD_WIDTH, 2 * HEAD_WIDTH :]
            same = jnp.dot(stack[at, :] * facing[...], ones, preferred_element_type=jnp.float32)
            shift[at, :] = same * SCALE_LOG2

    def soften(found, slot):
        for piece in range(block // HEAD_WIDTH):
            at = slice(piece * HEAD_WIDTH, (piece + 1) * HEAD_WIDTH)
            weights = jnp.exp2(found[:, at] * SCALE_LOG2 - shift[...])
            start = slot * block + piece * HEAD_WIDTH
            probs[:, start : start + HEAD_WIDTH] = weights.astype(jnp.bfloat16)

    def weigh():
        ahead = score(0) if count > 1 else None
        soften(nearest, count - 1)
        for slot in range(count - 1):
            found = ahead
            if slot < count - 2:
                ahead = score(slot + 1)
            soften(found, slot)

    def blend():
        found = jnp.dot(
            probs[:, :width], window[first:, HEAD_WIDTH:], preferred_element_type=jnp.float32
        )
        total = found[:, HEAD_WIDTH:]
        guess = pl.reciprocal(total, approx=True)
        guess = guess * (2.0 - total * guess)
        staged[...] = (found[:, :HEAD_WIDTH] * guess).astype(staged.dtype)
        return total

    def release(number):
        for h in range(STACK):
            out_ref[:, lanes(number * STACK + h)] = staged[h * rows : (h + 1) * rows]

    load(0)
    begin()

    def step(number, most):
        weigh()
        load(jnp.minimum(number + 1, STACKS - 1))
        begin()
        total = blend()
        for row in range(0, stacked, 8):
            most = jnp.maximum(most, total[row : row + 8])
        release(number)
        return most

    return jnp.max(lax.fori_loop(0, STACKS, step, jnp.zeros((8, HEAD_WIDTH), jnp.float32)))


def attend_rows_wide(visible, offset, q_ref, out_ref, work, block):
    rows = q_ref.shape[0]
    window, (peak, total, blended) = work[0], work[7:10]
    last = window.shape[0] - block
    tokens = lax.broadcasted_iota(jnp.int32, (rows, block), 0) + offset
    columns = lax.broadcasted_iota(jnp.int32, (rows, block), 1)

    @pl.loop(0, QUERY_PER_KEY)
    def _(head):
        peak[...] = jnp.full(peak.shape, -1e30, jnp.float32)
        total[...] = jnp.zeros(total.shape, jnp.float32)
        blended[...] = jnp.zeros(blended.shape, jnp.float32)

        @pl.loop(0, visible)
        def _(back):
            at = pl.ds(pl.multiple_of(last - back * block, block), block)
            found = lax.dot_general(
                q_ref[:, lanes(head)],
                window[at, :HEAD_WIDTH],
                (((1,), (1,)), ((), ())),
                preferred_element_type=jnp.float32,
            )
            found = jnp.where(columns <= tokens + back * block, found * SCALE_LOG2, -1e30)
            before = peak[...]
            now = jnp.maximum(before, jnp.max(found, axis=-1, keepdims=True))
            weights = jnp.exp2(found - now[:, :1])
            shrink = jnp.exp2(before - now)
            peak[...] = now
            total[...] = total[...] * shrink + jnp.sum(weights, axis=-1, keepdims=True)
            blended[...] = blended[...] * shrink + jnp.dot(
                weights.astype(jnp.bfloat16),
                window[at, HEAD_WIDTH : 2 * HEAD_WIDTH],
                preferred_element_type=jnp.float32,
            )

        out_ref[:, lanes(head)] = (blended[...] / total[...]).astype(out_ref.dtype)


def buffers_for(rows, span, block):
    stacked = STACK * rows
    return [
        pltpu.VMEM((span * block, 3 * HEAD_WIDTH), jnp.bfloat16),
        pltpu.VMEM((stacked, block), jnp.float32),
        pltpu.VMEM((stacked, HEAD_WIDTH), jnp.float32),
        pltpu.VMEM((stacked, span * block), jnp.bfloat16),
        pltpu.VMEM((stacked, HEAD_WIDTH), jnp.bfloat16),
        pltpu.VMEM((stacked, HEAD_WIDTH), jnp.bfloat16),
        pltpu.VMEM((rows, HEAD_WIDTH), jnp.bfloat16),
        pltpu.VMEM((rows, HEAD_WIDTH), jnp.float32),
        pltpu.VMEM((rows, HEAD_WIDTH), jnp.float32),
        pltpu.VMEM((rows, HEAD_WIDTH), jnp.float32),
        pltpu.SMEM((1,), jnp.float32),
    ]


WORK = 11


def attend_jobs(jobs, position_of, q_jobs, out_jobs, arrived, origin, meta, work, block, span, done=None):
    work[0][:, 2 * HEAD_WIDTH :] = jnp.ones((span * block, HEAD_WIDTH), jnp.bfloat16)

    @pl.loop(0, jobs)
    def _(job):
        index, offset = position_of(job)
        start = lax.div(first_visible(meta, index * block), block)
        visible = index - start + 1
        last = (index - origin + 1 - span) * block
        window, facing, most = work[0], work[6], work[10]
        moved = pl.ds(pl.multiple_of(last, block), span * block)
        window[:, : 2 * HEAD_WIDTH] = arrived[moved, :]
        here = pl.ds(pl.multiple_of(last + (span - 1) * block + offset, facing.shape[0]), facing.shape[0])
        facing[...] = arrived[here, :HEAD_WIDTH]
        for count in range(1, span + 1):

            @pl.when(visible == count)
            def _():
                most[0] = attend_rows(count, offset, q_jobs.at[job], out_jobs.at[job], work, block)

        @pl.when(jnp.logical_not(most[0] < 2.0**120))
        def _():
            attend_rows_wide(visible, offset, q_jobs.at[job], out_jobs.at[job], work, block)

        if done is not None:
            done(job)


PARTS = (0, 1, 2, 3)


def place_columns(meta, source, which):
    core, group = lax.rem(meta[0], 2), meta[1]
    from_core = 1 - core if source % 2 else core
    from_group = 1 - group if source // 2 else group
    column = ((from_group * 2 + from_core) * 2 + which) * GROUP_WIDTH
    return pl.ds(pl.multiple_of(column, GROUP_WIDTH), GROUP_WIDTH)


def place_copies(meta, inputs, sources, which, out, held, sems):
    loads, stores = [], []
    for number, (source, ref) in enumerate(zip(sources, inputs)):
        at = place_columns(meta, source, which)
        loads.append(pltpu.make_async_copy(ref, held.at[number], sems.at[0, number]))
        stores.append(pltpu.make_async_copy(held.at[number], out.at[:, at], sems.at[1, number]))
    return loads, stores


def place_kernel(meta, *refs, which, count):
    out, held, sems = refs[-3:]
    loads, stores = place_copies(meta, refs[:count], PARTS[:0:-1], which, out, held, sems)
    for load in loads:
        load.start()
    for load, store in zip(loads, stores):
        load.wait()
        store.start()
    for store in stores:
        store.wait()


def place(meta, arrays, which, out):
    rows, count = arrays[0].shape[0], len(arrays)
    return pl.pallas_call(
        lambda *refs: place_kernel(*refs, which=which, count=count),
        out_shape=jax.ShapeDtypeStruct(out.shape, out.dtype),
        grid_spec=pltpu.PrefetchScalarGridSpec(
            num_scalar_prefetch=1,
            grid=(),
            in_specs=[pl.BlockSpec(memory_space=pl.ANY)] * (count + 1),
            out_specs=pl.BlockSpec(memory_space=pltpu.HBM),
            scratch_shapes=[
                pltpu.VMEM((count, rows, GROUP_WIDTH), jnp.bfloat16),
                pltpu.SemaphoreType.DMA((2, count)),
            ],
        ),
        input_output_aliases={1 + count: 0},
        compiler_params=pltpu.CompilerParams(vmem_limit_bytes=8 * 1024 * 1024),
        cost_estimate=pl.CostEstimate(flops=0, bytes_accessed=3_000_000, transcendentals=0),
    )(meta, *arrays, out)


def pair_kernel(
    meta, queries, theirs, *refs, first_flip, flip_half, which, jobs, block, span, pieces, placed
):
    window, q_jobs, out_jobs, sems, held, held_sems = refs[-6 - WORK : -WORK]
    outs = refs[-6 - WORK - jobs : -6 - WORK]
    work = refs[-WORK:]
    rows = q_jobs.shape[1]
    mine, group = meta[0], meta[1]
    core = lax.rem(mine, 2)
    right = lax.rem(lax.div(mine, 2), 2)
    origin = mine - core - (span - 1)
    half = 1 - group if flip_half else group

    def fill(source, source_row, slot, size, sem):
        return pltpu.make_async_copy(
            source.at[pl.ds(source_row, size)], window.at[pl.ds(slot * block, size)], sems.at[sem]
        )

    if pieces == 1:
        chip = lax.div(mine, 2)

        def from_chip(back):
            return pl.multiple_of(jnp.maximum(chip - back, 0) * 2 * block, 2 * block)

        fixed = [fill(refs[0], from_chip(4) + block, 0, block, 0)]
        for number, back in enumerate((3, 2, 1, 0)):
            fixed.append(fill(refs[0], from_chip(back), 2 * number + 1, 2 * block, number + 1))
        by_side = []
    else:
        own, near, far, side_own, side_near, side_far = refs[:6]
        fixed = [
            fill(far, block, 0, block, 0),
            fill(near, 0, 3, 2 * block, 1),
            fill(own, 0, 7, 2 * block, 2),
        ]
        by_side = [
            (fill(side_far, 0, 1, 2 * block, 3), fill(side_near, 0, 1, 2 * block, 3)),
            (fill(side_near, 0, 5, 2 * block, 4), fill(side_own, 0, 5, 2 * block, 4)),
        ]
    for job in range(jobs):
        flip = first_flip - job
        source = theirs if flip else queries
        at = pl.ds(pl.multiple_of((2 * core + which) * GROUP_WIDTH, GROUP_WIDTH), GROUP_WIDTH)
        fixed.append(
            pltpu.make_async_copy(
                source.at[pl.ds(pl.multiple_of(half * rows, rows), rows), at],
                q_jobs.at[job],
                sems.at[5 + job],
            )
        )
    for copy in fixed:
        copy.start()
    for on_left, on_right in by_side:
        pl.when(right == 0)(on_left.start)
        pl.when(right == 1)(on_right.start)
    for copy in fixed:
        copy.wait()
    for on_left, _ in by_side:
        on_left.wait()

    def position_of(job):
        flip = first_flip - job
        return mine - core + jnp.where(flip == 1, 1 - core, core), half * rows

    if placed:
        loads, stores = place_copies(
            meta, refs[pieces : pieces + placed], PARTS, 0, outs[0], held, held_sems
        )
        for load in loads:
            load.start()
        targets = [outs[0].at[:, place_columns(meta, 0, which)]]
    else:
        loads, stores = [], []
        targets = outs
    copies = [
        pltpu.make_async_copy(out_jobs.at[job], out, sems.at[5 + job])
        for job, out in enumerate(targets)
    ]

    def done(job):
        for number, copy in enumerate(copies):
            pl.when(job == number)(copy.start)

    attend_jobs(
        jobs, position_of, q_jobs, out_jobs, window, origin, meta, work, block, span, done
    )
    for load, store in zip(loads, stores):
        load.wait()
        store.start()
    for copy in [*stores, *copies]:
        copy.wait()


def estimate(long=False):
    flops = 8_000_000_000 if long else 400_000_000
    return pl.CostEstimate(flops=flops, bytes_accessed=400_000, transcendentals=0)


def attend_pair(
    meta, queries, theirs, pieces, placed, earlier, first_flip, flip_half, which, jobs, rows, span
):
    block = queries.shape[0]
    args = [queries, theirs, *pieces, *placed, *earlier]
    width = 8 * GROUP_WIDTH if placed else GROUP_WIDTH
    return pl.pallas_call(
        lambda *refs: pair_kernel(
            *refs,
            first_flip=first_flip,
            flip_half=flip_half,
            which=which,
            jobs=jobs,
            block=block,
            span=span,
            pieces=len(pieces),
            placed=len(placed),
        ),
        out_shape=[jax.ShapeDtypeStruct((rows, width), jnp.bfloat16)] * jobs,
        grid_spec=pltpu.PrefetchScalarGridSpec(
            num_scalar_prefetch=1,
            grid=(),
            in_specs=[pl.BlockSpec(memory_space=pltpu.HBM)] * len(args),
            out_specs=[pl.BlockSpec(memory_space=pltpu.HBM)] * jobs,
            scratch_shapes=[
                pltpu.VMEM(((span + 1) * block, 2 * HEAD_WIDTH), jnp.bfloat16),
                pltpu.VMEM((jobs, rows, GROUP_WIDTH), jnp.bfloat16),
                pltpu.VMEM((jobs, rows, GROUP_WIDTH), jnp.bfloat16),
                pltpu.SemaphoreType.DMA((5 + jobs,)),
                pltpu.VMEM((max(len(placed), 1), rows, GROUP_WIDTH), jnp.bfloat16),
                pltpu.SemaphoreType.DMA((2, max(len(placed), 1))),
                *buffers_for(rows, span, block),
            ],
        ),
        compiler_params=pltpu.CompilerParams(vmem_limit_bytes=VMEM_LIMIT),
        cost_estimate=estimate(len(placed) > 0),
    )(meta, *args)


def own_kernel(meta, keys, values, theirs, *refs):
    outs, items, sems = refs[:2], refs[2], refs[3]
    core = lax.rem(meta[0], 2)
    block = keys.shape[0]
    mine = pl.ds(pl.multiple_of(core * block, block), block)
    other = pl.ds(pl.multiple_of((1 - core) * block, block), block)
    loads = []
    for which in range(2):
        for part, source in enumerate((keys, values)):
            at = slice(part * HEAD_WIDTH, (part + 1) * HEAD_WIDTH)
            loads.append((source.at[:, lanes(2 * core + which)], items.at[which, mine, at]))
            from_them = slice((2 * part + which) * HEAD_WIDTH, (2 * part + which + 1) * HEAD_WIDTH)
            loads.append((theirs.at[:, from_them], items.at[which, other, at]))
    loads = [
        pltpu.make_async_copy(source, target, sems.at[number])
        for number, (source, target) in enumerate(loads)
    ]
    stores = [
        pltpu.make_async_copy(items.at[which], outs[which], sems.at[8 + which])
        for which in range(2)
    ]
    for load in loads:
        load.start()
    for which in range(2):
        for load in loads[4 * which : 4 * which + 4]:
            load.wait()
        stores[which].start()
    for store in stores:
        store.wait()


def own_items(meta, keys, values, their_kv):
    block = keys.shape[0]
    shape = (2 * block, 2 * HEAD_WIDTH)
    return pl.pallas_call(
        own_kernel,
        out_shape=[jax.ShapeDtypeStruct(shape, jnp.bfloat16)] * 2,
        grid_spec=pltpu.PrefetchScalarGridSpec(
            num_scalar_prefetch=1,
            grid=(),
            in_specs=[pl.BlockSpec(memory_space=pltpu.HBM)] * 3,
            out_specs=[pl.BlockSpec(memory_space=pltpu.HBM)] * 2,
            scratch_shapes=[pltpu.VMEM((2, *shape), jnp.bfloat16), pltpu.SemaphoreType.DMA((10,))],
        ),
        compiler_params=pltpu.CompilerParams(vmem_limit_bytes=VMEM_LIMIT),
    )(meta, keys, values, their_kv)


def after(value, earlier):
    return pl.pallas_call(
        lambda *refs: None,
        out_shape=jax.ShapeDtypeStruct(value.shape, value.dtype),
        in_specs=[pl.BlockSpec(memory_space=pltpu.HBM)] * (1 + len(earlier)),
        out_specs=pl.BlockSpec(memory_space=pltpu.HBM),
        input_output_aliases={0: 0},
    )(value, *earlier)


def whole_kernel(meta, queries, gathered, out, window, q_jobs, out_jobs, sems, *work, which, block, span):
    jobs, rows = q_jobs.shape[0], q_jobs.shape[1]
    mine = meta[0]
    origin = mine - (span - 1)
    copies = []
    for slot in range(span):
        at = pl.ds(pl.multiple_of(jnp.maximum(origin + slot, 0) * block, block), block)
        copies.append(
            pltpu.make_async_copy(
                gathered.at[at], window.at[pl.ds(slot * block, block)], sems.at[jobs + slot]
            )
        )
    at = pl.ds(which * GROUP_WIDTH, GROUP_WIDTH)
    for job in range(jobs):
        copies.append(
            pltpu.make_async_copy(
                queries.at[pl.ds(job * rows, rows), at], q_jobs.at[job], sems.at[job]
            )
        )
    for copy in copies:
        copy.start()
    for copy in copies:
        copy.wait()
    attend_jobs(
        jobs,
        lambda job: (mine, job * rows),
        q_jobs,
        out_jobs,
        window,
        origin,
        meta,
        work,
        block,
        span,
    )
    copies = [
        pltpu.make_async_copy(out_jobs.at[job], out.at[pl.ds(job * rows, rows)], sems.at[job])
        for job in range(jobs)
    ]
    for copy in copies:
        copy.start()
    for copy in copies:
        copy.wait()


def shards_whole(meta, queries, keys, values, span):
    block, jobs = queries.shape[0], lax.axis_size("kvh")
    rows = block // jobs
    heads = []
    for which in range(keys.shape[1] // HEAD_WIDTH):
        at = slice(which * HEAD_WIDTH, (which + 1) * HEAD_WIDTH)
        item = jnp.concatenate([keys[:, at], values[:, at]], 1)
        gathered = lax.all_gather(item, "seq", axis=0, tiled=True)
        heads.append(
            pl.pallas_call(
                lambda *refs, which=which: whole_kernel(*refs, which=which, block=block, span=span),
                out_shape=jax.ShapeDtypeStruct((block, GROUP_WIDTH), jnp.bfloat16),
                grid_spec=pltpu.PrefetchScalarGridSpec(
                    num_scalar_prefetch=1,
                    grid=(),
                    in_specs=[pl.BlockSpec(memory_space=pltpu.HBM)] * 2,
                    out_specs=pl.BlockSpec(memory_space=pltpu.HBM),
                    scratch_shapes=[
                        pltpu.VMEM((span * block, 2 * HEAD_WIDTH), jnp.bfloat16),
                        pltpu.VMEM((jobs, rows, GROUP_WIDTH), jnp.bfloat16),
                        pltpu.VMEM((jobs, rows, GROUP_WIDTH), jnp.bfloat16),
                        pltpu.SemaphoreType.DMA((jobs + span,)),
                        *buffers_for(rows, span, block),
                    ],
                ),
                compiler_params=pltpu.CompilerParams(vmem_limit_bytes=VMEM_LIMIT),
            )(meta, queries, gathered)
        )
    return lax.all_to_all(
        jnp.concatenate(heads, 1), "kvh", split_axis=0, concat_axis=1, tiled=True
    )


def shards(queries, keys, values, answer_lengths):
    block = queries.shape[0]
    count, groups = lax.axis_size("seq"), lax.axis_size("kvh")
    span = min(12, count // 2)
    mine, group = lax.axis_index("seq"), lax.axis_index("kvh")
    meta = jnp.concatenate([jnp.stack([mine, group]).astype(jnp.int32), answer_lengths])
    if groups != 2 or span != 8 or count % 4 or keys.shape[1] != 4 * HEAD_WIDTH:
        return shards_whole(meta, queries, keys, values, span)
    core = lax.rem(mine, 2)
    rows = block // groups

    def theirs(value):
        width = value.shape[1] // 2
        return lax.dynamic_slice_in_dim(value, (1 - core) * width, width, 1)

    def permute(value, pairs):
        return lax.ppermute(value, "seq", pairs)

    swap = [(i, i ^ 1) for i in range(count)]
    ahead = [(i, i + 4) for i in range(count - 4)]
    rightward = [(i, i + 2) for i in range(count) if i % 4 < 2]
    leftward = [(i, i - 2) for i in range(count) if i % 4 >= 2]

    their_queries = permute(queries, swap)
    their_kv = permute(jnp.concatenate([theirs(keys), theirs(values)], 1), swap)

    def gather(own):
        near = permute(own, ahead)
        far = permute(near, ahead)
        side_own = permute(own, rightward)
        side_near = permute(near, rightward + leftward)
        side_far = permute(far, leftward)
        return [own, near, far, side_own, side_near, side_far]

    def send(value, flip_core, flip_group):
        pairs = [
            (i * groups + r, (i ^ flip_core) * groups + (r ^ flip_group))
            for i in range(count)
            for r in range(groups)
        ]
        return lax.ppermute(value, ("seq", "kvh"), pairs)

    def run(pieces, earlier, first_flip, flip_half, which, jobs, placed=()):
        return attend_pair(
            meta,
            queries,
            their_queries,
            pieces,
            placed,
            earlier,
            first_flip,
            flip_half,
            which,
            jobs,
            rows,
            span,
        )

    own_first, own_second = own_items(meta, keys, values, their_kv)
    pieces = gather(own_first)
    later = [
        lax.all_gather(
            after(own_second, pieces[2:5]),
            "seq",
            axis=0,
            tiled=True,
            axis_index_groups=[list(range(core, count, 2)) for core in (0, 1)],
        )
    ]
    far_a, across_a = run(pieces, (), 1, 1, 0, 2)
    got_far_a = send(far_a, 1, 1)
    got_across_a = send(across_a, 0, 1)
    beside_a, own_a = run(pieces, (far_a,), 1, 0, 0, 2)
    got_beside_a = send(beside_a, 1, 0)
    far_b, across_b = run(later, (beside_a, got_far_a), 1, 1, 1, 2)
    got_far_b = send(far_b, 1, 1)
    got_across_b = send(across_b, 0, 1)
    (beside_b,) = run(later, (far_b, got_across_a, got_beside_a), 1, 0, 1, 1)
    got_beside_b = send(beside_b, 1, 0)
    placed = (own_a, got_beside_a, got_across_a, got_far_a)
    (out,) = run(later, (beside_b,), 0, 0, 1, 1, placed)
    return place(meta, [got_far_b, got_across_b, got_beside_b], 1, out)


def solution(mesh):
    in_specs = (P("seq", "kvh"), P("seq", "kvh"), P("seq", "kvh"), P())
    out_specs = P(("seq", "kvh"), None)
    return jax.shard_map(shards, mesh=mesh, in_specs=in_specs, out_specs=out_specs, check_vma=False)
```

```python
import math

import jax
import jax.numpy as jnp
from jax import lax
from jax.experimental import pallas as pl
from jax.experimental.pallas import tpu as pltpu
from jax.sharding import PartitionSpec as P

QUERY_PER_KEY = 12
HEAD_WIDTH = 128
GROUP_WIDTH = QUERY_PER_KEY * HEAD_WIDTH
SCALE_LOG2 = math.log2(math.e) / math.sqrt(HEAD_WIDTH)
VMEM_LIMIT = 62 * 1024 * 1024
STACK = 4
STACKS = QUERY_PER_KEY // STACK


def lanes(start):
    return pl.ds(pl.multiple_of(start * HEAD_WIDTH, HEAD_WIDTH), HEAD_WIDTH)


def first_visible(meta, position):
    end = jnp.int32(0)
    start = jnp.int32(0)
    for answer in range(2, meta.shape[0]):
        end = end + meta[answer]
        start = jnp.where(end <= position, end, start)
    return start


def attend_rows(count, offset, q_ref, out_ref, work, block):
    rows = q_ref.shape[0]
    stacked = STACK * rows
    window, nearest, shift, probs, stack, staged, facing = work[:7]
    width = count * block
    first = window.shape[0] - width
    tokens = lax.rem(lax.broadcasted_iota(jnp.int32, (stacked, block), 0), rows) + offset
    mask = lax.broadcasted_iota(jnp.int32, (stacked, block), 1) <= tokens

    def load(number):
        for h in range(STACK):
            stack[h * rows : (h + 1) * rows, :] = q_ref[:, lanes(number * STACK + h)]

    def score(slot):
        keys = window[first + slot * block : first + (slot + 1) * block, :HEAD_WIDTH]
        return lax.dot_general(
            stack[...], keys, (((1,), (1,)), ((), ())), preferred_element_type=jnp.float32
        )

    def begin():
        nearest[...] = jnp.where(mask, score(count - 1), -1e30)
        for h in range(STACK):
            at = slice(h * rows, (h + 1) * rows)
            ones = window[first : first + HEAD_WIDTH, 2 * HEAD_WIDTH :]
            same = jnp.dot(stack[at, :] * facing[...], ones, preferred_element_type=jnp.float32)
            shift[at, :] = same * SCALE_LOG2

    def soften(found, slot):
        for piece in range(block // HEAD_WIDTH):
            at = slice(piece * HEAD_WIDTH, (piece + 1) * HEAD_WIDTH)
            weights = jnp.exp2(found[:, at] * SCALE_LOG2 - shift[...])
            start = slot * block + piece * HEAD_WIDTH
            probs[:, start : start + HEAD_WIDTH] = weights.astype(jnp.bfloat16)

    def weigh():
        ahead = score(0) if count > 1 else None
        soften(nearest, count - 1)
        for slot in range(count - 1):
            found = ahead
            if slot < count - 2:
                ahead = score(slot + 1)
            soften(found, slot)

    def blend():
        found = jnp.dot(
            probs[:, :width], window[first:, HEAD_WIDTH:], preferred_element_type=jnp.float32
        )
        total = found[:, HEAD_WIDTH:]
        guess = pl.reciprocal(total, approx=True)
        guess = guess * (2.0 - total * guess)
        staged[...] = (found[:, :HEAD_WIDTH] * guess).astype(staged.dtype)
        return total

    def release(number):
        for h in range(STACK):
            out_ref[:, lanes(number * STACK + h)] = staged[h * rows : (h + 1) * rows]

    load(0)
    begin()

    def step(number, most):
        weigh()
        load(jnp.minimum(number + 1, STACKS - 1))
        begin()
        total = blend()
        for row in range(0, stacked, 8):
            most = jnp.maximum(most, total[row : row + 8])
        release(number)
        return most

    return jnp.max(lax.fori_loop(0, STACKS, step, jnp.zeros((8, HEAD_WIDTH), jnp.float32)))


def attend_rows_wide(visible, offset, q_ref, out_ref, work, block):
    rows = q_ref.shape[0]
    window, (peak, total, blended) = work[0], work[7:10]
    last = window.shape[0] - block
    tokens = lax.broadcasted_iota(jnp.int32, (rows, block), 0) + offset
    columns = lax.broadcasted_iota(jnp.int32, (rows, block), 1)

    @pl.loop(0, QUERY_PER_KEY)
    def _(head):
        peak[...] = jnp.full(peak.shape, -1e30, jnp.float32)
        total[...] = jnp.zeros(total.shape, jnp.float32)
        blended[...] = jnp.zeros(blended.shape, jnp.float32)

        @pl.loop(0, visible)
        def _(back):
            at = pl.ds(pl.multiple_of(last - back * block, block), block)
            found = lax.dot_general(
                q_ref[:, lanes(head)],
                window[at, :HEAD_WIDTH],
                (((1,), (1,)), ((), ())),
                preferred_element_type=jnp.float32,
            )
            found = jnp.where(columns <= tokens + back * block, found * SCALE_LOG2, -1e30)
            before = peak[...]
            now = jnp.maximum(before, jnp.max(found, axis=-1, keepdims=True))
            weights = jnp.exp2(found - now[:, :1])
            shrink = jnp.exp2(before - now)
            peak[...] = now
            total[...] = total[...] * shrink + jnp.sum(weights, axis=-1, keepdims=True)
            blended[...] = blended[...] * shrink + jnp.dot(
                weights.astype(jnp.bfloat16),
                window[at, HEAD_WIDTH : 2 * HEAD_WIDTH],
                preferred_element_type=jnp.float32,
            )

        out_ref[:, lanes(head)] = (blended[...] / total[...]).astype(out_ref.dtype)


def buffers_for(rows, span, block):
    stacked = STACK * rows
    return [
        pltpu.VMEM((span * block, 3 * HEAD_WIDTH), jnp.bfloat16),
        pltpu.VMEM((stacked, block), jnp.float32),
        pltpu.VMEM((stacked, HEAD_WIDTH), jnp.float32),
        pltpu.VMEM((stacked, span * block), jnp.bfloat16),
        pltpu.VMEM((stacked, HEAD_WIDTH), jnp.bfloat16),
        pltpu.VMEM((stacked, HEAD_WIDTH), jnp.bfloat16),
        pltpu.VMEM((rows, HEAD_WIDTH), jnp.bfloat16),
        pltpu.VMEM((rows, HEAD_WIDTH), jnp.float32),
        pltpu.VMEM((rows, HEAD_WIDTH), jnp.float32),
        pltpu.VMEM((rows, HEAD_WIDTH), jnp.float32),
        pltpu.SMEM((1,), jnp.float32),
    ]


WORK = 11


def attend_jobs(jobs, position_of, q_jobs, out_jobs, arrived, origin, meta, work, block, span, done=None):
    work[0][:, 2 * HEAD_WIDTH :] = jnp.ones((span * block, HEAD_WIDTH), jnp.bfloat16)

    @pl.loop(0, jobs)
    def _(job):
        index, offset = position_of(job)
        start = lax.div(first_visible(meta, index * block), block)
        visible = index - start + 1
        last = (index - origin + 1 - span) * block
        window, facing, most = work[0], work[6], work[10]
        moved = pl.ds(pl.multiple_of(last, block), span * block)
        window[:, : 2 * HEAD_WIDTH] = arrived[moved, :]
        here = pl.ds(pl.multiple_of(last + (span - 1) * block + offset, facing.shape[0]), facing.shape[0])
        facing[...] = arrived[here, :HEAD_WIDTH]
        for count in range(1, span + 1):

            @pl.when(visible == count)
            def _():
                most[0] = attend_rows(count, offset, q_jobs.at[job], out_jobs.at[job], work, block)

        @pl.when(jnp.logical_not(most[0] < 2.0**120))
        def _():
            attend_rows_wide(visible, offset, q_jobs.at[job], out_jobs.at[job], work, block)

        if done is not None:
            done(job)


PARTS = (0, 1, 2, 3)


def place_columns(meta, source, which):
    core, group = lax.rem(meta[0], 2), meta[1]
    from_core = 1 - core if source % 2 else core
    from_group = 1 - group if source // 2 else group
    column = ((from_group * 2 + from_core) * 2 + which) * GROUP_WIDTH
    return pl.ds(pl.multiple_of(column, GROUP_WIDTH), GROUP_WIDTH)


def place_copies(meta, inputs, sources, which, out, held, sems):
    loads, stores = [], []
    for number, (source, ref) in enumerate(zip(sources, inputs)):
        at = place_columns(meta, source, which)
        loads.append(pltpu.make_async_copy(ref, held.at[number], sems.at[0, number]))
        stores.append(pltpu.make_async_copy(held.at[number], out.at[:, at], sems.at[1, number]))
    return loads, stores


def place_kernel(meta, *refs, which, count):
    out, held, sems = refs[-3:]
    loads, stores = place_copies(meta, refs[:count], PARTS[:0:-1], which, out, held, sems)
    for load in loads:
        load.start()
    for load, store in zip(loads, stores):
        load.wait()
        store.start()
    for store in stores:
        store.wait()


def place(meta, arrays, which, out):
    rows, count = arrays[0].shape[0], len(arrays)
    return pl.pallas_call(
        lambda *refs: place_kernel(*refs, which=which, count=count),
        out_shape=jax.ShapeDtypeStruct(out.shape, out.dtype),
        grid_spec=pltpu.PrefetchScalarGridSpec(
            num_scalar_prefetch=1,
            grid=(),
            in_specs=[pl.BlockSpec(memory_space=pl.ANY)] * (count + 1),
            out_specs=pl.BlockSpec(memory_space=pltpu.HBM),
            scratch_shapes=[
                pltpu.VMEM((count, rows, GROUP_WIDTH), jnp.bfloat16),
                pltpu.SemaphoreType.DMA((2, count)),
            ],
        ),
        input_output_aliases={1 + count: 0},
        compiler_params=pltpu.CompilerParams(vmem_limit_bytes=8 * 1024 * 1024),
        cost_estimate=pl.CostEstimate(flops=0, bytes_accessed=3_000_000, transcendentals=0),
    )(meta, *arrays, out)


def pair_kernel(
    meta, queries, theirs, *refs, first_flip, flip_half, which, jobs, block, span, pieces, placed
):
    window, q_jobs, out_jobs, sems, held, held_sems = refs[-6 - WORK : -WORK]
    outs = refs[-6 - WORK - jobs : -6 - WORK]
    work = refs[-WORK:]
    rows = q_jobs.shape[1]
    mine, group = meta[0], meta[1]
    core = lax.rem(mine, 2)
    right = lax.rem(lax.div(mine, 2), 2)
    origin = mine - core - (span - 1)
    half = 1 - group if flip_half else group

    def fill(source, source_row, slot, size, sem):
        return pltpu.make_async_copy(
            source.at[pl.ds(source_row, size)], window.at[pl.ds(slot * block, size)], sems.at[sem]
        )

    if pieces == 5:
        fixed = [fill(refs[4], 0, 0, block, 0)]
        for back in range(4):
            fixed.append(fill(refs[back], 0, 7 - 2 * back, 2 * block, back + 1))
        by_side = []
    else:
        own, near, far, side_own, side_near, side_far = refs[:6]
        fixed = [
            fill(far, block, 0, block, 0),
            fill(near, 0, 3, 2 * block, 1),
            fill(own, 0, 7, 2 * block, 2),
        ]
        by_side = [
            (fill(side_far, 0, 1, 2 * block, 3), fill(side_near, 0, 1, 2 * block, 3)),
            (fill(side_near, 0, 5, 2 * block, 4), fill(side_own, 0, 5, 2 * block, 4)),
        ]
    for job in range(jobs):
        flip = first_flip - job
        source = theirs if flip else queries
        at = pl.ds(pl.multiple_of((2 * core + which) * GROUP_WIDTH, GROUP_WIDTH), GROUP_WIDTH)
        fixed.append(
            pltpu.make_async_copy(
                source.at[pl.ds(pl.multiple_of(half * rows, rows), rows), at],
                q_jobs.at[job],
                sems.at[5 + job],
            )
        )
    for copy in fixed:
        copy.start()
    for on_left, on_right in by_side:
        pl.when(right == 0)(on_left.start)
        pl.when(right == 1)(on_right.start)
    for copy in fixed:
        copy.wait()
    for on_left, _ in by_side:
        on_left.wait()

    def position_of(job):
        flip = first_flip - job
        return mine - core + jnp.where(flip == 1, 1 - core, core), half * rows

    if placed:
        loads, stores = place_copies(
            meta, refs[pieces : pieces + placed], PARTS, 0, outs[0], held, held_sems
        )
        for load in loads:
            load.start()
        targets = [outs[0].at[:, place_columns(meta, 0, which)]]
    else:
        loads, stores = [], []
        targets = outs
    copies = [
        pltpu.make_async_copy(out_jobs.at[job], out, sems.at[5 + job])
        for job, out in enumerate(targets)
    ]

    def done(job):
        for number, copy in enumerate(copies):
            pl.when(job == number)(copy.start)

    attend_jobs(
        jobs, position_of, q_jobs, out_jobs, window, origin, meta, work, block, span, done
    )
    for load, store in zip(loads, stores):
        load.wait()
        store.start()
    for copy in [*stores, *copies]:
        copy.wait()


def estimate(long=False):
    flops = 8_000_000_000 if long else 400_000_000
    return pl.CostEstimate(flops=flops, bytes_accessed=400_000, transcendentals=0)


def attend_pair(
    meta, queries, theirs, pieces, placed, earlier, first_flip, flip_half, which, jobs, rows, span
):
    block = queries.shape[0]
    args = [queries, theirs, *pieces, *placed, *earlier]
    width = 8 * GROUP_WIDTH if placed else GROUP_WIDTH
    return pl.pallas_call(
        lambda *refs: pair_kernel(
            *refs,
            first_flip=first_flip,
            flip_half=flip_half,
            which=which,
            jobs=jobs,
            block=block,
            span=span,
            pieces=len(pieces),
            placed=len(placed),
        ),
        out_shape=[jax.ShapeDtypeStruct((rows, width), jnp.bfloat16)] * jobs,
        grid_spec=pltpu.PrefetchScalarGridSpec(
            num_scalar_prefetch=1,
            grid=(),
            in_specs=[pl.BlockSpec(memory_space=pltpu.HBM)] * len(args),
            out_specs=[pl.BlockSpec(memory_space=pltpu.HBM)] * jobs,
            scratch_shapes=[
                pltpu.VMEM(((span + 1) * block, 2 * HEAD_WIDTH), jnp.bfloat16),
                pltpu.VMEM((jobs, rows, GROUP_WIDTH), jnp.bfloat16),
                pltpu.VMEM((jobs, rows, GROUP_WIDTH), jnp.bfloat16),
                pltpu.SemaphoreType.DMA((5 + jobs,)),
                pltpu.VMEM((max(len(placed), 1), rows, GROUP_WIDTH), jnp.bfloat16),
                pltpu.SemaphoreType.DMA((2, max(len(placed), 1))),
                *buffers_for(rows, span, block),
            ],
        ),
        compiler_params=pltpu.CompilerParams(vmem_limit_bytes=VMEM_LIMIT),
        cost_estimate=estimate(len(placed) > 0),
    )(meta, *args)


def own_kernel(meta, keys, values, theirs, *refs):
    outs, items, sems = refs[:3], refs[3], refs[4]
    core = lax.rem(meta[0], 2)
    block = keys.shape[0]
    mine = pl.ds(pl.multiple_of(core * block, block), block)
    other = pl.ds(pl.multiple_of((1 - core) * block, block), block)
    loads = []
    for which in range(2):
        for part, source in enumerate((keys, values)):
            at = slice(part * HEAD_WIDTH, (part + 1) * HEAD_WIDTH)
            loads.append((source.at[:, lanes(2 * core + which)], items.at[which, mine, at]))
            from_them = slice((2 * part + which) * HEAD_WIDTH, (2 * part + which + 1) * HEAD_WIDTH)
            loads.append((theirs.at[:, from_them], items.at[which, other, at]))
    loads = [
        pltpu.make_async_copy(source, target, sems.at[number])
        for number, (source, target) in enumerate(loads)
    ]
    stores = [
        pltpu.make_async_copy(items.at[which], outs[which], sems.at[8 + which])
        for which in range(2)
    ]
    upper = pltpu.make_async_copy(items.at[1, pl.ds(block, block)], outs[2], sems.at[10])
    for load in loads:
        load.start()
    for which in range(2):
        for load in loads[4 * which : 4 * which + 4]:
            load.wait()
        stores[which].start()
    upper.start()
    for store in [*stores, upper]:
        store.wait()


def own_items(meta, keys, values, their_kv):
    block = keys.shape[0]
    shape = (2 * block, 2 * HEAD_WIDTH)
    return pl.pallas_call(
        own_kernel,
        out_shape=[jax.ShapeDtypeStruct((n * block, shape[1]), jnp.bfloat16) for n in (2, 2, 1)],
        grid_spec=pltpu.PrefetchScalarGridSpec(
            num_scalar_prefetch=1,
            grid=(),
            in_specs=[pl.BlockSpec(memory_space=pltpu.HBM)] * 3,
            out_specs=[pl.BlockSpec(memory_space=pltpu.HBM)] * 3,
            scratch_shapes=[pltpu.VMEM((2, *shape), jnp.bfloat16), pltpu.SemaphoreType.DMA((11,))],
        ),
        compiler_params=pltpu.CompilerParams(vmem_limit_bytes=VMEM_LIMIT),
    )(meta, keys, values, their_kv)


def after(values, earlier):
    return pl.pallas_call(
        lambda *refs: None,
        out_shape=[jax.ShapeDtypeStruct(value.shape, value.dtype) for value in values],
        in_specs=[pl.BlockSpec(memory_space=pltpu.HBM)] * (len(values) + len(earlier)),
        out_specs=[pl.BlockSpec(memory_space=pltpu.HBM)] * len(values),
        input_output_aliases={n: n for n in range(len(values))},
    )(*values, *earlier)


def whole_kernel(meta, queries, gathered, out, window, q_jobs, out_jobs, sems, *work, which, block, span):
    jobs, rows = q_jobs.shape[0], q_jobs.shape[1]
    mine = meta[0]
    origin = mine - (span - 1)
    copies = []
    for slot in range(span):
        at = pl.ds(pl.multiple_of(jnp.maximum(origin + slot, 0) * block, block), block)
        copies.append(
            pltpu.make_async_copy(
                gathered.at[at], window.at[pl.ds(slot * block, block)], sems.at[jobs + slot]
            )
        )
    at = pl.ds(which * GROUP_WIDTH, GROUP_WIDTH)
    for job in range(jobs):
        copies.append(
            pltpu.make_async_copy(
                queries.at[pl.ds(job * rows, rows), at], q_jobs.at[job], sems.at[job]
            )
        )
    for copy in copies:
        copy.start()
    for copy in copies:
        copy.wait()
    attend_jobs(
        jobs,
        lambda job: (mine, job * rows),
        q_jobs,
        out_jobs,
        window,
        origin,
        meta,
        work,
        block,
        span,
    )
    copies = [
        pltpu.make_async_copy(out_jobs.at[job], out.at[pl.ds(job * rows, rows)], sems.at[job])
        for job in range(jobs)
    ]
    for copy in copies:
        copy.start()
    for copy in copies:
        copy.wait()


def shards_whole(meta, queries, keys, values, span):
    block, jobs = queries.shape[0], lax.axis_size("kvh")
    rows = block // jobs
    heads = []
    for which in range(keys.shape[1] // HEAD_WIDTH):
        at = slice(which * HEAD_WIDTH, (which + 1) * HEAD_WIDTH)
        item = jnp.concatenate([keys[:, at], values[:, at]], 1)
        gathered = lax.all_gather(item, "seq", axis=0, tiled=True)
        heads.append(
            pl.pallas_call(
                lambda *refs, which=which: whole_kernel(*refs, which=which, block=block, span=span),
                out_shape=jax.ShapeDtypeStruct((block, GROUP_WIDTH), jnp.bfloat16),
                grid_spec=pltpu.PrefetchScalarGridSpec(
                    num_scalar_prefetch=1,
                    grid=(),
                    in_specs=[pl.BlockSpec(memory_space=pltpu.HBM)] * 2,
                    out_specs=pl.BlockSpec(memory_space=pltpu.HBM),
                    scratch_shapes=[
                        pltpu.VMEM((span * block, 2 * HEAD_WIDTH), jnp.bfloat16),
                        pltpu.VMEM((jobs, rows, GROUP_WIDTH), jnp.bfloat16),
                        pltpu.VMEM((jobs, rows, GROUP_WIDTH), jnp.bfloat16),
                        pltpu.SemaphoreType.DMA((jobs + span,)),
                        *buffers_for(rows, span, block),
                    ],
                ),
                compiler_params=pltpu.CompilerParams(vmem_limit_bytes=VMEM_LIMIT),
            )(meta, queries, gathered)
        )
    return lax.all_to_all(
        jnp.concatenate(heads, 1), "kvh", split_axis=0, concat_axis=1, tiled=True
    )


def shards(queries, keys, values, answer_lengths):
    block = queries.shape[0]
    count, groups = lax.axis_size("seq"), lax.axis_size("kvh")
    span = min(12, count // 2)
    mine, group = lax.axis_index("seq"), lax.axis_index("kvh")
    meta = jnp.concatenate([jnp.stack([mine, group]).astype(jnp.int32), answer_lengths])
    if groups != 2 or span != 8 or count % 4 or keys.shape[1] != 4 * HEAD_WIDTH:
        return shards_whole(meta, queries, keys, values, span)
    core = lax.rem(mine, 2)
    rows = block // groups

    def theirs(value):
        width = value.shape[1] // 2
        return lax.dynamic_slice_in_dim(value, (1 - core) * width, width, 1)

    def permute(value, pairs):
        return lax.ppermute(value, "seq", pairs)

    swap = [(i, i ^ 1) for i in range(count)]
    def chips_ahead(chips):
        return [(i, i + 2 * chips) for i in range(count - 2 * chips)]

    ahead = chips_ahead(2)
    rightward = [(i, i + 2) for i in range(count) if i % 4 < 2]
    leftward = [(i, i - 2) for i in range(count) if i % 4 >= 2]

    their_queries = permute(queries, swap)
    their_kv = permute(jnp.concatenate([theirs(keys), theirs(values)], 1), swap)

    def gather(own):
        near = permute(own, ahead)
        far = permute(near, ahead)
        side_own = permute(own, rightward)
        side_near = permute(near, rightward + leftward)
        side_far = permute(far, leftward)
        return [own, near, far, side_own, side_near, side_far]

    def send(value, flip_core, flip_group):
        pairs = [
            (i * groups + r, (i ^ flip_core) * groups + (r ^ flip_group))
            for i in range(count)
            for r in range(groups)
        ]
        return lax.ppermute(value, ("seq", "kvh"), pairs)

    def run(pieces, earlier, first_flip, flip_half, which, jobs, placed=()):
        return attend_pair(
            meta,
            queries,
            their_queries,
            pieces,
            placed,
            earlier,
            first_flip,
            flip_half,
            which,
            jobs,
            rows,
            span,
        )

    own_first, own_second, upper = own_items(meta, keys, values, their_kv)
    pieces = gather(own_first)
    own, upper = after((own_second, upper), pieces[2:5])
    later = [own] + [permute(own, chips_ahead(n)) for n in (1, 2, 3)] + [permute(upper, chips_ahead(4))]
    far_a, across_a = run(pieces, (), 1, 1, 0, 2)
    got_far_a = send(far_a, 1, 1)
    got_across_a = send(across_a, 0, 1)
    beside_a, own_a = run(pieces, (far_a, *later[1:5]), 1, 0, 0, 2)
    got_beside_a = send(beside_a, 1, 0)
    far_b, across_b = run(later, (beside_a, got_far_a), 1, 1, 1, 2)
    got_far_b = send(far_b, 1, 1)
    got_across_b = send(across_b, 0, 1)
    (beside_b,) = run(later, (far_b, got_across_a, got_beside_a), 1, 0, 1, 1)
    got_beside_b = send(beside_b, 1, 0)
    placed = (own_a, got_beside_a, got_across_a, got_far_a)
    (out,) = run(later, (beside_b,), 0, 0, 1, 1, placed)
    return place(meta, [got_far_b, got_across_b, got_beside_b], 1, out)


def solution(mesh):
    in_specs = (P("seq", "kvh"), P("seq", "kvh"), P("seq", "kvh"), P())
    out_specs = P(("seq", "kvh"), None)
    return jax.shard_map(shards, mesh=mesh, in_specs=in_specs, out_specs=out_specs, check_vma=False)
```

```python
import math

import jax
import jax.numpy as jnp
from jax import lax
from jax.experimental import pallas as pl
from jax.experimental.pallas import tpu as pltpu
from jax.sharding import PartitionSpec as P

QUERY_PER_KEY = 12
HEAD_WIDTH = 128
GROUP_WIDTH = QUERY_PER_KEY * HEAD_WIDTH
SCALE_LOG2 = math.log2(math.e) / math.sqrt(HEAD_WIDTH)
VMEM_LIMIT = 62 * 1024 * 1024
STACK = 4
STACKS = QUERY_PER_KEY // STACK


def lanes(start):
    return pl.ds(pl.multiple_of(start * HEAD_WIDTH, HEAD_WIDTH), HEAD_WIDTH)


def first_visible(meta, position):
    end = jnp.int32(0)
    start = jnp.int32(0)
    for answer in range(2, meta.shape[0]):
        end = end + meta[answer]
        start = jnp.where(end <= position, end, start)
    return start


def attend_rows(count, offset, q_ref, out_ref, work, block):
    rows = q_ref.shape[0]
    stacked = STACK * rows
    window, nearest, probs, stack, staged, facing = work[:6]
    width = count * block
    first = window.shape[0] - width
    tokens = lax.rem(lax.broadcasted_iota(jnp.int32, (stacked, block), 0), rows) + offset
    mask = lax.broadcasted_iota(jnp.int32, (stacked, block), 1) <= tokens

    def load(number):
        for h in range(STACK):
            stack[h * rows : (h + 1) * rows, :HEAD_WIDTH] = q_ref[:, lanes(number * STACK + h)]

    def score(slot):
        keys = window[first + slot * block : first + (slot + 1) * block, : 2 * HEAD_WIDTH]
        return lax.dot_general(
            stack[...], keys, (((1,), (1,)), ((), ())), preferred_element_type=jnp.float32
        )

    def begin():
        ones = window[first : first + HEAD_WIDTH, HEAD_WIDTH : 2 * HEAD_WIDTH]
        column = lax.broadcasted_iota(jnp.int32, (rows, HEAD_WIDTH), 1)
        for h in range(STACK):
            at = slice(h * rows, (h + 1) * rows)
            same = jnp.dot(
                stack[at, :HEAD_WIDTH] * facing[...], ones, preferred_element_type=jnp.float32
            )
            stack[at, HEAD_WIDTH:] = jnp.where(column == 0, -same, 0.0).astype(stack.dtype)
        nearest[...] = jnp.where(mask, score(count - 1), -1e30)

    def soften(found, slot):
        for piece in range(block // HEAD_WIDTH):
            at = slice(piece * HEAD_WIDTH, (piece + 1) * HEAD_WIDTH)
            weights = jnp.exp2(found[:, at] * SCALE_LOG2)
            start = slot * block + piece * HEAD_WIDTH
            probs[:, start : start + HEAD_WIDTH] = weights.astype(jnp.bfloat16)

    def weigh():
        ahead = score(0) if count > 1 else None
        soften(nearest, count - 1)
        for slot in range(count - 1):
            found = ahead
            if slot < count - 2:
                ahead = score(slot + 1)
            soften(found, slot)

    def blend():
        found = jnp.dot(
            probs[:, :width], window[first:, HEAD_WIDTH:], preferred_element_type=jnp.float32
        )
        total = found[:, :HEAD_WIDTH]
        guess = pl.reciprocal(total, approx=True)
        guess = guess * (2.0 - total * guess)
        staged[...] = (found[:, HEAD_WIDTH:] * guess).astype(staged.dtype)
        return total

    def release(number):
        for h in range(STACK):
            out_ref[:, lanes(number * STACK + h)] = staged[h * rows : (h + 1) * rows]

    load(0)
    begin()

    def step(number, most):
        weigh()
        load(jnp.minimum(number + 1, STACKS - 1))
        begin()
        total = blend()
        for row in range(0, stacked, 8):
            most = jnp.maximum(most, total[row : row + 8])
        release(number)
        return most

    return jnp.max(lax.fori_loop(0, STACKS, step, jnp.zeros((8, HEAD_WIDTH), jnp.float32)))


def attend_rows_wide(visible, offset, q_ref, out_ref, work, block):
    rows = q_ref.shape[0]
    window, (peak, total, blended) = work[0], work[6:9]
    last = window.shape[0] - block
    tokens = lax.broadcasted_iota(jnp.int32, (rows, block), 0) + offset
    columns = lax.broadcasted_iota(jnp.int32, (rows, block), 1)

    @pl.loop(0, QUERY_PER_KEY)
    def _(head):
        peak[...] = jnp.full(peak.shape, -1e30, jnp.float32)
        total[...] = jnp.zeros(total.shape, jnp.float32)
        blended[...] = jnp.zeros(blended.shape, jnp.float32)

        @pl.loop(0, visible)
        def _(back):
            at = pl.ds(pl.multiple_of(last - back * block, block), block)
            found = lax.dot_general(
                q_ref[:, lanes(head)],
                window[at, :HEAD_WIDTH],
                (((1,), (1,)), ((), ())),
                preferred_element_type=jnp.float32,
            )
            found = jnp.where(columns <= tokens + back * block, found * SCALE_LOG2, -1e30)
            before = peak[...]
            now = jnp.maximum(before, jnp.max(found, axis=-1, keepdims=True))
            weights = jnp.exp2(found - now[:, :1])
            shrink = jnp.exp2(before - now)
            peak[...] = now
            total[...] = total[...] * shrink + jnp.sum(weights, axis=-1, keepdims=True)
            blended[...] = blended[...] * shrink + jnp.dot(
                weights.astype(jnp.bfloat16),
                window[at, 2 * HEAD_WIDTH :],
                preferred_element_type=jnp.float32,
            )

        out_ref[:, lanes(head)] = (blended[...] / total[...]).astype(out_ref.dtype)


def buffers_for(rows, span, block):
    stacked = STACK * rows
    return [
        pltpu.VMEM((span * block, 3 * HEAD_WIDTH), jnp.bfloat16),
        pltpu.VMEM((stacked, block), jnp.float32),
        pltpu.VMEM((stacked, span * block), jnp.bfloat16),
        pltpu.VMEM((stacked, 2 * HEAD_WIDTH), jnp.bfloat16),
        pltpu.VMEM((stacked, HEAD_WIDTH), jnp.bfloat16),
        pltpu.VMEM((rows, HEAD_WIDTH), jnp.bfloat16),
        pltpu.VMEM((rows, HEAD_WIDTH), jnp.float32),
        pltpu.VMEM((rows, HEAD_WIDTH), jnp.float32),
        pltpu.VMEM((rows, HEAD_WIDTH), jnp.float32),
        pltpu.SMEM((1,), jnp.float32),
    ]


WORK = 10


def attend_jobs(jobs, position_of, q_jobs, out_jobs, arrived, origin, meta, work, block, span, done=None):
    work[0][:, HEAD_WIDTH : 2 * HEAD_WIDTH] = jnp.ones((span * block, HEAD_WIDTH), jnp.bfloat16)

    @pl.loop(0, jobs)
    def _(job):
        index, offset = position_of(job)
        start = lax.div(first_visible(meta, index * block), block)
        visible = index - start + 1
        last = (index - origin + 1 - span) * block
        window, facing, most = work[0], work[5], work[9]
        moved = pl.ds(pl.multiple_of(last, block), span * block)
        window[:, :HEAD_WIDTH] = arrived[moved, :HEAD_WIDTH]
        window[:, 2 * HEAD_WIDTH :] = arrived[moved, HEAD_WIDTH:]
        here = pl.ds(pl.multiple_of(last + (span - 1) * block + offset, facing.shape[0]), facing.shape[0])
        facing[...] = arrived[here, :HEAD_WIDTH]
        for count in range(1, span + 1):

            @pl.when(visible == count)
            def _():
                most[0] = attend_rows(count, offset, q_jobs.at[job], out_jobs.at[job], work, block)

        @pl.when(jnp.logical_not(most[0] < 2.0**120))
        def _():
            attend_rows_wide(visible, offset, q_jobs.at[job], out_jobs.at[job], work, block)

        if done is not None:
            done(job)


PARTS = (0, 1, 2, 3)


def place_columns(meta, source, which):
    core, group = lax.rem(meta[0], 2), meta[1]
    from_core = 1 - core if source % 2 else core
    from_group = 1 - group if source // 2 else group
    column = ((from_group * 2 + from_core) * 2 + which) * GROUP_WIDTH
    return pl.ds(pl.multiple_of(column, GROUP_WIDTH), GROUP_WIDTH)


def place_copies(meta, inputs, sources, which, out, held, sems):
    loads, stores = [], []
    for number, (source, ref) in enumerate(zip(sources, inputs)):
        at = place_columns(meta, source, which)
        loads.append(pltpu.make_async_copy(ref, held.at[number], sems.at[0, number]))
        stores.append(pltpu.make_async_copy(held.at[number], out.at[:, at], sems.at[1, number]))
    return loads, stores


def place_kernel(meta, *refs, which, sources):
    count = len(sources)
    out, held, sems = refs[-3:]
    loads, stores = place_copies(meta, refs[:count], sources, which, out, held, sems)
    for load in loads:
        load.start()
    for load, store in zip(loads, stores):
        load.wait()
        store.start()
    for store in stores:
        store.wait()


def place(meta, arrays, sources, which, out):
    rows, count = arrays[0].shape[0], len(arrays)
    return pl.pallas_call(
        lambda *refs: place_kernel(*refs, which=which, sources=sources),
        out_shape=jax.ShapeDtypeStruct(out.shape, out.dtype),
        grid_spec=pltpu.PrefetchScalarGridSpec(
            num_scalar_prefetch=1,
            grid=(),
            in_specs=[pl.BlockSpec(memory_space=pl.ANY)] * (count + 1),
            out_specs=pl.BlockSpec(memory_space=pltpu.HBM),
            scratch_shapes=[
                pltpu.VMEM((count, rows, GROUP_WIDTH), jnp.bfloat16),
                pltpu.SemaphoreType.DMA((2, count)),
            ],
        ),
        input_output_aliases={1 + count: 0},
        compiler_params=pltpu.CompilerParams(vmem_limit_bytes=8 * 1024 * 1024),
        cost_estimate=estimate(),
    )(meta, *arrays, out)


def pair_kernel(
    meta, queries, theirs, *refs, flip_half, which, jobs, block, span, pieces, placed
):
    window, q_jobs, out_jobs, sems, held, held_sems = refs[-6 - WORK : -WORK]
    outs = refs[-6 - WORK - jobs : -6 - WORK]
    work = refs[-WORK:]
    rows = q_jobs.shape[1]
    mine, group = meta[0], meta[1]
    core = lax.rem(mine, 2)
    right = lax.rem(lax.div(mine, 2), 2)
    origin = mine - core - (span - 1)

    def half_of(job):
        return 1 - group if flip_half and job < 2 else group


    def fill(source, source_row, slot, size, sem):
        return pltpu.make_async_copy(
            source.at[pl.ds(source_row, size)], window.at[pl.ds(slot * block, size)], sems.at[sem]
        )

    if pieces == 5:
        fixed = [fill(refs[4], 0, 0, block, 0)]
        for back in range(4):
            fixed.append(fill(refs[back], 0, 7 - 2 * back, 2 * block, back + 1))
        by_side = []
    else:
        own, near, far, side_own, side_near, side_far = refs[:6]
        fixed = [
            fill(far, block, 0, block, 0),
            fill(near, 0, 3, 2 * block, 1),
            fill(own, 0, 7, 2 * block, 2),
        ]
        by_side = [
            (fill(side_far, 0, 1, 2 * block, 3), fill(side_near, 0, 1, 2 * block, 3)),
            (fill(side_near, 0, 5, 2 * block, 4), fill(side_own, 0, 5, 2 * block, 4)),
        ]
    for job in range(jobs):
        source = queries if job % 2 else theirs
        at = pl.ds(pl.multiple_of((2 * core + which) * GROUP_WIDTH, GROUP_WIDTH), GROUP_WIDTH)
        fixed.append(
            pltpu.make_async_copy(
                source.at[pl.ds(pl.multiple_of(half_of(job) * rows, rows), rows), at],
                q_jobs.at[job],
                sems.at[5 + job],
            )
        )
    for copy in fixed:
        copy.start()
    for on_left, on_right in by_side:
        pl.when(right == 0)(on_left.start)
        pl.when(right == 1)(on_right.start)
    for copy in fixed:
        copy.wait()
    for on_left, _ in by_side:
        on_left.wait()

    def position_of(job):
        half = jnp.where(job < 2, half_of(0), half_of(2))
        return mine - core + jnp.where(lax.rem(job, 2) == 0, 1 - core, core), half * rows

    if placed:
        loads, stores = place_copies(
            meta, refs[pieces : pieces + placed], PARTS, 0, outs[-1], held, held_sems
        )
        for load in loads:
            load.start()
        targets = [*outs[:-1], outs[-1].at[:, place_columns(meta, 0, which)]]
    else:
        loads, stores = [], []
        targets = outs
    copies = [
        pltpu.make_async_copy(out_jobs.at[job], out, sems.at[5 + job])
        for job, out in enumerate(targets)
    ]

    def done(job):
        for number, copy in enumerate(copies):
            pl.when(job == number)(copy.start)

    attend_jobs(
        jobs, position_of, q_jobs, out_jobs, window, origin, meta, work, block, span, done
    )
    for load, store in zip(loads, stores):
        load.wait()
        store.start()
    for copy in [*stores, *copies]:
        copy.wait()


def estimate(long=True):
    flops = 8_000_000_000 if long else 400_000_000
    return pl.CostEstimate(flops=flops, bytes_accessed=400_000, transcendentals=0)


def attend_pair(
    meta, queries, theirs, pieces, placed, earlier, flip_half, which, jobs, rows, span
):
    block = queries.shape[0]
    args = [queries, theirs, *pieces, *placed, *earlier]
    widths = [GROUP_WIDTH] * (jobs - 1) + [8 * GROUP_WIDTH if placed else GROUP_WIDTH]
    return pl.pallas_call(
        lambda *refs: pair_kernel(
            *refs,
            flip_half=flip_half,
            which=which,
            jobs=jobs,
            block=block,
            span=span,
            pieces=len(pieces),
            placed=len(placed),
        ),
        out_shape=[jax.ShapeDtypeStruct((rows, width), jnp.bfloat16) for width in widths],
        grid_spec=pltpu.PrefetchScalarGridSpec(
            num_scalar_prefetch=1,
            grid=(),
            in_specs=[pl.BlockSpec(memory_space=pltpu.HBM)] * len(args),
            out_specs=[pl.BlockSpec(memory_space=pltpu.HBM)] * jobs,
            scratch_shapes=[
                pltpu.VMEM(((span + 1) * block, 2 * HEAD_WIDTH), jnp.bfloat16),
                pltpu.VMEM((jobs, rows, GROUP_WIDTH), jnp.bfloat16),
                pltpu.VMEM((jobs, rows, GROUP_WIDTH), jnp.bfloat16),
                pltpu.SemaphoreType.DMA((5 + jobs,)),
                pltpu.VMEM((max(len(placed), 1), rows, GROUP_WIDTH), jnp.bfloat16),
                pltpu.SemaphoreType.DMA((2, max(len(placed), 1))),
                *buffers_for(rows, span, block),
            ],
        ),
        compiler_params=pltpu.CompilerParams(vmem_limit_bytes=VMEM_LIMIT),
        cost_estimate=estimate(len(earlier) > 0),
    )(meta, *args)


def own_kernel(meta, keys, values, theirs, *refs):
    outs, items, sems = refs[:3], refs[3], refs[4]
    core = lax.rem(meta[0], 2)
    block = keys.shape[0]
    mine = pl.ds(pl.multiple_of(core * block, block), block)
    other = pl.ds(pl.multiple_of((1 - core) * block, block), block)
    loads = []
    for which in range(2):
        for part, source in enumerate((keys, values)):
            at = slice(part * HEAD_WIDTH, (part + 1) * HEAD_WIDTH)
            loads.append((source.at[:, lanes(2 * core + which)], items.at[which, mine, at]))
            from_them = slice((2 * part + which) * HEAD_WIDTH, (2 * part + which + 1) * HEAD_WIDTH)
            loads.append((theirs.at[:, from_them], items.at[which, other, at]))
    loads = [
        pltpu.make_async_copy(source, target, sems.at[number])
        for number, (source, target) in enumerate(loads)
    ]
    stores = [
        pltpu.make_async_copy(items.at[which], outs[which], sems.at[8 + which])
        for which in range(2)
    ]
    more = [
        pltpu.make_async_copy(items.at[1, pl.ds(block, block)], outs[2], sems.at[10]),
    ]
    for load in loads:
        load.start()
    for which in range(2):
        for load in loads[4 * which : 4 * which + 4]:
            load.wait()
        stores[which].start()
    for store in more:
        store.start()
    for store in [*stores, *more]:
        store.wait()


def own_items(meta, keys, values, their_kv):
    block = keys.shape[0]
    shape = (2 * block, 2 * HEAD_WIDTH)
    return pl.pallas_call(
        own_kernel,
        out_shape=[jax.ShapeDtypeStruct((n * block, shape[1]), jnp.bfloat16) for n in (2, 2, 1)],
        grid_spec=pltpu.PrefetchScalarGridSpec(
            num_scalar_prefetch=1,
            grid=(),
            in_specs=[pl.BlockSpec(memory_space=pltpu.HBM)] * 3,
            out_specs=[pl.BlockSpec(memory_space=pltpu.HBM)] * 3,
            scratch_shapes=[pltpu.VMEM((2, *shape), jnp.bfloat16), pltpu.SemaphoreType.DMA((11,))],
        ),
        compiler_params=pltpu.CompilerParams(vmem_limit_bytes=VMEM_LIMIT),
    )(meta, keys, values, their_kv)


def after(values, earlier):
    return pl.pallas_call(
        lambda *refs: None,
        out_shape=[jax.ShapeDtypeStruct(value.shape, value.dtype) for value in values],
        in_specs=[pl.BlockSpec(memory_space=pltpu.HBM)] * (len(values) + len(earlier)),
        out_specs=[pl.BlockSpec(memory_space=pltpu.HBM)] * len(values),
        input_output_aliases={n: n for n in range(len(values))},
    )(*values, *earlier)


def whole_kernel(meta, queries, gathered, out, window, q_jobs, out_jobs, sems, *work, which, block, span):
    jobs, rows = q_jobs.shape[0], q_jobs.shape[1]
    mine = meta[0]
    origin = mine - (span - 1)
    copies = []
    for slot in range(span):
        at = pl.ds(pl.multiple_of(jnp.maximum(origin + slot, 0) * block, block), block)
        copies.append(
            pltpu.make_async_copy(
                gathered.at[at], window.at[pl.ds(slot * block, block)], sems.at[jobs + slot]
            )
        )
    at = pl.ds(which * GROUP_WIDTH, GROUP_WIDTH)
    for job in range(jobs):
        copies.append(
            pltpu.make_async_copy(
                queries.at[pl.ds(job * rows, rows), at], q_jobs.at[job], sems.at[job]
            )
        )
    for copy in copies:
        copy.start()
    for copy in copies:
        copy.wait()
    attend_jobs(
        jobs,
        lambda job: (mine, job * rows),
        q_jobs,
        out_jobs,
        window,
        origin,
        meta,
        work,
        block,
        span,
    )
    copies = [
        pltpu.make_async_copy(out_jobs.at[job], out.at[pl.ds(job * rows, rows)], sems.at[job])
        for job in range(jobs)
    ]
    for copy in copies:
        copy.start()
    for copy in copies:
        copy.wait()


def shards_whole(meta, queries, keys, values, span):
    block, jobs = queries.shape[0], lax.axis_size("kvh")
    rows = block // jobs
    heads = []
    for which in range(keys.shape[1] // HEAD_WIDTH):
        at = slice(which * HEAD_WIDTH, (which + 1) * HEAD_WIDTH)
        item = jnp.concatenate([keys[:, at], values[:, at]], 1)
        gathered = lax.all_gather(item, "seq", axis=0, tiled=True)
        heads.append(
            pl.pallas_call(
                lambda *refs, which=which: whole_kernel(*refs, which=which, block=block, span=span),
                out_shape=jax.ShapeDtypeStruct((block, GROUP_WIDTH), jnp.bfloat16),
                grid_spec=pltpu.PrefetchScalarGridSpec(
                    num_scalar_prefetch=1,
                    grid=(),
                    in_specs=[pl.BlockSpec(memory_space=pltpu.HBM)] * 2,
                    out_specs=pl.BlockSpec(memory_space=pltpu.HBM),
                    scratch_shapes=[
                        pltpu.VMEM((span * block, 2 * HEAD_WIDTH), jnp.bfloat16),
                        pltpu.VMEM((jobs, rows, GROUP_WIDTH), jnp.bfloat16),
                        pltpu.VMEM((jobs, rows, GROUP_WIDTH), jnp.bfloat16),
                        pltpu.SemaphoreType.DMA((jobs + span,)),
                        *buffers_for(rows, span, block),
                    ],
                ),
                compiler_params=pltpu.CompilerParams(vmem_limit_bytes=VMEM_LIMIT),
            )(meta, queries, gathered)
        )
    return lax.all_to_all(
        jnp.concatenate(heads, 1), "kvh", split_axis=0, concat_axis=1, tiled=True
    )


def shards(queries, keys, values, answer_lengths):
    block = queries.shape[0]
    count, groups = lax.axis_size("seq"), lax.axis_size("kvh")
    span = min(12, count // 2)
    mine, group = lax.axis_index("seq"), lax.axis_index("kvh")
    meta = jnp.concatenate([jnp.stack([mine, group]).astype(jnp.int32), answer_lengths])
    if groups != 2 or span != 8 or count % 4 or keys.shape[1] != 4 * HEAD_WIDTH:
        return shards_whole(meta, queries, keys, values, span)
    core = lax.rem(mine, 2)
    rows = block // groups

    def theirs(value):
        width = value.shape[1] // 2
        return lax.dynamic_slice_in_dim(value, (1 - core) * width, width, 1)

    def permute(value, pairs):
        return lax.ppermute(value, "seq", pairs)

    swap = [(i, i ^ 1) for i in range(count)]
    def chips_ahead(chips):
        return [(i, i + 2 * chips) for i in range(count - 2 * chips)]

    ahead = chips_ahead(2)
    rightward = [(i, i + 2) for i in range(count) if i % 4 < 2]
    leftward = [(i, i - 2) for i in range(count) if i % 4 >= 2]

    their_queries = permute(queries, swap)
    their_kv = permute(jnp.concatenate([theirs(keys), theirs(values)], 1), swap)

    def gather(own):
        near = permute(own, ahead)
        far = permute(near, ahead)
        side_own = permute(own, rightward)
        side_near = permute(near, rightward + leftward)
        side_far = permute(far, leftward)
        return [own, near, far, side_own, side_near, side_far]

    def send(value, flip_core, flip_group):
        pairs = [
            (i * groups + r, (i ^ flip_core) * groups + (r ^ flip_group))
            for i in range(count)
            for r in range(groups)
        ]
        return lax.ppermute(value, ("seq", "kvh"), pairs)

    def run(pieces, earlier, flip_half, which, jobs, placed=()):
        return attend_pair(
            meta,
            queries,
            their_queries,
            pieces,
            placed,
            earlier,
            flip_half,
            which,
            jobs,
            rows,
            span,
        )

    own_first, own_second, upper = own_items(meta, keys, values, their_kv)
    pieces = gather(own_first)
    own, upper = after((own_second, upper), pieces[2:5])
    later = [own] + [permute(own, chips_ahead(n)) for n in (1, 2, 3)] + [permute(upper, chips_ahead(4))]
    far_a, across_a, beside_a, own_a = run(pieces, (), 1, 0, 4)
    got_far_a = send(far_a, 1, 1)
    got_across_a = send(across_a, 0, 1)
    got_beside_a = send(beside_a, 1, 0)
    far_b, across_b = run(later, (beside_a,), 1, 1, 2)
    got_far_b = send(far_b, 1, 1)
    got_across_b = send(across_b, 0, 1)
    placed = (own_a, got_beside_a, got_across_a, got_far_a)
    beside_b, out = run(later, (far_b,), 0, 1, 2, placed)
    got_beside_b = send(beside_b, 1, 0)
    out = place(meta, [got_far_b, got_across_b], (3, 2), 1, out)
    return place(meta, [got_beside_b], (1,), 1, out)


def solution(mesh):
    in_specs = (P("seq", "kvh"), P("seq", "kvh"), P("seq", "kvh"), P())
    out_specs = P(("seq", "kvh"), None)
    return jax.shard_map(shards, mesh=mesh, in_specs=in_specs, out_specs=out_specs, check_vma=False)
```

```python
import math

import jax
import jax.numpy as jnp
from jax import lax
from jax.experimental import pallas as pl
from jax.experimental.pallas import tpu as pltpu
from jax.sharding import PartitionSpec as P

QUERY_PER_KEY = 12
HEAD_WIDTH = 128
GROUP_WIDTH = QUERY_PER_KEY * HEAD_WIDTH
SCALE_LOG2 = math.log2(math.e) / math.sqrt(HEAD_WIDTH)
VMEM_LIMIT = 62 * 1024 * 1024
STACK = 4
STACKS = QUERY_PER_KEY // STACK


def lanes(start):
    return pl.ds(pl.multiple_of(start * HEAD_WIDTH, HEAD_WIDTH), HEAD_WIDTH)


def first_visible(meta, position):
    end = jnp.int32(0)
    start = jnp.int32(0)
    for answer in range(2, meta.shape[0]):
        end = end + meta[answer]
        start = jnp.where(end <= position, end, start)
    return start


def attend_rows(count, offset, q_ref, out_ref, work, block):
    rows = q_ref.shape[0]
    stacked = STACK * rows
    window, nearest, shift, probs, stack, staged, facing = work[:7]
    width = count * block
    first = window.shape[0] - width
    tokens = lax.rem(lax.broadcasted_iota(jnp.int32, (stacked, block), 0), rows) + offset
    mask = lax.broadcasted_iota(jnp.int32, (stacked, block), 1) <= tokens

    def load(number):
        for h in range(STACK):
            stack[h * rows : (h + 1) * rows, :] = q_ref[:, lanes(number * STACK + h)]

    def score(slot):
        keys = window[first + slot * block : first + (slot + 1) * block, :HEAD_WIDTH]
        return lax.dot_general(
            stack[...], keys, (((1,), (1,)), ((), ())), preferred_element_type=jnp.float32
        )

    def begin():
        nearest[...] = jnp.where(mask, score(count - 1), -1e30)
        for h in range(STACK):
            at = slice(h * rows, (h + 1) * rows)
            ones = window[first : first + HEAD_WIDTH, 2 * HEAD_WIDTH :]
            same = jnp.dot(stack[at, :] * facing[...], ones, preferred_element_type=jnp.float32)
            shift[at, :] = same * SCALE_LOG2

    def soften(found, slot):
        for piece in range(block // HEAD_WIDTH):
            at = slice(piece * HEAD_WIDTH, (piece + 1) * HEAD_WIDTH)
            weights = jnp.exp2(found[:, at] * SCALE_LOG2 - shift[...])
            start = slot * block + piece * HEAD_WIDTH
            probs[:, start : start + HEAD_WIDTH] = weights.astype(jnp.bfloat16)

    def weigh():
        ahead = score(0) if count > 1 else None
        soften(nearest, count - 1)
        for slot in range(count - 1):
            found = ahead
            if slot < count - 2:
                ahead = score(slot + 1)
            soften(found, slot)

    def blend():
        found = jnp.dot(
            probs[:, :width], window[first:, HEAD_WIDTH:], preferred_element_type=jnp.float32
        )
        total = found[:, HEAD_WIDTH:]
        guess = pl.reciprocal(total, approx=True)
        guess = guess * (2.0 - total * guess)
        staged[...] = (found[:, :HEAD_WIDTH] * guess).astype(staged.dtype)
        return total

    def release(number):
        for h in range(STACK):
            out_ref[:, lanes(number * STACK + h)] = staged[h * rows : (h + 1) * rows]

    load(0)
    begin()

    def step(number, most):
        weigh()
        load(jnp.minimum(number + 1, STACKS - 1))
        begin()
        total = blend()
        for row in range(0, stacked, 8):
            most = jnp.maximum(most, total[row : row + 8])
        release(number)
        return most

    return jnp.max(lax.fori_loop(0, STACKS, step, jnp.zeros((8, HEAD_WIDTH), jnp.float32)))


def attend_rows_wide(visible, offset, q_ref, out_ref, work, block):
    rows = q_ref.shape[0]
    window, (peak, total, blended) = work[0], work[7:10]
    last = window.shape[0] - block
    tokens = lax.broadcasted_iota(jnp.int32, (rows, block), 0) + offset
    columns = lax.broadcasted_iota(jnp.int32, (rows, block), 1)

    @pl.loop(0, QUERY_PER_KEY)
    def _(head):
        peak[...] = jnp.full(peak.shape, -1e30, jnp.float32)
        total[...] = jnp.zeros(total.shape, jnp.float32)
        blended[...] = jnp.zeros(blended.shape, jnp.float32)

        @pl.loop(0, visible)
        def _(back):
            at = pl.ds(pl.multiple_of(last - back * block, block), block)
            found = lax.dot_general(
                q_ref[:, lanes(head)],
                window[at, :HEAD_WIDTH],
                (((1,), (1,)), ((), ())),
                preferred_element_type=jnp.float32,
            )
            found = jnp.where(columns <= tokens + back * block, found * SCALE_LOG2, -1e30)
            before = peak[...]
            now = jnp.maximum(before, jnp.max(found, axis=-1, keepdims=True))
            weights = jnp.exp2(found - now[:, :1])
            shrink = jnp.exp2(before - now)
            peak[...] = now
            total[...] = total[...] * shrink + jnp.sum(weights, axis=-1, keepdims=True)
            blended[...] = blended[...] * shrink + jnp.dot(
                weights.astype(jnp.bfloat16),
                window[at, HEAD_WIDTH : 2 * HEAD_WIDTH],
                preferred_element_type=jnp.float32,
            )

        out_ref[:, lanes(head)] = (blended[...] / total[...]).astype(out_ref.dtype)


def buffers_for(rows, span, block):
    stacked = STACK * rows
    return [
        pltpu.VMEM((span * block, 3 * HEAD_WIDTH), jnp.bfloat16),
        pltpu.VMEM((stacked, block), jnp.float32),
        pltpu.VMEM((stacked, HEAD_WIDTH), jnp.float32),
        pltpu.VMEM((stacked, span * block), jnp.bfloat16),
        pltpu.VMEM((stacked, HEAD_WIDTH), jnp.bfloat16),
        pltpu.VMEM((stacked, HEAD_WIDTH), jnp.bfloat16),
        pltpu.VMEM((rows, HEAD_WIDTH), jnp.bfloat16),
        pltpu.VMEM((rows, HEAD_WIDTH), jnp.float32),
        pltpu.VMEM((rows, HEAD_WIDTH), jnp.float32),
        pltpu.VMEM((rows, HEAD_WIDTH), jnp.float32),
        pltpu.SMEM((1,), jnp.float32),
    ]


WORK = 11


def attend_jobs(jobs, position_of, q_jobs, out_jobs, arrived, origin, meta, work, block, span, ready=None, done=None):
    work[0][:, 2 * HEAD_WIDTH :] = jnp.ones((span * block, HEAD_WIDTH), jnp.bfloat16)

    @pl.loop(0, jobs)
    def _(job):
        if ready is not None:
            ready(job)
        index, offset = position_of(job)
        start = lax.div(first_visible(meta, index * block), block)
        visible = index - start + 1
        last = (index - origin + 1 - span) * block
        window, facing, most = work[0], work[6], work[10]
        moved = pl.ds(pl.multiple_of(last, block), span * block)
        window[:, : 2 * HEAD_WIDTH] = arrived[moved, :]
        here = pl.ds(pl.multiple_of(last + (span - 1) * block + offset, facing.shape[0]), facing.shape[0])
        facing[...] = arrived[here, :HEAD_WIDTH]
        for count in range(1, span + 1):

            @pl.when(visible == count)
            def _():
                most[0] = attend_rows(count, offset, q_jobs.at[job], out_jobs.at[job], work, block)

        @pl.when(jnp.logical_not(most[0] < 2.0**120))
        def _():
            attend_rows_wide(visible, offset, q_jobs.at[job], out_jobs.at[job], work, block)

        if done is not None:
            done(job)


PARTS = (0, 1, 2, 3)


def place_columns(meta, source, which):
    core, group = lax.rem(meta[0], 2), meta[1]
    from_core = 1 - core if source % 2 else core
    from_group = 1 - group if source // 2 else group
    column = ((from_group * 2 + from_core) * 2 + which) * GROUP_WIDTH
    return pl.ds(pl.multiple_of(column, GROUP_WIDTH), GROUP_WIDTH)


def place_copies(meta, inputs, sources, which, out, held, sems):
    loads, stores = [], []
    for number, (source, ref) in enumerate(zip(sources, inputs)):
        at = place_columns(meta, source, which)
        loads.append(pltpu.make_async_copy(ref, held.at[number], sems.at[0, number]))
        stores.append(pltpu.make_async_copy(held.at[number], out.at[:, at], sems.at[1, number]))
    return loads, stores


def place_kernel(meta, *refs, which, sources):
    count = len(sources)
    out, held, sems = refs[-3:]
    loads, stores = place_copies(meta, refs[:count], sources, which, out, held, sems)
    for load in loads:
        load.start()
    for load, store in zip(loads, stores):
        load.wait()
        store.start()
    for store in stores:
        store.wait()


def place(meta, arrays, sources, which, out):
    rows, count = arrays[0].shape[0], len(arrays)
    return pl.pallas_call(
        lambda *refs: place_kernel(*refs, which=which, sources=sources),
        out_shape=jax.ShapeDtypeStruct(out.shape, out.dtype),
        grid_spec=pltpu.PrefetchScalarGridSpec(
            num_scalar_prefetch=1,
            grid=(),
            in_specs=[pl.BlockSpec(memory_space=pl.ANY)] * (count + 1),
            out_specs=pl.BlockSpec(memory_space=pltpu.HBM),
            scratch_shapes=[
                pltpu.VMEM((count, rows, GROUP_WIDTH), jnp.bfloat16),
                pltpu.SemaphoreType.DMA((2, count)),
            ],
        ),
        input_output_aliases={1 + count: 0},
        compiler_params=pltpu.CompilerParams(vmem_limit_bytes=8 * 1024 * 1024),
        cost_estimate=estimate(),
    )(meta, *arrays, out)


def pair_kernel(
    meta, queries, theirs, *refs, flip_half, which, jobs, block, span, pieces, placed
):
    window, q_jobs, out_jobs, sems, held, held_sems = refs[-6 - WORK : -WORK]
    outs = refs[-6 - WORK - jobs : -6 - WORK]
    work = refs[-WORK:]
    rows = q_jobs.shape[1]
    mine, group = meta[0], meta[1]
    core = lax.rem(mine, 2)
    right = lax.rem(lax.div(mine, 2), 2)
    origin = mine - core - (span - 1)

    def half_of(job):
        return 1 - group if flip_half and job < 2 else group


    def fill(source, source_row, slot, size, sem):
        return pltpu.make_async_copy(
            source.at[pl.ds(source_row, size)], window.at[pl.ds(slot * block, size)], sems.at[sem]
        )

    if pieces == 5:
        fixed = [fill(refs[4], 0, 0, block, 0)]
        for back in range(4):
            fixed.append(fill(refs[back], 0, 7 - 2 * back, 2 * block, back + 1))
        by_side = []
    else:
        own, near, far, side_own, side_near, side_far = refs[:6]
        fixed = [
            fill(far, block, 0, block, 0),
            fill(near, 0, 3, 2 * block, 1),
            fill(own, 0, 7, 2 * block, 2),
        ]
        by_side = [
            (fill(side_far, 0, 1, 2 * block, 3), fill(side_near, 0, 1, 2 * block, 3)),
            (fill(side_near, 0, 5, 2 * block, 4), fill(side_own, 0, 5, 2 * block, 4)),
        ]
    queries_in = []
    for job in range(jobs):
        source = queries if job % 2 else theirs
        at = pl.ds(pl.multiple_of((2 * core + which) * GROUP_WIDTH, GROUP_WIDTH), GROUP_WIDTH)
        queries_in.append(
            pltpu.make_async_copy(
                source.at[pl.ds(pl.multiple_of(half_of(job) * rows, rows), rows), at],
                q_jobs.at[job],
                sems.at[5 + job],
            )
        )
    for copy in fixed:
        copy.start()
    for on_left, on_right in by_side:
        pl.when(right == 0)(on_left.start)
        pl.when(right == 1)(on_right.start)
    for copy in queries_in:
        copy.start()
    for copy in fixed:
        copy.wait()
    for on_left, _ in by_side:
        on_left.wait()

    def position_of(job):
        half = jnp.where(job < 2, half_of(0), half_of(2))
        return mine - core + jnp.where(lax.rem(job, 2) == 0, 1 - core, core), half * rows

    if placed:
        loads, stores = place_copies(
            meta, refs[pieces : pieces + placed], PARTS, 0, outs[-1], held, held_sems
        )
        for load in loads:
            load.start()
        targets = [*outs[:-1], outs[-1].at[:, place_columns(meta, 0, which)]]
    else:
        loads, stores = [], []
        targets = outs
    copies = [
        pltpu.make_async_copy(out_jobs.at[job], out, sems.at[5 + job])
        for job, out in enumerate(targets)
    ]

    def ready(job):
        for number, copy in enumerate(queries_in):
            pl.when(job == number)(copy.wait)

    def done(job):
        for number, copy in enumerate(copies):
            pl.when(job == number)(copy.start)

    attend_jobs(
        jobs, position_of, q_jobs, out_jobs, window, origin, meta, work, block, span, ready, done
    )
    for load, store in zip(loads, stores):
        load.wait()
        store.start()
    for copy in [*stores, *copies]:
        copy.wait()


def estimate(long=True):
    flops = 8_000_000_000 if long else 400_000_000
    return pl.CostEstimate(flops=flops, bytes_accessed=400_000, transcendentals=0)


def attend_pair(
    meta, queries, theirs, pieces, placed, earlier, flip_half, which, jobs, rows, span
):
    block = queries.shape[0]
    args = [queries, theirs, *pieces, *placed, *earlier]
    widths = [GROUP_WIDTH] * (jobs - 1) + [8 * GROUP_WIDTH if placed else GROUP_WIDTH]
    return pl.pallas_call(
        lambda *refs: pair_kernel(
            *refs,
            flip_half=flip_half,
            which=which,
            jobs=jobs,
            block=block,
            span=span,
            pieces=len(pieces),
            placed=len(placed),
        ),
        out_shape=[jax.ShapeDtypeStruct((rows, width), jnp.bfloat16) for width in widths],
        grid_spec=pltpu.PrefetchScalarGridSpec(
            num_scalar_prefetch=1,
            grid=(),
            in_specs=[pl.BlockSpec(memory_space=pltpu.HBM)] * len(args),
            out_specs=[pl.BlockSpec(memory_space=pltpu.HBM)] * jobs,
            scratch_shapes=[
                pltpu.VMEM(((span + 1) * block, 2 * HEAD_WIDTH), jnp.bfloat16),
                pltpu.VMEM((jobs, rows, GROUP_WIDTH), jnp.bfloat16),
                pltpu.VMEM((jobs, rows, GROUP_WIDTH), jnp.bfloat16),
                pltpu.SemaphoreType.DMA((5 + jobs,)),
                pltpu.VMEM((max(len(placed), 1), rows, GROUP_WIDTH), jnp.bfloat16),
                pltpu.SemaphoreType.DMA((2, max(len(placed), 1))),
                *buffers_for(rows, span, block),
            ],
        ),
        compiler_params=pltpu.CompilerParams(vmem_limit_bytes=VMEM_LIMIT),
        cost_estimate=estimate(len(earlier) > 0),
    )(meta, *args)


def own_kernel(meta, keys, values, theirs, *refs):
    outs, items, sems = refs[:3], refs[3], refs[4]
    core = lax.rem(meta[0], 2)
    block = keys.shape[0]
    mine = pl.ds(pl.multiple_of(core * block, block), block)
    other = pl.ds(pl.multiple_of((1 - core) * block, block), block)
    loads = []
    for which in range(2):
        for part, source in enumerate((keys, values)):
            at = slice(part * HEAD_WIDTH, (part + 1) * HEAD_WIDTH)
            loads.append((source.at[:, lanes(2 * core + which)], items.at[which, mine, at]))
            from_them = slice((2 * part + which) * HEAD_WIDTH, (2 * part + which + 1) * HEAD_WIDTH)
            loads.append((theirs.at[:, from_them], items.at[which, other, at]))
    loads = [
        pltpu.make_async_copy(source, target, sems.at[number])
        for number, (source, target) in enumerate(loads)
    ]
    stores = [
        pltpu.make_async_copy(items.at[which], outs[which], sems.at[8 + which])
        for which in range(2)
    ]
    more = [
        pltpu.make_async_copy(items.at[1, pl.ds(block, block)], outs[2], sems.at[10]),
    ]
    for load in loads:
        load.start()
    for which in range(2):
        for load in loads[4 * which : 4 * which + 4]:
            load.wait()
        stores[which].start()
    for store in more:
        store.start()
    for store in [*stores, *more]:
        store.wait()


def own_items(meta, keys, values, their_kv):
    block = keys.shape[0]
    shape = (2 * block, 2 * HEAD_WIDTH)
    return pl.pallas_call(
        own_kernel,
        out_shape=[jax.ShapeDtypeStruct((n * block, shape[1]), jnp.bfloat16) for n in (2, 2, 1)],
        grid_spec=pltpu.PrefetchScalarGridSpec(
            num_scalar_prefetch=1,
            grid=(),
            in_specs=[pl.BlockSpec(memory_space=pltpu.HBM)] * 3,
            out_specs=[pl.BlockSpec(memory_space=pltpu.HBM)] * 3,
            scratch_shapes=[pltpu.VMEM((2, *shape), jnp.bfloat16), pltpu.SemaphoreType.DMA((11,))],
        ),
        compiler_params=pltpu.CompilerParams(vmem_limit_bytes=VMEM_LIMIT),
    )(meta, keys, values, their_kv)


def after(values, earlier):
    return pl.pallas_call(
        lambda *refs: None,
        out_shape=[jax.ShapeDtypeStruct(value.shape, value.dtype) for value in values],
        in_specs=[pl.BlockSpec(memory_space=pltpu.HBM)] * (len(values) + len(earlier)),
        out_specs=[pl.BlockSpec(memory_space=pltpu.HBM)] * len(values),
        input_output_aliases={n: n for n in range(len(values))},
    )(*values, *earlier)


def whole_kernel(meta, queries, gathered, out, window, q_jobs, out_jobs, sems, *work, which, block, span):
    jobs, rows = q_jobs.shape[0], q_jobs.shape[1]
    mine = meta[0]
    origin = mine - (span - 1)
    copies = []
    for slot in range(span):
        at = pl.ds(pl.multiple_of(jnp.maximum(origin + slot, 0) * block, block), block)
        copies.append(
            pltpu.make_async_copy(
                gathered.at[at], window.at[pl.ds(slot * block, block)], sems.at[jobs + slot]
            )
        )
    at = pl.ds(which * GROUP_WIDTH, GROUP_WIDTH)
    for job in range(jobs):
        copies.append(
            pltpu.make_async_copy(
                queries.at[pl.ds(job * rows, rows), at], q_jobs.at[job], sems.at[job]
            )
        )
    for copy in copies:
        copy.start()
    for copy in copies:
        copy.wait()
    attend_jobs(
        jobs,
        lambda job: (mine, job * rows),
        q_jobs,
        out_jobs,
        window,
        origin,
        meta,
        work,
        block,
        span,
    )
    copies = [
        pltpu.make_async_copy(out_jobs.at[job], out.at[pl.ds(job * rows, rows)], sems.at[job])
        for job in range(jobs)
    ]
    for copy in copies:
        copy.start()
    for copy in copies:
        copy.wait()


def shards_whole(meta, queries, keys, values, span):
    block, jobs = queries.shape[0], lax.axis_size("kvh")
    rows = block // jobs
    heads = []
    for which in range(keys.shape[1] // HEAD_WIDTH):
        at = slice(which * HEAD_WIDTH, (which + 1) * HEAD_WIDTH)
        item = jnp.concatenate([keys[:, at], values[:, at]], 1)
        gathered = lax.all_gather(item, "seq", axis=0, tiled=True)
        heads.append(
            pl.pallas_call(
                lambda *refs, which=which: whole_kernel(*refs, which=which, block=block, span=span),
                out_shape=jax.ShapeDtypeStruct((block, GROUP_WIDTH), jnp.bfloat16),
                grid_spec=pltpu.PrefetchScalarGridSpec(
                    num_scalar_prefetch=1,
                    grid=(),
                    in_specs=[pl.BlockSpec(memory_space=pltpu.HBM)] * 2,
                    out_specs=pl.BlockSpec(memory_space=pltpu.HBM),
                    scratch_shapes=[
                        pltpu.VMEM((span * block, 2 * HEAD_WIDTH), jnp.bfloat16),
                        pltpu.VMEM((jobs, rows, GROUP_WIDTH), jnp.bfloat16),
                        pltpu.VMEM((jobs, rows, GROUP_WIDTH), jnp.bfloat16),
                        pltpu.SemaphoreType.DMA((jobs + span,)),
                        *buffers_for(rows, span, block),
                    ],
                ),
                compiler_params=pltpu.CompilerParams(vmem_limit_bytes=VMEM_LIMIT),
            )(meta, queries, gathered)
        )
    return lax.all_to_all(
        jnp.concatenate(heads, 1), "kvh", split_axis=0, concat_axis=1, tiled=True
    )


def shards(queries, keys, values, answer_lengths):
    block = queries.shape[0]
    count, groups = lax.axis_size("seq"), lax.axis_size("kvh")
    span = min(12, count // 2)
    mine, group = lax.axis_index("seq"), lax.axis_index("kvh")
    meta = jnp.concatenate([jnp.stack([mine, group]).astype(jnp.int32), answer_lengths])
    if groups != 2 or span != 8 or count % 4 or keys.shape[1] != 4 * HEAD_WIDTH:
        return shards_whole(meta, queries, keys, values, span)
    core = lax.rem(mine, 2)
    rows = block // groups

    def theirs(value):
        width = value.shape[1] // 2
        return lax.dynamic_slice_in_dim(value, (1 - core) * width, width, 1)

    def permute(value, pairs):
        return lax.ppermute(value, "seq", pairs)

    swap = [(i, i ^ 1) for i in range(count)]
    def chips_ahead(chips):
        return [(i, i + 2 * chips) for i in range(count - 2 * chips)]

    ahead = chips_ahead(2)
    rightward = [(i, i + 2) for i in range(count) if i % 4 < 2]
    leftward = [(i, i - 2) for i in range(count) if i % 4 >= 2]

    their_queries = permute(queries, swap)
    their_kv = permute(jnp.concatenate([theirs(keys), theirs(values)], 1), swap)

    def gather(own):
        near = permute(own, ahead)
        far = permute(near, ahead)
        side_own = permute(own, rightward)
        side_near = permute(near, rightward + leftward)
        side_far = permute(far, leftward)
        return [own, near, far, side_own, side_near, side_far]

    def send(value, flip_core, flip_group):
        pairs = [
            (i * groups + r, (i ^ flip_core) * groups + (r ^ flip_group))
            for i in range(count)
            for r in range(groups)
        ]
        return lax.ppermute(value, ("seq", "kvh"), pairs)

    def run(pieces, earlier, flip_half, which, jobs, placed=()):
        return attend_pair(
            meta,
            queries,
            their_queries,
            pieces,
            placed,
            earlier,
            flip_half,
            which,
            jobs,
            rows,
            span,
        )

    own_first, own_second, upper = own_items(meta, keys, values, their_kv)
    pieces = gather(own_first)
    own, upper = after((own_second, upper), pieces[2:4])
    later = [own] + [permute(own, chips_ahead(n)) for n in (1, 2, 3)] + [permute(upper, chips_ahead(4))]
    far_a, across_a, beside_a, own_a = run(pieces, (), 1, 0, 4)
    got_far_a = send(far_a, 1, 1)
    got_across_a = send(across_a, 0, 1)
    got_beside_a = send(beside_a, 1, 0)
    far_b, across_b = run(later, (beside_a,), 1, 1, 2)
    got_far_b = send(far_b, 1, 1)
    got_across_b = send(across_b, 0, 1)
    placed = (own_a, got_beside_a, got_across_a, got_far_a)
    beside_b, out = run(later, (far_b,), 0, 1, 2, placed)
    got_beside_b = send(beside_b, 1, 0)
    out = place(meta, [got_far_b, got_across_b], (3, 2), 1, out)
    return place(meta, [got_beside_b], (1,), 1, out)


def solution(mesh):
    in_specs = (P("seq", "kvh"), P("seq", "kvh"), P("seq", "kvh"), P())
    out_specs = P(("seq", "kvh"), None)
    return jax.shard_map(shards, mesh=mesh, in_specs=in_specs, out_specs=out_specs, check_vma=False)
```

```python
import math

import jax
import jax.numpy as jnp
from jax import lax
from jax.experimental import pallas as pl
from jax.experimental.pallas import tpu as pltpu
from jax.sharding import PartitionSpec as P

QUERY_PER_KEY = 12
HEAD_WIDTH = 128
GROUP_WIDTH = QUERY_PER_KEY * HEAD_WIDTH
SCALE_LOG2 = math.log2(math.e) / math.sqrt(HEAD_WIDTH)
VMEM_LIMIT = 62 * 1024 * 1024
STACK = 6
STACKS = QUERY_PER_KEY // STACK


def lanes(start):
    return pl.ds(pl.multiple_of(start * HEAD_WIDTH, HEAD_WIDTH), HEAD_WIDTH)


def first_visible(meta, position):
    end = jnp.int32(0)
    start = jnp.int32(0)
    for answer in range(2, meta.shape[0]):
        end = end + meta[answer]
        start = jnp.where(end <= position, end, start)
    return start


def attend_rows(count, offset, q_ref, out_ref, work, block):
    rows = q_ref.shape[0]
    stacked = STACK * rows
    window, nearest, shift, probs, stack, staged, facing = work[:7]
    width = count * block
    first = window.shape[0] - width
    tokens = lax.rem(lax.broadcasted_iota(jnp.int32, (stacked, block), 0), rows) + offset
    mask = lax.broadcasted_iota(jnp.int32, (stacked, block), 1) <= tokens

    def load(number):
        for h in range(STACK):
            stack[h * rows : (h + 1) * rows, :] = q_ref[:, lanes(number * STACK + h)]

    def score(slot):
        keys = window[first + slot * block : first + (slot + 1) * block, :HEAD_WIDTH]
        return lax.dot_general(
            stack[...], keys, (((1,), (1,)), ((), ())), preferred_element_type=jnp.float32
        )

    def begin():
        nearest[...] = jnp.where(mask, score(count - 1), -1e30)
        for h in range(STACK):
            at = slice(h * rows, (h + 1) * rows)
            ones = window[first : first + HEAD_WIDTH, 2 * HEAD_WIDTH :]
            same = jnp.dot(stack[at, :] * facing[...], ones, preferred_element_type=jnp.float32)
            shift[at, :] = same * SCALE_LOG2

    def soften(found, slot):
        for piece in range(block // HEAD_WIDTH):
            at = slice(piece * HEAD_WIDTH, (piece + 1) * HEAD_WIDTH)
            weights = jnp.exp2(found[:, at] * SCALE_LOG2 - shift[...])
            start = slot * block + piece * HEAD_WIDTH
            probs[:, start : start + HEAD_WIDTH] = weights.astype(jnp.bfloat16)

    def weigh():
        ahead = score(0) if count > 1 else None
        soften(nearest, count - 1)
        for slot in range(count - 1):
            found = ahead
            if slot < count - 2:
                ahead = score(slot + 1)
            soften(found, slot)

    def blend():
        found = jnp.dot(
            probs[:, :width], window[first:, HEAD_WIDTH:], preferred_element_type=jnp.float32
        )
        total = found[:, HEAD_WIDTH:]
        guess = pl.reciprocal(total, approx=True)
        guess = guess * (2.0 - total * guess)
        staged[...] = (found[:, :HEAD_WIDTH] * guess).astype(staged.dtype)
        return total

    def release(number):
        for h in range(STACK):
            out_ref[:, lanes(number * STACK + h)] = staged[h * rows : (h + 1) * rows]

    load(0)
    begin()

    def step(number, most):
        weigh()
        load(jnp.minimum(number + 1, STACKS - 1))
        begin()
        total = blend()
        for row in range(0, stacked, 8):
            most = jnp.maximum(most, total[row : row + 8])
        release(number)
        return most

    return jnp.max(lax.fori_loop(0, STACKS, step, jnp.zeros((8, HEAD_WIDTH), jnp.float32)))


def attend_rows_wide(visible, offset, q_ref, out_ref, work, block):
    rows = q_ref.shape[0]
    window, (peak, total, blended) = work[0], work[7:10]
    last = window.shape[0] - block
    tokens = lax.broadcasted_iota(jnp.int32, (rows, block), 0) + offset
    columns = lax.broadcasted_iota(jnp.int32, (rows, block), 1)

    @pl.loop(0, QUERY_PER_KEY)
    def _(head):
        peak[...] = jnp.full(peak.shape, -1e30, jnp.float32)
        total[...] = jnp.zeros(total.shape, jnp.float32)
        blended[...] = jnp.zeros(blended.shape, jnp.float32)

        @pl.loop(0, visible)
        def _(back):
            at = pl.ds(pl.multiple_of(last - back * block, block), block)
            found = lax.dot_general(
                q_ref[:, lanes(head)],
                window[at, :HEAD_WIDTH],
                (((1,), (1,)), ((), ())),
                preferred_element_type=jnp.float32,
            )
            found = jnp.where(columns <= tokens + back * block, found * SCALE_LOG2, -1e30)
            before = peak[...]
            now = jnp.maximum(before, jnp.max(found, axis=-1, keepdims=True))
            weights = jnp.exp2(found - now[:, :1])
            shrink = jnp.exp2(before - now)
            peak[...] = now
            total[...] = total[...] * shrink + jnp.sum(weights, axis=-1, keepdims=True)
            blended[...] = blended[...] * shrink + jnp.dot(
                weights.astype(jnp.bfloat16),
                window[at, HEAD_WIDTH : 2 * HEAD_WIDTH],
                preferred_element_type=jnp.float32,
            )

        out_ref[:, lanes(head)] = (blended[...] / total[...]).astype(out_ref.dtype)


def buffers_for(rows, span, block):
    stacked = STACK * rows
    return [
        pltpu.VMEM((span * block, 3 * HEAD_WIDTH), jnp.bfloat16),
        pltpu.VMEM((stacked, block), jnp.float32),
        pltpu.VMEM((stacked, HEAD_WIDTH), jnp.float32),
        pltpu.VMEM((stacked, span * block), jnp.bfloat16),
        pltpu.VMEM((stacked, HEAD_WIDTH), jnp.bfloat16),
        pltpu.VMEM((stacked, HEAD_WIDTH), jnp.bfloat16),
        pltpu.VMEM((rows, HEAD_WIDTH), jnp.bfloat16),
        pltpu.VMEM((rows, HEAD_WIDTH), jnp.float32),
        pltpu.VMEM((rows, HEAD_WIDTH), jnp.float32),
        pltpu.VMEM((rows, HEAD_WIDTH), jnp.float32),
        pltpu.SMEM((1,), jnp.float32),
    ]


WORK = 11


def attend_jobs(jobs, position_of, q_jobs, out_jobs, arrived, origin, meta, work, block, span, ready=None, done=None):
    work[0][:, 2 * HEAD_WIDTH :] = jnp.ones((span * block, HEAD_WIDTH), jnp.bfloat16)

    @pl.loop(0, jobs)
    def _(job):
        if ready is not None:
            ready(job)
        index, offset = position_of(job)
        start = lax.div(first_visible(meta, index * block), block)
        visible = index - start + 1
        last = (index - origin + 1 - span) * block
        window, facing, most = work[0], work[6], work[10]
        moved = pl.ds(pl.multiple_of(last, block), span * block)
        window[:, : 2 * HEAD_WIDTH] = arrived[moved, :]
        here = pl.ds(pl.multiple_of(last + (span - 1) * block + offset, facing.shape[0]), facing.shape[0])
        facing[...] = arrived[here, :HEAD_WIDTH]
        for count in range(1, span + 1):

            @pl.when(visible == count)
            def _():
                most[0] = attend_rows(count, offset, q_jobs.at[job], out_jobs.at[job], work, block)

        @pl.when(jnp.logical_not(most[0] < 2.0**120))
        def _():
            attend_rows_wide(visible, offset, q_jobs.at[job], out_jobs.at[job], work, block)

        if done is not None:
            done(job)


PARTS = (0, 1, 2, 3)


def place_columns(meta, source, which):
    core, group = lax.rem(meta[0], 2), meta[1]
    from_core = 1 - core if source % 2 else core
    from_group = 1 - group if source // 2 else group
    column = ((from_group * 2 + from_core) * 2 + which) * GROUP_WIDTH
    return pl.ds(pl.multiple_of(column, GROUP_WIDTH), GROUP_WIDTH)


def place_copies(meta, inputs, sources, which, out, held, sems):
    loads, stores = [], []
    for number, (source, ref) in enumerate(zip(sources, inputs)):
        at = place_columns(meta, source, which)
        loads.append(pltpu.make_async_copy(ref, held.at[number], sems.at[0, number]))
        stores.append(pltpu.make_async_copy(held.at[number], out.at[:, at], sems.at[1, number]))
    return loads, stores


def place_kernel(meta, *refs, which, sources):
    count = len(sources)
    out, held, sems = refs[-3:]
    loads, stores = place_copies(meta, refs[:count], sources, which, out, held, sems)
    for load in loads:
        load.start()
    for load, store in zip(loads, stores):
        load.wait()
        store.start()
    for store in stores:
        store.wait()


def place(meta, arrays, sources, which, out):
    rows, count = arrays[0].shape[0], len(arrays)
    return pl.pallas_call(
        lambda *refs: place_kernel(*refs, which=which, sources=sources),
        out_shape=jax.ShapeDtypeStruct(out.shape, out.dtype),
        grid_spec=pltpu.PrefetchScalarGridSpec(
            num_scalar_prefetch=1,
            grid=(),
            in_specs=[pl.BlockSpec(memory_space=pl.ANY)] * (count + 1),
            out_specs=pl.BlockSpec(memory_space=pltpu.HBM),
            scratch_shapes=[
                pltpu.VMEM((count, rows, GROUP_WIDTH), jnp.bfloat16),
                pltpu.SemaphoreType.DMA((2, count)),
            ],
        ),
        input_output_aliases={1 + count: 0},
        compiler_params=pltpu.CompilerParams(vmem_limit_bytes=8 * 1024 * 1024),
        cost_estimate=estimate(),
    )(meta, *arrays, out)


def pair_kernel(
    meta, queries, theirs, *refs, flip_half, which, jobs, block, span, pieces, placed
):
    window, q_jobs, out_jobs, sems, held, held_sems = refs[-6 - WORK : -WORK]
    outs = refs[-6 - WORK - jobs : -6 - WORK]
    work = refs[-WORK:]
    rows = q_jobs.shape[1]
    mine, group = meta[0], meta[1]
    core = lax.rem(mine, 2)
    right = lax.rem(lax.div(mine, 2), 2)
    origin = mine - core - (span - 1)

    def half_of(job):
        return 1 - group if flip_half and job < 2 else group


    def fill(source, source_row, slot, size, sem):
        return pltpu.make_async_copy(
            source.at[pl.ds(source_row, size)], window.at[pl.ds(slot * block, size)], sems.at[sem]
        )

    if pieces == 5:
        fixed = [fill(refs[4], 0, 0, block, 0)]
        for back in range(4):
            fixed.append(fill(refs[back], 0, 7 - 2 * back, 2 * block, back + 1))
        by_side = []
    else:
        own, near, far, side_own, side_near, side_far = refs[:6]
        fixed = [
            fill(far, block, 0, block, 0),
            fill(near, 0, 3, 2 * block, 1),
            fill(own, 0, 7, 2 * block, 2),
        ]
        by_side = [
            (fill(side_far, 0, 1, 2 * block, 3), fill(side_near, 0, 1, 2 * block, 3)),
            (fill(side_near, 0, 5, 2 * block, 4), fill(side_own, 0, 5, 2 * block, 4)),
        ]
    queries_in = []
    for job in range(jobs):
        source = queries if job % 2 else theirs
        at = pl.ds(pl.multiple_of((2 * core + which) * GROUP_WIDTH, GROUP_WIDTH), GROUP_WIDTH)
        queries_in.append(
            pltpu.make_async_copy(
                source.at[pl.ds(pl.multiple_of(half_of(job) * rows, rows), rows), at],
                q_jobs.at[job],
                sems.at[5 + job],
            )
        )
    for copy in fixed:
        copy.start()
    for on_left, on_right in by_side:
        pl.when(right == 0)(on_left.start)
        pl.when(right == 1)(on_right.start)
    for copy in queries_in:
        copy.start()
    for copy in fixed:
        copy.wait()
    for on_left, _ in by_side:
        on_left.wait()

    def position_of(job):
        half = jnp.where(job < 2, half_of(0), half_of(2))
        return mine - core + jnp.where(lax.rem(job, 2) == 0, 1 - core, core), half * rows

    if placed:
        loads, stores = place_copies(
            meta, refs[pieces : pieces + placed], PARTS, 0, outs[-1], held, held_sems
        )
        for load in loads:
            load.start()
        targets = [*outs[:-1], outs[-1].at[:, place_columns(meta, 0, which)]]
    else:
        loads, stores = [], []
        targets = outs
    copies = [
        pltpu.make_async_copy(out_jobs.at[job], out, sems.at[5 + job])
        for job, out in enumerate(targets)
    ]

    def ready(job):
        for number, copy in enumerate(queries_in):
            pl.when(job == number)(copy.wait)

    def done(job):
        for number, copy in enumerate(copies):
            pl.when(job == number)(copy.start)

    attend_jobs(
        jobs, position_of, q_jobs, out_jobs, window, origin, meta, work, block, span, ready, done
    )
    for load, store in zip(loads, stores):
        load.wait()
        store.start()
    for copy in [*stores, *copies]:
        copy.wait()


def estimate(long=True):
    flops = 8_000_000_000 if long else 400_000_000
    return pl.CostEstimate(flops=flops, bytes_accessed=400_000, transcendentals=0)


def attend_pair(
    meta, queries, theirs, pieces, placed, earlier, flip_half, which, jobs, rows, span
):
    block = queries.shape[0]
    args = [queries, theirs, *pieces, *placed, *earlier]
    widths = [GROUP_WIDTH] * (jobs - 1) + [8 * GROUP_WIDTH if placed else GROUP_WIDTH]
    return pl.pallas_call(
        lambda *refs: pair_kernel(
            *refs,
            flip_half=flip_half,
            which=which,
            jobs=jobs,
            block=block,
            span=span,
            pieces=len(pieces),
            placed=len(placed),
        ),
        out_shape=[jax.ShapeDtypeStruct((rows, width), jnp.bfloat16) for width in widths],
        grid_spec=pltpu.PrefetchScalarGridSpec(
            num_scalar_prefetch=1,
            grid=(),
            in_specs=[pl.BlockSpec(memory_space=pltpu.HBM)] * len(args),
            out_specs=[pl.BlockSpec(memory_space=pltpu.HBM)] * jobs,
            scratch_shapes=[
                pltpu.VMEM(((span + 1) * block, 2 * HEAD_WIDTH), jnp.bfloat16),
                pltpu.VMEM((jobs, rows, GROUP_WIDTH), jnp.bfloat16),
                pltpu.VMEM((jobs, rows, GROUP_WIDTH), jnp.bfloat16),
                pltpu.SemaphoreType.DMA((5 + jobs,)),
                pltpu.VMEM((max(len(placed), 1), rows, GROUP_WIDTH), jnp.bfloat16),
                pltpu.SemaphoreType.DMA((2, max(len(placed), 1))),
                *buffers_for(rows, span, block),
            ],
        ),
        compiler_params=pltpu.CompilerParams(vmem_limit_bytes=VMEM_LIMIT),
        cost_estimate=estimate(len(earlier) > 0),
    )(meta, *args)


def own_kernel(meta, keys, values, theirs, *refs):
    outs, items, sems = refs[:3], refs[3], refs[4]
    core = lax.rem(meta[0], 2)
    block = keys.shape[0]
    mine = pl.ds(pl.multiple_of(core * block, block), block)
    other = pl.ds(pl.multiple_of((1 - core) * block, block), block)
    loads = []
    for which in range(2):
        for part, source in enumerate((keys, values)):
            at = slice(part * HEAD_WIDTH, (part + 1) * HEAD_WIDTH)
            loads.append((source.at[:, lanes(2 * core + which)], items.at[which, mine, at]))
            from_them = slice((2 * part + which) * HEAD_WIDTH, (2 * part + which + 1) * HEAD_WIDTH)
            loads.append((theirs.at[:, from_them], items.at[which, other, at]))
    loads = [
        pltpu.make_async_copy(source, target, sems.at[number])
        for number, (source, target) in enumerate(loads)
    ]
    stores = [
        pltpu.make_async_copy(items.at[which], outs[which], sems.at[8 + which])
        for which in range(2)
    ]
    more = [
        pltpu.make_async_copy(items.at[1, pl.ds(block, block)], outs[2], sems.at[10]),
    ]
    for load in loads:
        load.start()
    for which in range(2):
        for load in loads[4 * which : 4 * which + 4]:
            load.wait()
        stores[which].start()
    for store in more:
        store.start()
    for store in [*stores, *more]:
        store.wait()


def own_items(meta, keys, values, their_kv):
    block = keys.shape[0]
    shape = (2 * block, 2 * HEAD_WIDTH)
    return pl.pallas_call(
        own_kernel,
        out_shape=[jax.ShapeDtypeStruct((n * block, shape[1]), jnp.bfloat16) for n in (2, 2, 1)],
        grid_spec=pltpu.PrefetchScalarGridSpec(
            num_scalar_prefetch=1,
            grid=(),
            in_specs=[pl.BlockSpec(memory_space=pltpu.HBM)] * 3,
            out_specs=[pl.BlockSpec(memory_space=pltpu.HBM)] * 3,
            scratch_shapes=[pltpu.VMEM((2, *shape), jnp.bfloat16), pltpu.SemaphoreType.DMA((11,))],
        ),
        compiler_params=pltpu.CompilerParams(vmem_limit_bytes=VMEM_LIMIT),
    )(meta, keys, values, their_kv)


def after(values, earlier):
    return pl.pallas_call(
        lambda *refs: None,
        out_shape=[jax.ShapeDtypeStruct(value.shape, value.dtype) for value in values],
        in_specs=[pl.BlockSpec(memory_space=pltpu.HBM)] * (len(values) + len(earlier)),
        out_specs=[pl.BlockSpec(memory_space=pltpu.HBM)] * len(values),
        input_output_aliases={n: n for n in range(len(values))},
    )(*values, *earlier)


def whole_kernel(meta, queries, gathered, out, window, q_jobs, out_jobs, sems, *work, which, block, span):
    jobs, rows = q_jobs.shape[0], q_jobs.shape[1]
    mine = meta[0]
    origin = mine - (span - 1)
    copies = []
    for slot in range(span):
        at = pl.ds(pl.multiple_of(jnp.maximum(origin + slot, 0) * block, block), block)
        copies.append(
            pltpu.make_async_copy(
                gathered.at[at], window.at[pl.ds(slot * block, block)], sems.at[jobs + slot]
            )
        )
    at = pl.ds(which * GROUP_WIDTH, GROUP_WIDTH)
    for job in range(jobs):
        copies.append(
            pltpu.make_async_copy(
                queries.at[pl.ds(job * rows, rows), at], q_jobs.at[job], sems.at[job]
            )
        )
    for copy in copies:
        copy.start()
    for copy in copies:
        copy.wait()
    attend_jobs(
        jobs,
        lambda job: (mine, job * rows),
        q_jobs,
        out_jobs,
        window,
        origin,
        meta,
        work,
        block,
        span,
    )
    copies = [
        pltpu.make_async_copy(out_jobs.at[job], out.at[pl.ds(job * rows, rows)], sems.at[job])
        for job in range(jobs)
    ]
    for copy in copies:
        copy.start()
    for copy in copies:
        copy.wait()


def shards_whole(meta, queries, keys, values, span):
    block, jobs = queries.shape[0], lax.axis_size("kvh")
    rows = block // jobs
    heads = []
    for which in range(keys.shape[1] // HEAD_WIDTH):
        at = slice(which * HEAD_WIDTH, (which + 1) * HEAD_WIDTH)
        item = jnp.concatenate([keys[:, at], values[:, at]], 1)
        gathered = lax.all_gather(item, "seq", axis=0, tiled=True)
        heads.append(
            pl.pallas_call(
                lambda *refs, which=which: whole_kernel(*refs, which=which, block=block, span=span),
                out_shape=jax.ShapeDtypeStruct((block, GROUP_WIDTH), jnp.bfloat16),
                grid_spec=pltpu.PrefetchScalarGridSpec(
                    num_scalar_prefetch=1,
                    grid=(),
                    in_specs=[pl.BlockSpec(memory_space=pltpu.HBM)] * 2,
                    out_specs=pl.BlockSpec(memory_space=pltpu.HBM),
                    scratch_shapes=[
                        pltpu.VMEM((span * block, 2 * HEAD_WIDTH), jnp.bfloat16),
                        pltpu.VMEM((jobs, rows, GROUP_WIDTH), jnp.bfloat16),
                        pltpu.VMEM((jobs, rows, GROUP_WIDTH), jnp.bfloat16),
                        pltpu.SemaphoreType.DMA((jobs + span,)),
                        *buffers_for(rows, span, block),
                    ],
                ),
                compiler_params=pltpu.CompilerParams(vmem_limit_bytes=VMEM_LIMIT),
            )(meta, queries, gathered)
        )
    return lax.all_to_all(
        jnp.concatenate(heads, 1), "kvh", split_axis=0, concat_axis=1, tiled=True
    )


def shards(queries, keys, values, answer_lengths):
    block = queries.shape[0]
    count, groups = lax.axis_size("seq"), lax.axis_size("kvh")
    span = min(12, count // 2)
    mine, group = lax.axis_index("seq"), lax.axis_index("kvh")
    meta = jnp.concatenate([jnp.stack([mine, group]).astype(jnp.int32), answer_lengths])
    if groups != 2 or span != 8 or count % 4 or keys.shape[1] != 4 * HEAD_WIDTH:
        return shards_whole(meta, queries, keys, values, span)
    core = lax.rem(mine, 2)
    rows = block // groups

    def theirs(value):
        width = value.shape[1] // 2
        return lax.dynamic_slice_in_dim(value, (1 - core) * width, width, 1)

    def permute(value, pairs):
        return lax.ppermute(value, "seq", pairs)

    swap = [(i, i ^ 1) for i in range(count)]
    def chips_ahead(chips):
        return [(i, i + 2 * chips) for i in range(count - 2 * chips)]

    ahead = chips_ahead(2)
    rightward = [(i, i + 2) for i in range(count) if i % 4 < 2]
    leftward = [(i, i - 2) for i in range(count) if i % 4 >= 2]

    their_queries = permute(queries, swap)
    their_kv = permute(jnp.concatenate([theirs(keys), theirs(values)], 1), swap)

    def gather(own):
        near = permute(own, ahead)
        far = permute(near, ahead)
        side_own = permute(own, rightward)
        side_near = permute(near, rightward + leftward)
        side_far = permute(far, leftward)
        return [own, near, far, side_own, side_near, side_far]

    def send(value, flip_core, flip_group):
        pairs = [
            (i * groups + r, (i ^ flip_core) * groups + (r ^ flip_group))
            for i in range(count)
            for r in range(groups)
        ]
        return lax.ppermute(value, ("seq", "kvh"), pairs)

    def run(pieces, earlier, flip_half, which, jobs, placed=()):
        return attend_pair(
            meta,
            queries,
            their_queries,
            pieces,
            placed,
            earlier,
            flip_half,
            which,
            jobs,
            rows,
            span,
        )

    own_first, own_second, upper = own_items(meta, keys, values, their_kv)
    pieces = gather(own_first)
    own, upper = after((own_second, upper), pieces[2:4])
    later = [own] + [permute(own, chips_ahead(n)) for n in (1, 2, 3)] + [permute(upper, chips_ahead(4))]
    far_a, across_a, beside_a, own_a = run(pieces, (), 1, 0, 4)
    got_far_a = send(far_a, 1, 1)
    got_across_a = send(across_a, 0, 1)
    got_beside_a = send(beside_a, 1, 0)
    far_b, across_b = run(later, (beside_a,), 1, 1, 2)
    got_far_b = send(far_b, 1, 1)
    got_across_b = send(across_b, 0, 1)
    placed = (own_a, got_beside_a, got_across_a, got_far_a)
    beside_b, out = run(later, (far_b,), 0, 1, 2, placed)
    got_beside_b = send(beside_b, 1, 0)
    out = place(meta, [got_far_b, got_across_b], (3, 2), 1, out)
    return place(meta, [got_beside_b], (1,), 1, out)


def solution(mesh):
    in_specs = (P("seq", "kvh"), P("seq", "kvh"), P("seq", "kvh"), P())
    out_specs = P(("seq", "kvh"), None)
    return jax.shard_map(shards, mesh=mesh, in_specs=in_specs, out_specs=out_specs, check_vma=False)
```
